32 devices in a mesh: expert: 4 (over z), dp: 8 (over y, x, core).
Axes of the slice: x: 2, y: 2, z: 4, core: 2. Of those that a mesh axis runs over, the one named last changes fastest.
Arguments:
- act_attn: bfloat16 [8192, 32], P(('expert', 'dp')), may hold values from -10 to 10
- dy_attn: bfloat16 [8192, 6144], P(('expert', 'dp')), may hold values from -10 to 10
- act_exp: bfloat16 [4, 1024, 16], P('expert', 'dp'), may hold values from -10 to 10
- dy_exp: bfloat16 [4, 1024, 6144], P('expert', 'dp'), may hold values from -10 to 10
- w_attn: float32 [32, 6144], P(('expert', 'dp')), may hold values from -0.3 to 0.3
- m_attn: float32 [32, 6144], P(('expert', 'dp')), may hold values from -1.5 to 1.5
- v_attn: float32 [32, 6144], P(('expert', 'dp')), may hold values from 0.05 to 1
- w_exp: float32 [4, 16, 6144], P('expert', 'dp'), may hold values from -0.3 to 0.3
- m_exp: float32 [4, 16, 6144], P('expert', 'dp'), may hold values from -1.5 to 1.5
- v_exp: float32 [4, 16, 6144], P('expert', 'dp'), may hold values from 0.05 to 1
Outputs:
- w_attn_new: float32 [32, 6144], P(('expert', 'dp'))
- m_attn_new: float32 [32, 6144], P(('expert', 'dp'))
- v_attn_new: float32 [32, 6144], P(('expert', 'dp'))
- w_exp_new: float32 [4, 16, 6144], P('expert', 'dp')
- m_exp_new: float32 [4, 16, 6144], P('expert', 'dp')
- v_exp_new: float32 [4, 16, 6144], P('expert', 'dp')
- attn_weights: bfloat16 [32, 6144], replicated
- expert_weights: bfloat16 [4, 16, 6144], P('expert')
The draws below stay inside these ranges and needn't reach their ends.
All inputs are finite; a program needn't handle non-finite values.
Results may differ from the reference program's by a relative error of at most 0.0075.
Values may be sent and summed in bfloat16 or wider, within the bound.
No kernel may reach another device: no remote copies, remote signals or barrier semaphores. Data moves between devices by JAX's collectives and lax.ppermute only.
A program may use at most 64 MiB of HBM per device.

```python
import math
import jax
import jax.numpy as jnp
from jax import lax

D = 6144
TOK_DEV = 256
EXP_TOK_DEV = 128
ATT_ROWS = 32
EXP_ROWS = 16
TOKENS = 8192
EXP_TOKENS = 1024
PARAMS = 589824
N_EXPERT = 4


def rows_draw(key, lead, count, rows):
    shape = lead + (count, rows)
    levels = 0.25 * jnp.exp(math.log(10.0) * jnp.arange(rows, dtype=jnp.float32) / max(rows - 1, 1))
    base = jax.random.normal(key, shape, jnp.float32)
    return (jnp.clip(base, -4.0, 4.0) * levels).astype(jnp.bfloat16)


def cols_draw(key, lead, count, cols, block):
    shape = lead + (count, cols)
    order = jax.random.permutation(jax.random.fold_in(key, 5), cols).astype(jnp.float32)
    levels = 0.25 * jnp.exp(math.log(10.0) * order / max(cols - 1, 1))
    blocks = count // block
    block_log = jax.random.uniform(jax.random.fold_in(key, 7), lead + (blocks, 1, 1), jnp.float32, math.log(0.25), 0.0)
    block_scale = jnp.exp(block_log)
    base = jax.random.normal(key, shape, jnp.float32)
    values = jnp.clip(base, -4.0, 4.0) * levels
    values = values.reshape(lead + (blocks, block, cols)) * block_scale
    return values.reshape(shape).astype(jnp.bfloat16)


def draw_act_attn(key, part):
    return rows_draw(jax.random.fold_in(key, 101), (), TOKENS, ATT_ROWS)


def draw_dy_attn(key, part):
    return cols_draw(jax.random.fold_in(key, 202), (), TOKENS, D, TOK_DEV)


def draw_act_exp(key, part):
    return rows_draw(jax.random.fold_in(key, 303), (N_EXPERT,), EXP_TOKENS, EXP_ROWS)


def draw_dy_exp(key, part):
    return cols_draw(jax.random.fold_in(key, 404), (N_EXPERT,), EXP_TOKENS, D, EXP_TOK_DEV)


def level_of(own_key, extent, split, low, top_value):
    loudness = 1.0
    for dim, parts in split:
        heights = jax.random.uniform(jax.random.fold_in(jax.random.fold_in(own_key, 6), dim), (parts,), jnp.float32, low / len(split), top_value / len(split))
        loudness = loudness * jnp.repeat(jnp.exp(heights), extent[dim] // parts).reshape((-1,) + (1,) * (len(extent) - 1 - dim))
    return loudness


def scatter_about(own_key, shape, deviation, bound, shards=(), kind=jnp.bfloat16):
    level = level_of(own_key, shape, shards, -0.22, 0.18) if shards else 1.0
    result = jax.random.normal(own_key, shape, jnp.float32) * deviation * level
    return jnp.minimum(jnp.maximum(result, -bound), bound).astype(kind)


def setup_inputs(seed: int = 0) -> dict:
    arg_keys = jax.random.split(jax.random.key(seed), 11)
    act_attn = draw_act_attn(jax.random.fold_in(arg_keys[10], 71), 0)
    dy_attn = draw_dy_attn(jax.random.fold_in(arg_keys[10], 71), 0)
    act_exp = draw_act_exp(jax.random.fold_in(arg_keys[10], 71), 0)
    dy_exp = draw_dy_exp(jax.random.fold_in(arg_keys[10], 71), 0)
    w_attn = scatter_about(arg_keys[4], (ATT_ROWS, D), 0.05, 0.3, ((0, 32),), jnp.float32)
    m_attn = scatter_about(arg_keys[5], (ATT_ROWS, D), 0.3, 1.5, ((0, 32),), jnp.float32)
    v_attn = jnp.clip(jnp.exp(math.log(1.0) - 2.9957323 * jax.random.uniform(arg_keys[6], (ATT_ROWS, D), jnp.float32) ** level_of(arg_keys[6], (ATT_ROWS, D), ((0, 32),), -0.2, 0.2)), 0.05, 1.0)
    w_exp = scatter_about(arg_keys[7], (N_EXPERT, EXP_ROWS, D), 0.05, 0.3, ((0, 4), (1, 8)), jnp.float32)
    m_exp = scatter_about(arg_keys[8], (N_EXPERT, EXP_ROWS, D), 0.3, 1.5, ((0, 4), (1, 8)), jnp.float32)
    v_exp = jnp.clip(jnp.exp(math.log(1.0) - 2.9957323 * jax.random.uniform(arg_keys[9], (N_EXPERT, EXP_ROWS, D), jnp.float32) ** level_of(arg_keys[9], (N_EXPERT, EXP_ROWS, D), ((0, 4), (1, 8)), -0.2, 0.2)), 0.05, 1.0)
    return dict(act_attn=act_attn, dy_attn=dy_attn, act_exp=act_exp, dy_exp=dy_exp, w_attn=w_attn, m_attn=m_attn, v_attn=v_attn, w_exp=w_exp, m_exp=m_exp, v_exp=v_exp)


beta_first = 0.9
beta_second = 0.95
bias_first = 1.0 - 0.9 ** 10
bias_second = 1.0 - 0.95 ** 10
learn_rate = 0.01
decay_rate = 0.1
adam_eps = 1e-08

def contract_rows(left, right):
    return lax.dot_general(left, right, (((0,), (0,)), ((), ())), preferred_element_type=jnp.float32)

def adamw(grad, weight, moment, second, factor):
    scaled = factor * grad
    moment_new = beta_first * moment + (1.0 - beta_first) * scaled
    second_new = beta_second * second + (1.0 - beta_second) * scaled * scaled
    update = moment_new / bias_first / (jnp.sqrt(second_new / bias_second) + adam_eps)
    weight_new = weight - learn_rate * (update + decay_rate * weight)
    return (weight_new, moment_new, second_new)

def reference(act_attn, dy_attn, act_exp, dy_exp, w_attn, m_attn, v_attn, w_exp, m_exp, v_exp):
    g_attn = contract_rows(act_attn, dy_attn)
    g_exp = jnp.stack([contract_rows(act_exp[index], dy_exp[index]) for index in range(N_EXPERT)])
    total = jnp.sum(g_attn * g_attn) + jnp.sum(g_exp * g_exp)
    norm = jnp.sqrt(total)
    factor = jnp.minimum(1.0, 0.5 * math.sqrt(PARAMS) / (norm + 1e-06))
    wa_new, ma_new, va_new = adamw(g_attn, w_attn, m_attn, v_attn, factor)
    we_new, me_new, ve_new = adamw(g_exp, w_exp, m_exp, v_exp, factor)
    return (wa_new, ma_new, va_new, we_new, me_new, ve_new, wa_new.astype(jnp.bfloat16), we_new.astype(jnp.bfloat16))
```

```python
import math

import jax
import jax.numpy as jnp
from jax import lax
from jax.sharding import PartitionSpec as P

beta_first = 0.9
beta_second = 0.95
bias_first = 1.0 - 0.9**10
bias_second = 1.0 - 0.95**10
learn_rate = 0.01
decay_rate = 0.1
adam_eps = 1e-08


def contract_rows(left, right):
    return lax.dot_general(
        left, right, (((0,), (0,)), ((), ())), preferred_element_type=jnp.float32
    )


def adamw(grad, weight, moment, second, factor):
    scaled = factor * grad
    moment_new = beta_first * moment + (1.0 - beta_first) * scaled
    second_new = beta_second * second + (1.0 - beta_second) * scaled * scaled
    update = moment_new / bias_first / (jnp.sqrt(second_new / bias_second) + adam_eps)
    weight_new = weight - learn_rate * (update + decay_rate * weight)
    return (weight_new, moment_new, second_new)


def doubling_sum(value, axis):
    size = lax.axis_size(axis)
    step = 1
    while step < size:
        value = value + lax.ppermute(value, axis, [(i, i ^ step) for i in range(size)])
        step *= 2
    return value


def body(act_attn, dy_attn, act_exp, dy_exp, w_attn, m_attn, v_attn, w_exp, m_exp, v_exp):
    width = w_attn.shape[1]
    n_expert = lax.axis_size("expert")
    n_dp = lax.axis_size("dp")
    rows_a = w_attn.shape[0]
    rows_e = w_exp.shape[1]
    total_params = width * (act_attn.shape[1] + n_expert * act_exp.shape[2])
    limit = 0.5 * math.sqrt(total_params)
    terms_a = contract_rows(act_attn, dy_attn).astype(jnp.bfloat16)
    terms_e = contract_rows(act_exp[0], dy_exp[0]).astype(jnp.bfloat16)
    terms_a = terms_a.reshape(n_expert, n_dp, rows_a, width).transpose(1, 0, 2, 3)
    terms = jnp.concatenate(
        [terms_a.reshape(n_dp, n_expert * rows_a, width), terms_e.reshape(n_dp, rows_e, width)], axis=1
    )
    got = lax.all_to_all(terms, "dp", split_axis=0, concat_axis=0, tiled=True)
    part = jnp.sum(got.astype(jnp.float32), axis=0)
    g_exp = part[n_expert * rows_a :]
    part_a = part[: n_expert * rows_a].reshape(n_expert, rows_a, width).astype(jnp.bfloat16)
    got_a = lax.all_to_all(part_a, "expert", split_axis=0, concat_axis=0, tiled=True)
    g_attn = jnp.sum(got_a.astype(jnp.float32), axis=0)
    square = jnp.sum(g_attn * g_attn) + jnp.sum(g_exp * g_exp)
    square = doubling_sum(doubling_sum(jnp.full((1, 128), square), "dp"), "expert")
    norm = jnp.sqrt(square[0, 0])
    factor = jnp.minimum(1.0, limit / (norm + 1e-06))
    wa_new, ma_new, va_new = adamw(g_attn, w_attn, m_attn, v_attn, factor)
    we_new, me_new, ve_new = adamw(g_exp[None], w_exp, m_exp, v_exp, factor)
    half_a = lax.all_gather(wa_new.astype(jnp.bfloat16), "expert", axis=0, tiled=False)
    both = jnp.concatenate(
        [half_a.reshape(n_expert * rows_a, width), we_new[0].astype(jnp.bfloat16)], axis=0
    )
    full = lax.all_gather(both, "dp", axis=0, tiled=False)
    attn_full = full[:, : n_expert * rows_a].reshape(n_dp, n_expert, rows_a, width)
    attn_full = attn_full.transpose(1, 0, 2, 3).reshape(-1, width)
    expert_full = full[:, n_expert * rows_a :].reshape(1, n_dp * rows_e, width)
    return (wa_new, ma_new, va_new, we_new, me_new, ve_new, attn_full, expert_full)


def solution(mesh):
    return jax.shard_map(
        body,
        mesh=mesh,
        in_specs=(
            P(("expert", "dp"), None),
            P(("expert", "dp"), None),
            P("expert", "dp", None),
            P("expert", "dp", None),
            P(("expert", "dp"), None),
            P(("expert", "dp"), None),
            P(("expert", "dp"), None),
            P("expert", "dp", None),
            P("expert", "dp", None),
            P("expert", "dp", None),
        ),
        out_specs=(
            P(("expert", "dp"), None),
            P(("expert", "dp"), None),
            P(("expert", "dp"), None),
            P("expert", "dp", None),
            P("expert", "dp", None),
            P("expert", "dp", None),
            P(),
            P("expert", None, None),
        ),
        check_vma=False,
    )
```

```python
import math

import jax
import jax.numpy as jnp
from jax import lax
from jax.experimental import pallas as pl
from jax.experimental.pallas import tpu as pltpu
from jax.sharding import PartitionSpec as P

beta_first = 0.9
beta_second = 0.95
bias_first = 1.0 - 0.9**10
bias_second = 1.0 - 0.95**10
learn_rate = 0.01
decay_rate = 0.1
adam_eps = 1e-08


def adamw(grad, weight, moment, second, factor):
    scaled = factor * grad
    moment_new = beta_first * moment + (1.0 - beta_first) * scaled
    second_new = beta_second * second + (1.0 - beta_second) * scaled * scaled
    update = moment_new / bias_first / (jnp.sqrt(second_new / bias_second) + adam_eps)
    weight_new = weight - learn_rate * (update + decay_rate * weight)
    return (weight_new, moment_new, second_new)


class Plan:
    def __init__(self, n_expert, n_dp, rows_a, rows_e):
        self.n_expert, self.n_dp, self.rows_a, self.rows_e = n_expert, n_dp, rows_a, rows_e
        self.chips = n_dp // 2
        self.split = n_expert * rows_a
        self.chunk = -(-(self.split + rows_e) // 8) * 8
        self.rows = n_dp * self.chunk

    def columns(self, place, me_dp, me_ex):
        half = place // (self.chips * self.chunk)
        chip = (place // self.chunk) % self.chips
        row = place % self.chunk
        owner = (2 * chip + half) ^ me_dp
        expert = (row // self.rows_a) ^ me_ex
        attn = (expert * self.n_dp + owner) * self.rows_a + row % self.rows_a
        exp = owner * self.rows_e + row - self.split
        attn = jnp.where(row < self.split, attn, -1)
        exp = jnp.where((row >= self.split) & (row < self.split + self.rows_e), exp, -1)
        return attn, exp


def select(place, index):
    return (place == index).astype(jnp.bfloat16)


def dot(left, right):
    return lax.dot_general(left, right, (((1,), (0,)), ((), ())), preferred_element_type=jnp.float32)


def terms_kernel(plan, act_a, dy_a, act_e, dy_e, keep, send, left_a, left_e):
    @pl.when(pl.program_id(0) == 0)
    def _():
        me_dp, me_ex = lax.axis_index("dp"), lax.axis_index("expert")
        count_a, count_e = act_a.shape[0], act_e.shape[0]
        place = lax.broadcasted_iota(jnp.int32, (plan.rows, count_a), 0)
        want, _unused = plan.columns(place, me_dp, me_ex)
        pick = select(want, lax.broadcasted_iota(jnp.int32, (plan.rows, count_a), 1))
        left_a[...] = dot(pick, act_a[...]).astype(jnp.bfloat16)
        place = lax.broadcasted_iota(jnp.int32, (plan.rows, count_e), 0)
        _unused, want = plan.columns(place, me_dp, me_ex)
        pick = select(want, lax.broadcasted_iota(jnp.int32, (plan.rows, count_e), 1))
        left_e[...] = dot(pick, act_e[...]).astype(jnp.bfloat16)

    terms = dot(left_a[...], dy_a[...]) + dot(left_e[...], dy_e[...])
    half = plan.rows // 2
    keep[...] = terms[:half]
    send[...] = terms[half:].astype(jnp.bfloat16)


def make_terms(plan, act_a, dy_a, act_e, dy_e):
    width = dy_a.shape[1]
    tile = width // 4
    half = plan.rows // 2
    return pl.pallas_call(
        lambda *refs: terms_kernel(plan, *refs),
        grid=(width // tile,),
        in_specs=[
            pl.BlockSpec(act_a.shape, lambda i: (0, 0)),
            pl.BlockSpec((dy_a.shape[0], tile), lambda i: (0, i)),
            pl.BlockSpec(act_e.shape, lambda i: (0, 0)),
            pl.BlockSpec((dy_e.shape[0], tile), lambda i: (0, i)),
        ],
        out_specs=[pl.BlockSpec((half, tile), lambda i: (0, i))] * 2,
        out_shape=[
            jax.ShapeDtypeStruct((half, width), jnp.float32),
            jax.ShapeDtypeStruct((half, width), jnp.bfloat16),
        ],
        scratch_shapes=[
            pltpu.VMEM((plan.rows, act_a.shape[1]), jnp.bfloat16),
            pltpu.VMEM((plan.rows, act_e.shape[1]), jnp.bfloat16),
        ],
        compiler_params=pltpu.CompilerParams(vmem_limit_bytes=48 * 1024 * 1024),
    )(act_a, dy_a, act_e, dy_e)


def order_kernel(plan, n_parts, *refs):
    parts, (attn, exp) = refs[:n_parts], refs[n_parts:]
    me_dp, me_ex = lax.axis_index("dp"), lax.axis_index("expert")
    rows = jnp.concatenate([part[...].astype(jnp.float32) for part in parts], axis=0).astype(jnp.bfloat16)
    count_a, count_e = attn.shape[0], exp.shape[1]
    place = lax.broadcasted_iota(jnp.int32, (count_a, plan.rows), 1)
    want, _unused = plan.columns(place, me_dp, me_ex)
    attn[...] = dot(select(want, lax.broadcasted_iota(jnp.int32, (count_a, plan.rows), 0)), rows).astype(jnp.bfloat16)
    place = lax.broadcasted_iota(jnp.int32, (count_e, plan.rows), 1)
    _unused, want = plan.columns(place, me_dp, me_ex)
    exp[0] = dot(select(want, lax.broadcasted_iota(jnp.int32, (count_e, plan.rows), 0)), rows).astype(jnp.bfloat16)


def put_in_order(plan, parts):
    width = parts[0].shape[1]
    tile = width // 4
    count_a = plan.n_expert * plan.n_dp * plan.rows_a
    count_e = plan.n_dp * plan.rows_e
    return pl.pallas_call(
        lambda *refs: order_kernel(plan, len(parts), *refs),
        grid=(width // tile,),
        in_specs=[pl.BlockSpec((part.shape[0], tile), lambda i: (0, i)) for part in parts],
        out_specs=[
            pl.BlockSpec((count_a, tile), lambda i: (0, i)),
            pl.BlockSpec((1, count_e, tile), lambda i: (0, 0, i)),
        ],
        out_shape=[
            jax.ShapeDtypeStruct((count_a, width), jnp.bfloat16),
            jax.ShapeDtypeStruct((1, count_e, width), jnp.bfloat16),
        ],
        compiler_params=pltpu.CompilerParams(vmem_limit_bytes=48 * 1024 * 1024),
    )(*parts)


def swap(value, axis, distance):
    size = lax.axis_size(axis)
    return lax.ppermute(value, axis, [(i, i ^ distance) for i in range(size)])


def body(act_attn, dy_attn, act_exp, dy_exp, w_attn, m_attn, v_attn, w_exp, m_exp, v_exp):
    width = w_attn.shape[1]
    n_expert = lax.axis_size("expert")
    n_dp = lax.axis_size("dp")
    rows_a, rows_e = w_attn.shape[0], w_exp.shape[1]
    plan = Plan(n_expert, n_dp, rows_a, rows_e)
    total_params = width * (act_attn.shape[1] + n_expert * act_exp.shape[2])
    limit = 0.5 * math.sqrt(total_params)
    chips, chunk, split = plan.chips, plan.chunk, plan.split

    keep, send = make_terms(plan, act_attn.T, dy_attn, act_exp[0].T, dy_exp[0])
    got = swap(send, "dp", 1)
    sums = [
        keep[c * chunk : (c + 1) * chunk] + got[c * chunk : (c + 1) * chunk].astype(jnp.float32)
        for c in range(chips)
    ]
    got = [swap(sums[c].astype(jnp.bfloat16), "dp", 2 * c) for c in range(1, chips)]
    part = sums[0] + sum(piece.astype(jnp.float32) for piece in got)
    g_exp = part[split : split + rows_e]
    got = [
        swap(part[q * rows_a : (q + 1) * rows_a].astype(jnp.bfloat16), "expert", q) for q in range(1, n_expert)
    ]
    g_attn = part[:rows_a] + sum(piece.astype(jnp.float32) for piece in got)
    square = jnp.sum(g_attn * g_attn) + jnp.sum(g_exp * g_exp)
    square = jnp.full((1, 128), square)
    square = square + swap(square, "dp", 1)
    square = square + sum([swap(square, "dp", 2 * c) for c in range(1, chips)])
    square = square + sum([swap(square, "expert", q) for q in range(1, n_expert)])
    norm = jnp.sqrt(square[0, 0])
    factor = jnp.minimum(1.0, limit / (norm + 1e-06))
    wa_new, ma_new, va_new = adamw(g_attn, w_attn, m_attn, v_attn, factor)
    we_new, me_new, ve_new = adamw(g_exp[None], w_exp, m_exp, v_exp, factor)

    half_a = wa_new.astype(jnp.bfloat16)
    mine = [half_a] + [swap(half_a, "expert", q) for q in range(1, n_expert)]
    mine.append(we_new[0].astype(jnp.bfloat16))
    if chunk > split + rows_e:
        mine.append(jnp.zeros((chunk - split - rows_e, width), jnp.bfloat16))
    mine = jnp.concatenate(mine, axis=0)
    near = [mine] + [swap(mine, "dp", 2 * c) for c in range(1, chips)]
    far = [swap(piece, "dp", 1) for piece in near]
    attn_full, expert_full = put_in_order(plan, near + far)
    return (wa_new, ma_new, va_new, we_new, me_new, ve_new, attn_full, expert_full)


def solution(mesh):
    return jax.shard_map(
        body,
        mesh=mesh,
        in_specs=(
            P(("expert", "dp"), None),
            P(("expert", "dp"), None),
            P("expert", "dp", None),
            P("expert", "dp", None),
            P(("expert", "dp"), None),
            P(("expert", "dp"), None),
            P(("expert", "dp"), None),
            P("expert", "dp", None),
            P("expert", "dp", None),
            P("expert", "dp", None),
        ),
        out_specs=(
            P(("expert", "dp"), None),
            P(("expert", "dp"), None),
            P(("expert", "dp"), None),
            P("expert", "dp", None),
            P("expert", "dp", None),
            P("expert", "dp", None),
            P(),
            P("expert", None, None),
        ),
        check_vma=False,
    )
```

```python
import math

import jax
import jax.numpy as jnp
from jax import lax
from jax.experimental import pallas as pl
from jax.experimental.pallas import tpu as pltpu
from jax.sharding import PartitionSpec as P

beta_first = 0.9
beta_second = 0.95
bias_first = 1.0 - 0.9**10
bias_second = 1.0 - 0.95**10
learn_rate = 0.01
decay_rate = 0.1
adam_eps = 1e-08

LANES = 128
f32, bf16 = jnp.float32, jnp.bfloat16


def adamw(grad, weight, moment, second, factor):
    scaled = factor * grad
    moment_new = beta_first * moment + (1.0 - beta_first) * scaled
    second_new = beta_second * second + (1.0 - beta_second) * scaled * scaled
    update = moment_new / bias_first / (jnp.sqrt(second_new / bias_second) + adam_eps)
    weight_new = weight - learn_rate * (update + decay_rate * weight)
    return (weight_new, moment_new, second_new)


class Plan:
    def __init__(self, n_expert, n_dp, rows_a, rows_e, width):
        self.n_expert, self.n_dp, self.rows_a, self.rows_e = n_expert, n_dp, rows_a, rows_e
        self.width = width
        self.chips = n_dp // 2
        self.blocks = width // LANES
        self.size_a = self.blocks * rows_a
        self.size_e = self.blocks * rows_e
        self.all_a = n_expert * self.size_a
        self.chunk = self.all_a + self.size_e

    def places(self, block):
        attn = [
            (e * self.rows_a + r, e * self.size_a + block * self.rows_a + r)
            for e in range(self.n_expert)
            for r in range(self.rows_a)
        ]
        exp = [(r, self.all_a + block * self.rows_e + r) for r in range(self.rows_e)]
        return attn, exp


def dot(left, right):
    return lax.dot_general(left, right, (((1,), (0,)), ((), ())), preferred_element_type=f32)


def call(kernel, args, outs, scratch=(), specs=None):
    whole = pl.BlockSpec(memory_space=pltpu.VMEM)
    return pl.pallas_call(
        kernel,
        in_specs=specs or [whole] * len(args),
        out_specs=[whole] * len(outs),
        out_shape=[jax.ShapeDtypeStruct(shape, dtype) for shape, dtype in outs],
        scratch_shapes=list(scratch),
        compiler_params=pltpu.CompilerParams(vmem_limit_bytes=48 * 1024 * 1024),
    )(*args)


def two_pieces(value):
    high = value.astype(bf16).astype(f32)
    return high, (value - high).astype(bf16).astype(f32)


def by_eights(value):
    return jnp.sum(value.reshape(-1, 8, LANES), axis=0)


STEPS = 4


def terms_kernel(plan, act_a, dy_a, act_e, dy_e, w, m, v, full, send, pack, act_a_v, dy_a_v, act_e_v, dy_e_v, state, sems):
    tile = plan.width // STEPS
    small = [
        pltpu.make_async_copy(act_a, act_a_v, sems.at[0]),
        pltpu.make_async_copy(act_e, act_e_v, sems.at[1]),
    ]
    big = []
    for t in range(STEPS):
        cols = pl.ds(t * tile, tile)
        big.append(pltpu.make_async_copy(dy_a.at[:, cols], dy_a_v.at[:, cols], sems.at[2 + 2 * t]))
        big.append(pltpu.make_async_copy(dy_e.at[:, cols], dy_e_v.at[:, cols], sems.at[3 + 2 * t]))
    extra = [pltpu.make_async_copy(ref, state.at[i], sems.at[2 + 2 * STEPS + i]) for i, ref in enumerate((w, m, v))]
    for copy in small + big + extra:
        copy.start()

    me = lax.axis_index("dp")

    def pick(groups, per_owner, count):
        shape = (groups * plan.n_dp, count)
        row = lax.broadcasted_iota(jnp.int32, shape, 0)
        col = lax.broadcasted_iota(jnp.int32, shape, 1)
        group, place = row // plan.n_dp, row % plan.n_dp
        owner = (2 * (place % plan.chips) + place // plan.chips) ^ me
        want = ((group // per_owner) * plan.n_dp + owner) * per_owner + group % per_owner
        return (want == col).astype(bf16)

    for copy in small:
        copy.wait()
    left_a = dot(pick(plan.n_expert * plan.rows_a, plan.rows_a, act_a.shape[0]), act_a_v[...]).astype(bf16)
    left_e = dot(pick(plan.rows_e, plan.rows_e, act_e.shape[0]), act_e_v[...]).astype(bf16)
    n_dp = plan.n_dp
    for t in range(STEPS):
        cols = pl.ds(t * tile, tile)
        big[2 * t].wait()
        terms_a = dot(left_a, dy_a_v[:, cols])
        big[2 * t + 1].wait()
        terms_e = dot(left_e, dy_e_v[:, cols])
        for b in range(tile // LANES):
            attn, exp = plan.places(t * (tile // LANES) + b)
            span = slice(b * LANES, (b + 1) * LANES)
            for terms, places in ((terms_a, attn), (terms_e, exp)):
                for group, start in places:
                    full[pl.ds(start, n_dp, stride=plan.chunk), :] = terms[group * n_dp : (group + 1) * n_dp, span]
    for c in range(plan.chips):
        send[pl.ds(c * plan.chunk, plan.chunk), :] = full[
            pl.ds((plan.chips + c) * plan.chunk, plan.chunk), :
        ].astype(bf16)
    for copy in extra:
        copy.wait()
    size = plan.size_a
    high, low = two_pieces(state[0])
    for i, value in enumerate((high, low, state[1], state[2])):
        pack[pl.ds(i * size, size), :] = value.astype(bf16)


def make_terms(plan, act_a, dy_a, act_e, dy_e, w, m, v):
    args = (act_a, dy_a, act_e, dy_e, w, m, v)
    half = plan.chips * plan.chunk
    return call(
        lambda *refs: terms_kernel(plan, *refs),
        args,
        [((2 * half, LANES), f32), ((half, LANES), bf16), ((4 * plan.size_a, LANES), bf16)],
        [
            pltpu.VMEM(act_a.shape, bf16),
            pltpu.VMEM(dy_a.shape, bf16),
            pltpu.VMEM(act_e.shape, bf16),
            pltpu.VMEM(dy_e.shape, bf16),
            pltpu.VMEM((3,) + w.shape, f32),
            pltpu.SemaphoreType.DMA((5 + 2 * STEPS,)),
        ],
        [pl.BlockSpec(memory_space=pltpu.HBM)] * len(args),
    )


def share_kernel(plan, *refs):
    own, got, (payload, g_exp) = refs[0], refs[1:-2], refs[-2:]
    total = own[...]
    for ref in got:
        total = total + ref[...].astype(f32)
    a = plan.all_a
    exp = total[a:]
    g_exp[...] = exp
    payload[:a, :] = total[:a].astype(bf16)
    payload[a:, :] = jnp.concatenate(two_pieces(by_eights(exp * exp)), axis=0).astype(bf16)


def pair_sum(plan, mine, other):
    a = plan.all_a
    attn = mine[:a, :].astype(f32) + other[:a, :].astype(f32)
    one, two = mine[a:, :].astype(f32), other[a:, :].astype(f32)
    return attn, (one[:8] + one[8:]) + (two[:8] + two[8:])


def again_kernel(plan, mine, other, payload):
    attn, square = pair_sum(plan, mine, other)
    a = plan.all_a
    payload[:a, :] = attn.astype(bf16)
    payload[a:, :] = jnp.concatenate(two_pieces(square), axis=0).astype(bf16)


def last_kernel(plan, mine, other, g_attn, square):
    attn, partial = pair_sum(plan, mine, other)
    g_attn[...] = attn
    square[...] = partial + by_eights(attn * attn)


def update_kernel(plan, limit, *refs):
    square, g_attn, g_exp, wa, ma, va, we, me, ve = refs[:9]
    packs = refs[9 : 9 + plan.n_expert]
    wa_new, ma_new, va_new, we_new, me_new, ve_new, mine = refs[9 + plan.n_expert :]
    norm = jnp.sqrt(jnp.sum(square[...], keepdims=True))
    factor = jnp.minimum(1.0, limit / (norm + 1e-06))
    place = lax.axis_index("expert")
    size = plan.size_a

    def rows(expert):
        return pl.ds(pl.multiple_of(expert * size, 16), size)

    wa_new[...], ma_new[...], va_new[...] = adamw(g_attn[rows(place), :], wa[...], ma[...], va[...], factor)
    for q, pack in enumerate(packs):
        high, low, moment, second = [pack[pl.ds(i * size, size), :].astype(f32) for i in range(4)]
        weight, _, _ = adamw(g_attn[rows(place ^ q), :], high + low, moment, second, factor)
        mine[rows(place ^ q), :] = weight.astype(bf16)
    weight, moment, second = adamw(g_exp[...], we[...], me[...], ve[...], factor)
    we_new[...], me_new[...], ve_new[...] = weight, moment, second
    mine[plan.all_a :, :] = weight.astype(bf16)


def order_kernel(plan, *refs):
    n_dp = plan.n_dp
    parts, (attn, exp, rows, rows_a, rows_e) = refs[:n_dp], refs[n_dp:]
    me = lax.axis_index("dp")
    for i, part in enumerate(parts):
        owner = (2 * (i % plan.chips) + i // plan.chips) ^ me
        rows[pl.ds(pl.multiple_of(owner * plan.chunk, 16), plan.chunk), :] = part[...].astype(f32)
    count_a, count_e = attn.shape[0], exp.shape[1]
    for b in range(plan.blocks):
        places_a, places_e = plan.places(b)
        span = pl.ds(b * LANES, LANES)
        values = [rows[pl.ds(start, n_dp, stride=plan.chunk), :] for _, start in places_a]
        if plan.rows_a == 1:
            attn[:, span] = jnp.concatenate(values, axis=0).astype(bf16)
        else:
            for (group, _), value in zip(places_a, values):
                start = (group // plan.rows_a) * n_dp * plan.rows_a + group % plan.rows_a
                rows_a[pl.ds(start, n_dp, stride=plan.rows_a), :] = value
            attn[:, span] = rows_a[...].astype(bf16)
        for r, start in places_e:
            rows_e[pl.ds(b * count_e + r, n_dp, stride=plan.rows_e), :] = rows[
                pl.ds(start, n_dp, stride=plan.chunk), :
            ]
    for b in range(plan.blocks):
        exp[0, :, pl.ds(b * LANES, LANES)] = rows_e[pl.ds(b * count_e, count_e), :].astype(bf16)


def put_in_order(plan, parts):
    count_a = plan.n_expert * plan.n_dp * plan.rows_a
    count_e = plan.n_dp * plan.rows_e
    return call(
        lambda *refs: order_kernel(plan, *refs),
        parts,
        [((count_a, plan.width), bf16), ((1, count_e, plan.width), bf16)],
        [
            pltpu.VMEM((plan.n_dp * plan.chunk, LANES), f32),
            pltpu.VMEM((count_a, LANES), f32),
            pltpu.VMEM((plan.blocks * count_e, LANES), f32),
        ],
    )


def swap(value, axis, distance):
    size = lax.axis_size(axis)
    return lax.ppermute(value, axis, [(i, i ^ distance) for i in range(size)])


def to_blocks(value):
    rows, width = value.shape
    return value.reshape(rows, width // LANES, LANES).transpose(1, 0, 2).reshape(-1, LANES)


def from_blocks(value, rows):
    return value.reshape(-1, rows, LANES).transpose(1, 0, 2).reshape(rows, -1)


def body(act_attn, dy_attn, act_exp, dy_exp, w_attn, m_attn, v_attn, w_exp, m_exp, v_exp):
    width = w_attn.shape[1]
    n_expert = lax.axis_size("expert")
    n_dp = lax.axis_size("dp")
    rows_a, rows_e = w_attn.shape[0], w_exp.shape[1]
    plan = Plan(n_expert, n_dp, rows_a, rows_e, width)
    total_params = width * (act_attn.shape[1] + n_expert * act_exp.shape[2])
    limit = 0.5 * math.sqrt(total_params)
    chips, chunk = plan.chips, plan.chunk
    state_a = [to_blocks(value) for value in (w_attn, m_attn, v_attn)]
    state_e = [to_blocks(value[0]) for value in (w_exp, m_exp, v_exp)]

    full, send, pack = make_terms(plan, act_attn.T, dy_attn, act_exp[0].T, dy_exp[0], *state_a)
    got = swap(send, "dp", 1)
    packs = [pack] + [swap(pack, "expert", q) for q in range(1, n_expert)]
    sums = [
        full[c * chunk : (c + 1) * chunk] + got[c * chunk : (c + 1) * chunk].astype(f32) for c in range(chips)
    ]
    got = [swap(sums[c].astype(bf16), "dp", 2 * c) for c in range(1, chips)]
    shared = ((plan.all_a + 16, LANES), bf16)
    payload, g_exp = call(
        lambda *refs: share_kernel(plan, *refs), [sums[0]] + got, [shared, ((plan.size_e, LANES), f32)]
    )
    distance = 1
    while 2 * distance < n_expert:
        other = swap(payload, "expert", distance)
        (payload,) = call(lambda *refs: again_kernel(plan, *refs), [payload, other], [shared])
        distance *= 2
    other = swap(payload, "expert", distance)
    g_attn, square = call(
        lambda *refs: last_kernel(plan, *refs), [payload, other], [((plan.all_a, LANES), f32), ((8, LANES), f32)]
    )
    distance = 1
    while distance < n_dp:
        square = square + swap(square, "dp", distance)
        distance *= 2
    block_a, block_e = ((plan.size_a, LANES), f32), ((plan.size_e, LANES), f32)
    wa, ma, va, we, me, ve, mine = call(
        lambda *refs: update_kernel(plan, limit, *refs),
        [square, g_attn, g_exp, *state_a, *state_e, *packs],
        [block_a] * 3 + [block_e] * 3 + [((chunk, LANES), bf16)],
    )
    near = [mine] + [swap(mine, "dp", 2 * c) for c in range(1, chips)]
    far = [swap(piece, "dp", 1) for piece in near]
    attn_full, expert_full = put_in_order(plan, near + far)
    new_a = [from_blocks(value, rows_a) for value in (wa, ma, va)]
    new_e = [from_blocks(value, rows_e)[None] for value in (we, me, ve)]
    return (*new_a, *new_e, attn_full, expert_full)


def solution(mesh):
    return jax.shard_map(
        body,
        mesh=mesh,
        in_specs=(
            P(("expert", "dp"), None),
            P(("expert", "dp"), None),
            P("expert", "dp", None),
            P("expert", "dp", None),
            P(("expert", "dp"), None),
            P(("expert", "dp"), None),
            P(("expert", "dp"), None),
            P("expert", "dp", None),
            P("expert", "dp", None),
            P("expert", "dp", None),
        ),
        out_specs=(
            P(("expert", "dp"), None),
            P(("expert", "dp"), None),
            P(("expert", "dp"), None),
            P("expert", "dp", None),
            P("expert", "dp", None),
            P("expert", "dp", None),
            P(),
            P("expert", None, None),
        ),
        check_vma=False,
    )
```

```python
import math

import jax
import jax.numpy as jnp
from jax import lax
from jax.experimental import pallas as pl
from jax.experimental.pallas import tpu as pltpu
from jax.sharding import PartitionSpec as P

beta_first = 0.9
beta_second = 0.95
bias_first = 1.0 - 0.9**10
bias_second = 1.0 - 0.95**10
learn_rate = 0.01
decay_rate = 0.1
adam_eps = 1e-08

LANES = 128
f32, bf16 = jnp.float32, jnp.bfloat16


def adamw(grad, weight, moment, second, factor):
    scaled = factor * grad
    moment_new = beta_first * moment + (1.0 - beta_first) * scaled
    second_new = beta_second * second + (1.0 - beta_second) * scaled * scaled
    update = moment_new / bias_first / (jnp.sqrt(second_new / bias_second) + adam_eps)
    weight_new = weight - learn_rate * (update + decay_rate * weight)
    return (weight_new, moment_new, second_new)


class Plan:
    def __init__(self, n_expert, n_dp, rows_a, rows_e, width):
        self.n_expert, self.n_dp, self.rows_a, self.rows_e = n_expert, n_dp, rows_a, rows_e
        self.width = width
        self.chips = n_dp // 2
        self.blocks = width // LANES
        self.size_a = self.blocks * rows_a
        self.size_e = self.blocks * rows_e
        self.all_a = n_expert * self.size_a
        self.chunk = self.all_a + self.size_e

    def places(self, block):
        attn = [
            (e * self.rows_a + r, e * self.size_a + block * self.rows_a + r)
            for e in range(self.n_expert)
            for r in range(self.rows_a)
        ]
        exp = [(r, self.all_a + block * self.rows_e + r) for r in range(self.rows_e)]
        return attn, exp


def dot(left, right):
    return lax.dot_general(left, right, (((1,), (0,)), ((), ())), preferred_element_type=f32)


def call(kernel, args, outs, scratch=(), specs=None):
    whole = pl.BlockSpec(memory_space=pltpu.VMEM)
    return pl.pallas_call(
        kernel,
        in_specs=specs or [whole] * len(args),
        out_specs=[whole] * len(outs),
        out_shape=[jax.ShapeDtypeStruct(shape, dtype) for shape, dtype in outs],
        scratch_shapes=list(scratch),
        compiler_params=pltpu.CompilerParams(vmem_limit_bytes=48 * 1024 * 1024),
    )(*args)


def two_pieces(value):
    high = value.astype(bf16).astype(f32)
    return high, (value - high).astype(bf16).astype(f32)


def by_eights(value):
    return jnp.sum(value.reshape(-1, 8, LANES), axis=0)


STEPS = 4


def each(count, step, unrolled):
    if unrolled:
        for i in range(count):
            step(i)
    else:
        pl.loop(0, count)(step)


def terms_kernel(plan, act_a, dy_a, act_e, dy_e, w, m, v, full, send, pack, act_a_v, dy_a_v, act_e_v, dy_e_v, state, sems):
    tile = plan.width // STEPS
    small = [
        pltpu.make_async_copy(act_a, act_a_v, sems.at[0]),
        pltpu.make_async_copy(act_e, act_e_v, sems.at[1]),
    ]
    big = []
    for t in range(STEPS):
        cols = pl.ds(t * tile, tile)
        big.append(pltpu.make_async_copy(dy_a.at[:, cols], dy_a_v.at[:, cols], sems.at[2 + 2 * t]))
        big.append(pltpu.make_async_copy(dy_e.at[:, cols], dy_e_v.at[:, cols], sems.at[3 + 2 * t]))
    extra = [pltpu.make_async_copy(ref, state.at[i], sems.at[2 + 2 * STEPS + i]) for i, ref in enumerate((w, m, v))]
    for copy in small + big + extra:
        copy.start()

    me = lax.axis_index("dp")

    def pick(groups, per_owner, count):
        shape = (groups * plan.n_dp, count)
        row = lax.broadcasted_iota(jnp.int32, shape, 0)
        col = lax.broadcasted_iota(jnp.int32, shape, 1)
        group, place = row // plan.n_dp, row % plan.n_dp
        owner = (2 * (place % plan.chips) + place // plan.chips) ^ me
        want = ((group // per_owner) * plan.n_dp + owner) * per_owner + group % per_owner
        return (want == col).astype(bf16)

    for copy in small:
        copy.wait()
    left_a = dot(pick(plan.n_expert * plan.rows_a, plan.rows_a, act_a.shape[0]), act_a_v[...]).astype(bf16)
    left_e = dot(pick(plan.rows_e, plan.rows_e, act_e.shape[0]), act_e_v[...]).astype(bf16)
    n_dp = plan.n_dp
    for t in range(STEPS):
        cols = pl.ds(t * tile, tile)
        big[2 * t].wait()
        terms_a = dot(left_a, dy_a_v[:, cols])
        big[2 * t + 1].wait()
        terms_e = dot(left_e, dy_e_v[:, cols])
        for b in range(tile // LANES):
            attn, exp = plan.places(t * (tile // LANES) + b)
            span = slice(b * LANES, (b + 1) * LANES)
            for terms, places in ((terms_a, attn), (terms_e, exp)):
                for group, start in places:
                    full[pl.ds(start, n_dp, stride=plan.chunk), :] = terms[group * n_dp : (group + 1) * n_dp, span]
    for c in range(plan.chips):
        send[pl.ds(c * plan.chunk, plan.chunk), :] = full[
            pl.ds((plan.chips + c) * plan.chunk, plan.chunk), :
        ].astype(bf16)
    for copy in extra:
        copy.wait()
    size = plan.size_a
    high, low = two_pieces(state[0])
    for i, value in enumerate((high, low, state[1], state[2])):
        pack[pl.ds(i * size, size), :] = value.astype(bf16)


def make_terms(plan, act_a, dy_a, act_e, dy_e, w, m, v):
    args = (act_a, dy_a, act_e, dy_e, w, m, v)
    half = plan.chips * plan.chunk
    return call(
        lambda *refs: terms_kernel(plan, *refs),
        args,
        [((2 * half, LANES), f32), ((half, LANES), bf16), ((4 * plan.size_a, LANES), bf16)],
        [
            pltpu.VMEM(act_a.shape, bf16),
            pltpu.VMEM(dy_a.shape, bf16),
            pltpu.VMEM(act_e.shape, bf16),
            pltpu.VMEM(dy_e.shape, bf16),
            pltpu.VMEM((3,) + w.shape, f32),
            pltpu.SemaphoreType.DMA((5 + 2 * STEPS,)),
        ],
        [pl.BlockSpec(memory_space=pltpu.HBM)] * len(args),
    )


def share_kernel(plan, *refs):
    packs, refs = refs[: plan.n_expert], refs[plan.n_expert :]
    own, got, (payload, g_exp, states) = refs[0], refs[1:-3], refs[-3:]
    place = lax.axis_index("expert")
    for q, pack in enumerate(packs):
        states[place ^ q] = pack[...]
    total = own[...]
    for ref in got:
        total = total + ref[...].astype(f32)
    a = plan.all_a
    exp = total[a:]
    g_exp[...] = exp
    payload[:a, :] = total[:a].astype(bf16)
    payload[a:, :] = jnp.concatenate(two_pieces(by_eights(exp * exp)), axis=0).astype(bf16)


def pair_sum(plan, mine, other):
    a = plan.all_a
    attn = mine[:a, :].astype(f32) + other[:a, :].astype(f32)
    one, two = mine[a:, :].astype(f32), other[a:, :].astype(f32)
    return attn, (one[:8] + one[8:]) + (two[:8] + two[8:])


def again_kernel(plan, mine, other, payload):
    attn, square = pair_sum(plan, mine, other)
    a = plan.all_a
    payload[:a, :] = attn.astype(bf16)
    payload[a:, :] = jnp.concatenate(two_pieces(square), axis=0).astype(bf16)


def last_kernel(plan, mine, other, g_attn, square):
    attn, partial = pair_sum(plan, mine, other)
    g_attn[...] = attn
    square[...] = partial + by_eights(attn * attn)


def update_kernel(plan, limit, *refs):
    square, g_attn, g_exp, wa, ma, va, we, me, ve = refs[:9]
    states, wa_new, ma_new, va_new, we_new, me_new, ve_new, mine = refs[9:]
    norm = jnp.sqrt(jnp.sum(square[...], keepdims=True))
    factor = jnp.minimum(1.0, limit / (norm + 1e-06))
    place = lax.axis_index("expert")
    size = plan.size_a

    def rows(expert):
        return pl.ds(pl.multiple_of(expert * size, 16), size)

    wa_new[...], ma_new[...], va_new[...] = adamw(g_attn[rows(place), :], wa[...], ma[...], va[...], factor)
    for e in range(plan.n_expert):
        high, low, moment, second = [states[e, pl.ds(i * size, size), :].astype(f32) for i in range(4)]
        weight, _, _ = adamw(g_attn[pl.ds(e * size, size), :], high + low, moment, second, factor)
        mine[pl.ds(e * size, size), :] = weight.astype(bf16)
    weight, moment, second = adamw(g_exp[...], we[...], me[...], ve[...], factor)
    we_new[...], me_new[...], ve_new[...] = weight, moment, second
    mine[plan.all_a :, :] = weight.astype(bf16)


def order_kernel(plan, *refs):
    n_dp = plan.n_dp
    parts, (attn, exp, rows, rows_a, rows_e) = refs[:n_dp], refs[n_dp:]
    me = lax.axis_index("dp")
    for i, part in enumerate(parts):
        owner = (2 * (i % plan.chips) + i // plan.chips) ^ me
        rows[pl.ds(pl.multiple_of(owner * plan.chunk, 16), plan.chunk), :] = part[...].astype(f32)
    count_a, count_e = attn.shape[0], exp.shape[1]

    def one(b):
        places_a, places_e = plan.places(b)
        span = pl.ds(b * LANES if isinstance(b, int) else pl.multiple_of(b * LANES, LANES), LANES)
        values = [rows[pl.ds(start, n_dp, stride=plan.chunk), :] for _, start in places_a]
        if plan.rows_a == 1:
            attn[:, span] = jnp.concatenate(values, axis=0).astype(bf16)
        else:
            for (group, _), value in zip(places_a, values):
                start = (group // plan.rows_a) * n_dp * plan.rows_a + group % plan.rows_a
                rows_a[pl.ds(start, n_dp, stride=plan.rows_a), :] = value
            attn[:, span] = rows_a[...].astype(bf16)
        for r, start in places_e:
            rows_e[pl.ds(b * count_e + r, n_dp, stride=plan.rows_e), :] = rows[
                pl.ds(start, n_dp, stride=plan.chunk), :
            ]

    each(plan.blocks, one, n_dp <= 8)
    for b in range(plan.blocks):
        exp[0, :, pl.ds(b * LANES, LANES)] = rows_e[pl.ds(b * count_e, count_e), :].astype(bf16)


def put_in_order(plan, parts):
    count_a = plan.n_expert * plan.n_dp * plan.rows_a
    count_e = plan.n_dp * plan.rows_e
    return call(
        lambda *refs: order_kernel(plan, *refs),
        parts,
        [((count_a, plan.width), bf16), ((1, count_e, plan.width), bf16)],
        [
            pltpu.VMEM((plan.n_dp * plan.chunk, LANES), f32),
            pltpu.VMEM((count_a, LANES), f32),
            pltpu.VMEM((plan.blocks * count_e, LANES), f32),
        ],
    )


def swap(value, axis, distance):
    size = lax.axis_size(axis)
    return lax.ppermute(value, axis, [(i, i ^ distance) for i in range(size)])


def to_blocks(value):
    rows, width = value.shape
    return value.reshape(rows, width // LANES, LANES).transpose(1, 0, 2).reshape(-1, LANES)


def from_blocks(value, rows):
    return value.reshape(-1, rows, LANES).transpose(1, 0, 2).reshape(rows, -1)


def body(act_attn, dy_attn, act_exp, dy_exp, w_attn, m_attn, v_attn, w_exp, m_exp, v_exp):
    width = w_attn.shape[1]
    n_expert = lax.axis_size("expert")
    n_dp = lax.axis_size("dp")
    rows_a, rows_e = w_attn.shape[0], w_exp.shape[1]
    plan = Plan(n_expert, n_dp, rows_a, rows_e, width)
    total_params = width * (act_attn.shape[1] + n_expert * act_exp.shape[2])
    limit = 0.5 * math.sqrt(total_params)
    chips, chunk = plan.chips, plan.chunk
    state_a = [to_blocks(value) for value in (w_attn, m_attn, v_attn)]
    state_e = [to_blocks(value[0]) for value in (w_exp, m_exp, v_exp)]

    held = [pltpu.with_memory_space_constraint(x, pltpu.HBM) for x in (act_attn.T, dy_attn, act_exp[0].T, dy_exp[0])]
    full, send, pack = make_terms(plan, *held, *[pltpu.with_memory_space_constraint(x, pltpu.HBM) for x in state_a])
    got = swap(send, "dp", 1)
    packs = [pack] + [swap(pack, "expert", q) for q in range(1, n_expert)]
    sums = [
        full[c * chunk : (c + 1) * chunk] + got[c * chunk : (c + 1) * chunk].astype(f32) for c in range(chips)
    ]
    got = [swap(sums[c].astype(bf16), "dp", 2 * c) for c in range(1, chips)]
    shared = ((plan.all_a + 16, LANES), bf16)
    payload, g_exp, states = call(
        lambda *refs: share_kernel(plan, *refs),
        packs + [sums[0]] + got,
        [shared, ((plan.size_e, LANES), f32), ((n_expert, 4 * plan.size_a, LANES), bf16)],
    )
    distance = 1
    while 2 * distance < n_expert:
        other = swap(payload, "expert", distance)
        (payload,) = call(lambda *refs: again_kernel(plan, *refs), [payload, other], [shared])
        distance *= 2
    other = swap(payload, "expert", distance)
    g_attn, square = call(
        lambda *refs: last_kernel(plan, *refs), [payload, other], [((plan.all_a, LANES), f32), ((8, LANES), f32)]
    )
    distance = 1
    while distance < n_dp:
        square = square + swap(square, "dp", distance)
        distance *= 2
    block_a, block_e = ((plan.size_a, LANES), f32), ((plan.size_e, LANES), f32)
    wa, ma, va, we, me, ve, mine = call(
        lambda *refs: update_kernel(plan, limit, *refs),
        [square, g_attn, g_exp, *state_a, *state_e, states],
        [block_a] * 3 + [block_e] * 3 + [((chunk, LANES), bf16)],
    )
    near = [mine] + [swap(mine, "dp", 2 * c) for c in range(1, chips)]
    far = [swap(piece, "dp", 1) for piece in near]
    attn_full, expert_full = put_in_order(plan, near + far)
    new_a = [from_blocks(value, rows_a) for value in (wa, ma, va)]
    new_e = [from_blocks(value, rows_e)[None] for value in (we, me, ve)]
    return (*new_a, *new_e, attn_full, expert_full)


def solution(mesh):
    return jax.shard_map(
        body,
        mesh=mesh,
        in_specs=(
            P(("expert", "dp"), None),
            P(("expert", "dp"), None),
            P("expert", "dp", None),
            P("expert", "dp", None),
            P(("expert", "dp"), None),
            P(("expert", "dp"), None),
            P(("expert", "dp"), None),
            P("expert", "dp", None),
            P("expert", "dp", None),
            P("expert", "dp", None),
        ),
        out_specs=(
            P(("expert", "dp"), None),
            P(("expert", "dp"), None),
            P(("expert", "dp"), None),
            P("expert", "dp", None),
            P("expert", "dp", None),
            P("expert", "dp", None),
            P(),
            P("expert", None, None),
        ),
        check_vma=False,
    )
```

```python
import math

import jax
import jax.numpy as jnp
from jax import lax
from jax.experimental import pallas as pl
from jax.experimental.pallas import tpu as pltpu
from jax.sharding import PartitionSpec as P

beta_first = 0.9
beta_second = 0.95
bias_first = 1.0 - 0.9**10
bias_second = 1.0 - 0.95**10
learn_rate = 0.01
decay_rate = 0.1
adam_eps = 1e-08

LANES = 128
f32, bf16 = jnp.float32, jnp.bfloat16


def adamw(grad, weight, moment, second, factor):
    scaled = factor * grad
    moment_new = beta_first * moment + (1.0 - beta_first) * scaled
    second_new = beta_second * second + (1.0 - beta_second) * scaled * scaled
    update = moment_new / bias_first / (jnp.sqrt(second_new / bias_second) + adam_eps)
    weight_new = weight - learn_rate * (update + decay_rate * weight)
    return (weight_new, moment_new, second_new)


class Plan:
    def __init__(self, n_expert, n_dp, rows_a, rows_e, width):
        self.n_expert, self.n_dp, self.rows_a, self.rows_e = n_expert, n_dp, rows_a, rows_e
        self.width = width
        self.chips = n_dp // 2
        self.blocks = width // LANES
        self.size_a = self.blocks * rows_a
        self.size_e = self.blocks * rows_e
        self.all_a = n_expert * self.size_a
        self.chunk = self.all_a + self.size_e

    def places(self, block):
        attn = [
            (e * self.rows_a + r, e * self.size_a + block * self.rows_a + r)
            for e in range(self.n_expert)
            for r in range(self.rows_a)
        ]
        exp = [(r, self.all_a + block * self.rows_e + r) for r in range(self.rows_e)]
        return attn, exp


def dot(left, right):
    return lax.dot_general(left, right, (((1,), (0,)), ((), ())), preferred_element_type=f32)


def call(kernel, args, outs, scratch=(), specs=None):
    whole = pl.BlockSpec(memory_space=pltpu.VMEM)
    return pl.pallas_call(
        kernel,
        in_specs=specs or [whole] * len(args),
        out_specs=[whole] * len(outs),
        out_shape=[jax.ShapeDtypeStruct(shape, dtype) for shape, dtype in outs],
        scratch_shapes=list(scratch),
        compiler_params=pltpu.CompilerParams(vmem_limit_bytes=48 * 1024 * 1024),
    )(*args)


def two_pieces(value):
    high = value.astype(bf16).astype(f32)
    return high, (value - high).astype(bf16).astype(f32)


def by_eights(value):
    return jnp.sum(value.reshape(-1, 8, LANES), axis=0)


STEPS = 4


def each(count, step, unrolled):
    if unrolled:
        for i in range(count):
            step(i)
    else:
        pl.loop(0, count)(step)


def terms_kernel(plan, act_a, dy_a, act_e, dy_e, w, m, v, full, send, pack, act_a_v, dy_a_v, act_e_v, dy_e_v, state, sems):
    tile = plan.width // STEPS
    small = [
        pltpu.make_async_copy(act_a, act_a_v, sems.at[0]),
        pltpu.make_async_copy(act_e, act_e_v, sems.at[1]),
    ]
    big = []
    for t in range(STEPS):
        cols = pl.ds(t * tile, tile)
        big.append(pltpu.make_async_copy(dy_a.at[:, cols], dy_a_v.at[:, cols], sems.at[2 + 2 * t]))
        big.append(pltpu.make_async_copy(dy_e.at[:, cols], dy_e_v.at[:, cols], sems.at[3 + 2 * t]))
    extra = [pltpu.make_async_copy(ref, state.at[i], sems.at[2 + 2 * STEPS + i]) for i, ref in enumerate((w, m, v))]
    for copy in small + big + extra:
        copy.start()

    me = lax.axis_index("dp")

    def pick(groups, per_owner, count):
        shape = (groups * plan.n_dp, count)
        row = lax.broadcasted_iota(jnp.int32, shape, 0)
        col = lax.broadcasted_iota(jnp.int32, shape, 1)
        group, place = row // plan.n_dp, row % plan.n_dp
        owner = 2 * (place % plan.chips) + ((place // plan.chips) ^ (me % 2))
        want = ((group // per_owner) * plan.n_dp + owner) * per_owner + group % per_owner
        return (want == col).astype(bf16)

    for copy in small:
        copy.wait()
    left_a = dot(pick(plan.n_expert * plan.rows_a, plan.rows_a, act_a.shape[0]), act_a_v[...]).astype(bf16)
    left_e = dot(pick(plan.rows_e, plan.rows_e, act_e.shape[0]), act_e_v[...]).astype(bf16)
    n_dp = plan.n_dp
    for t in range(STEPS):
        cols = pl.ds(t * tile, tile)
        big[2 * t].wait()
        terms_a = dot(left_a, dy_a_v[:, cols])
        big[2 * t + 1].wait()
        terms_e = dot(left_e, dy_e_v[:, cols])
        for b in range(tile // LANES):
            attn, exp = plan.places(t * (tile // LANES) + b)
            span = slice(b * LANES, (b + 1) * LANES)
            for terms, places in ((terms_a, attn), (terms_e, exp)):
                for group, start in places:
                    full[pl.ds(start, n_dp, stride=plan.chunk), :] = terms[group * n_dp : (group + 1) * n_dp, span]
    for c in range(plan.chips):
        send[pl.ds(c * plan.chunk, plan.chunk), :] = full[
            pl.ds((plan.chips + c) * plan.chunk, plan.chunk), :
        ].astype(bf16)
    for copy in extra:
        copy.wait()
    size = plan.size_a
    high, low = two_pieces(state[0])
    for i, value in enumerate((high, low, state[1], state[2])):
        pack[pl.ds(i * size, size), :] = value.astype(bf16)


def make_terms(plan, act_a, dy_a, act_e, dy_e, w, m, v):
    args = (act_a, dy_a, act_e, dy_e, w, m, v)
    half = plan.chips * plan.chunk
    return call(
        lambda *refs: terms_kernel(plan, *refs),
        args,
        [((2 * half, LANES), f32), ((half, LANES), bf16), ((4 * plan.size_a, LANES), bf16)],
        [
            pltpu.VMEM(act_a.shape, bf16),
            pltpu.VMEM(dy_a.shape, bf16),
            pltpu.VMEM(act_e.shape, bf16),
            pltpu.VMEM(dy_e.shape, bf16),
            pltpu.VMEM((3,) + w.shape, f32),
            pltpu.SemaphoreType.DMA((5 + 2 * STEPS,)),
        ],
        [pl.BlockSpec(memory_space=pltpu.HBM)] * len(args),
    )


def share_kernel(plan, got, payload, g_exp):
    total = jnp.sum(got[...].astype(f32), axis=0)
    a = plan.all_a
    exp = total[a:]
    g_exp[...] = exp
    payload[:a, :] = total[:a].astype(bf16)
    payload[a:, :] = jnp.concatenate(two_pieces(by_eights(exp * exp)), axis=0).astype(bf16)


def pair_sum(plan, mine, other):
    a = plan.all_a
    attn = mine[:a, :].astype(f32) + other[:a, :].astype(f32)
    one, two = mine[a:, :].astype(f32), other[a:, :].astype(f32)
    return attn, (one[:8] + one[8:]) + (two[:8] + two[8:])


def again_kernel(plan, mine, other, *refs):
    packs, (payload, states) = refs[:-2], refs[-2:]
    attn, square = pair_sum(plan, mine, other)
    a = plan.all_a
    payload[:a, :] = attn.astype(bf16)
    payload[a:, :] = jnp.concatenate(two_pieces(square), axis=0).astype(bf16)
    place = lax.axis_index("expert")
    for q, pack in enumerate(packs):
        states[place ^ q] = pack[...]


def last_kernel(plan, mine, other, g_attn, square):
    attn, partial = pair_sum(plan, mine, other)
    g_attn[...] = attn
    square[...] = jnp.broadcast_to((partial + by_eights(attn * attn))[None], square.shape)


def update_kernel(plan, limit, *refs):
    square, g_attn, g_exp, wa, ma, va, we, me, ve = refs[:9]
    states, wa_new, ma_new, va_new, we_new, me_new, ve_new, mine = refs[9:]
    norm = jnp.sqrt(jnp.sum(jnp.sum(square[...], axis=0), keepdims=True))
    factor = jnp.minimum(1.0, limit / (norm + 1e-06))
    place = lax.axis_index("expert")
    size = plan.size_a

    def rows(expert):
        return pl.ds(pl.multiple_of(expert * size, 16), size)

    wa_new[...], ma_new[...], va_new[...] = adamw(g_attn[rows(place), :], wa[...], ma[...], va[...], factor)
    for e in range(plan.n_expert):
        high, low, moment, second = [states[e, pl.ds(i * size, size), :].astype(f32) for i in range(4)]
        weight, _, _ = adamw(g_attn[pl.ds(e * size, size), :], high + low, moment, second, factor)
        for c in range(plan.chips):
            mine[c, pl.ds(e * size, size), :] = weight.astype(bf16)
    weight, moment, second = adamw(g_exp[...], we[...], me[...], ve[...], factor)
    we_new[...], me_new[...], ve_new[...] = weight, moment, second
    for c in range(plan.chips):
        mine[c, plan.all_a :, :] = weight.astype(bf16)


def order_kernel(plan, *refs):
    n_dp = plan.n_dp
    near, far, attn, exp, rows, rows_a, rows_e = refs
    core = lax.axis_index("dp") % 2
    for part, bit in ((near, core), (far, 1 - core)):
        for c in range(plan.chips):
            start = pl.multiple_of((2 * c + bit) * plan.chunk, 16)
            rows[pl.ds(start, plan.chunk), :] = part[c].astype(f32)
    count_a, count_e = attn.shape[0], exp.shape[1]

    def one(b):
        places_a, places_e = plan.places(b)
        span = pl.ds(b * LANES if isinstance(b, int) else pl.multiple_of(b * LANES, LANES), LANES)
        values = [rows[pl.ds(start, n_dp, stride=plan.chunk), :] for _, start in places_a]
        if plan.rows_a == 1:
            attn[:, span] = jnp.concatenate(values, axis=0).astype(bf16)
        else:
            for (group, _), value in zip(places_a, values):
                start = (group // plan.rows_a) * n_dp * plan.rows_a + group % plan.rows_a
                rows_a[pl.ds(start, n_dp, stride=plan.rows_a), :] = value
            attn[:, span] = rows_a[...].astype(bf16)
        for r, start in places_e:
            rows_e[pl.ds(b * count_e + r, n_dp, stride=plan.rows_e), :] = rows[
                pl.ds(start, n_dp, stride=plan.chunk), :
            ]

    each(plan.blocks, one, n_dp <= 8)
    for b in range(plan.blocks):
        exp[0, :, pl.ds(b * LANES, LANES)] = rows_e[pl.ds(b * count_e, count_e), :].astype(bf16)


def put_in_order(plan, parts):
    count_a = plan.n_expert * plan.n_dp * plan.rows_a
    count_e = plan.n_dp * plan.rows_e
    return call(
        lambda *refs: order_kernel(plan, *refs),
        parts,
        [((count_a, plan.width), bf16), ((1, count_e, plan.width), bf16)],
        [
            pltpu.VMEM((plan.n_dp * plan.chunk, LANES), f32),
            pltpu.VMEM((count_a, LANES), f32),
            pltpu.VMEM((plan.blocks * count_e, LANES), f32),
        ],
    )


def swap(value, axis, distance):
    size = lax.axis_size(axis)
    return lax.ppermute(value, axis, [(i, i ^ distance) for i in range(size)])


def between_chips(value):
    size = lax.axis_size("dp")
    groups = [list(range(core, size, 2)) for core in range(2)]
    return lax.all_to_all(value, "dp", 0, 0, axis_index_groups=groups, tiled=True)


def to_blocks(value):
    rows, width = value.shape
    return value.reshape(rows, width // LANES, LANES).transpose(1, 0, 2).reshape(-1, LANES)


def from_blocks(value, rows):
    return value.reshape(-1, rows, LANES).transpose(1, 0, 2).reshape(rows, -1)


def body(act_attn, dy_attn, act_exp, dy_exp, w_attn, m_attn, v_attn, w_exp, m_exp, v_exp):
    width = w_attn.shape[1]
    n_expert = lax.axis_size("expert")
    n_dp = lax.axis_size("dp")
    rows_a, rows_e = w_attn.shape[0], w_exp.shape[1]
    plan = Plan(n_expert, n_dp, rows_a, rows_e, width)
    total_params = width * (act_attn.shape[1] + n_expert * act_exp.shape[2])
    limit = 0.5 * math.sqrt(total_params)
    chips, chunk = plan.chips, plan.chunk
    state_a = [to_blocks(value) for value in (w_attn, m_attn, v_attn)]
    state_e = [to_blocks(value[0]) for value in (w_exp, m_exp, v_exp)]

    held = [pltpu.with_memory_space_constraint(x, pltpu.HBM) for x in (act_attn.T, dy_attn, act_exp[0].T, dy_exp[0])]
    full, send, pack = make_terms(plan, *held, *[pltpu.with_memory_space_constraint(x, pltpu.HBM) for x in state_a])
    got = swap(send, "dp", 1)
    packs = [pack] + [swap(pack, "expert", q) for q in range(1, n_expert)]
    sums = (full[: chips * chunk] + got.astype(f32)).astype(bf16).reshape(chips, chunk, LANES)
    got = between_chips(sums)
    shared = ((plan.all_a + 16, LANES), bf16)
    payload, g_exp = call(
        lambda *refs: share_kernel(plan, *refs), [got], [shared, ((plan.size_e, LANES), f32)]
    )
    other = swap(payload, "expert", 1)
    payload, states = call(
        lambda *refs: again_kernel(plan, *refs),
        [payload, other, *packs],
        [shared, ((n_expert, 4 * plan.size_a, LANES), bf16)],
    )
    other = swap(payload, "expert", 2)
    g_attn, square = call(
        lambda *refs: last_kernel(plan, *refs), [payload, other], [((plan.all_a, LANES), f32), ((n_dp, 8, LANES), f32)]
    )
    square = lax.all_to_all(square, "dp", 0, 0, tiled=True)
    block_a, block_e = ((plan.size_a, LANES), f32), ((plan.size_e, LANES), f32)
    wa, ma, va, we, me, ve, mine = call(
        lambda *refs: update_kernel(plan, limit, *refs),
        [square, g_attn, g_exp, *state_a, *state_e, states],
        [block_a] * 3 + [block_e] * 3 + [((chips, chunk, LANES), bf16)],
    )
    near = between_chips(mine)
    far = swap(near, "dp", 1)
    attn_full, expert_full = put_in_order(plan, [near, far])
    new_a = [from_blocks(value, rows_a) for value in (wa, ma, va)]
    new_e = [from_blocks(value, rows_e)[None] for value in (we, me, ve)]
    return (*new_a, *new_e, attn_full, expert_full)


def solution(mesh):
    return jax.shard_map(
        body,
        mesh=mesh,
        in_specs=(
            P(("expert", "dp"), None),
            P(("expert", "dp"), None),
            P("expert", "dp", None),
            P("expert", "dp", None),
            P(("expert", "dp"), None),
            P(("expert", "dp"), None),
            P(("expert", "dp"), None),
            P("expert", "dp", None),
            P("expert", "dp", None),
            P("expert", "dp", None),
        ),
        out_specs=(
            P(("expert", "dp"), None),
            P(("expert", "dp"), None),
            P(("expert", "dp"), None),
            P("expert", "dp", None),
            P("expert", "dp", None),
            P("expert", "dp", None),
            P(),
            P("expert", None, None),
        ),
        check_vma=False,
    )
```

```python
import math

import jax
import jax.numpy as jnp
from jax import lax
from jax.experimental import pallas as pl
from jax.experimental.pallas import tpu as pltpu
from jax.sharding import PartitionSpec as P

beta_first = 0.9
beta_second = 0.95
bias_first = 1.0 - 0.9**10
bias_second = 1.0 - 0.95**10
learn_rate = 0.01
decay_rate = 0.1
adam_eps = 1e-08

LANES = 128
f32, bf16 = jnp.float32, jnp.bfloat16


def adamw(grad, weight, moment, second, factor):
    scaled = factor * grad
    moment_new = beta_first * moment + (1.0 - beta_first) * scaled
    second_new = beta_second * second + (1.0 - beta_second) * scaled * scaled
    update = moment_new / bias_first / (jnp.sqrt(second_new / bias_second) + adam_eps)
    weight_new = weight - learn_rate * (update + decay_rate * weight)
    return (weight_new, moment_new, second_new)


class Plan:
    def __init__(self, n_expert, n_dp, rows_a, rows_e, width):
        self.n_expert, self.n_dp, self.rows_a, self.rows_e = n_expert, n_dp, rows_a, rows_e
        self.width = width
        self.chips = n_dp // 2
        self.blocks = width // LANES
        self.size_a = self.blocks * rows_a
        self.size_e = self.blocks * rows_e
        self.all_a = n_expert * self.size_a
        self.chunk = self.all_a + self.size_e

    def places(self, block):
        attn = [
            (e * self.rows_a + r, e * self.size_a + block * self.rows_a + r)
            for e in range(self.n_expert)
            for r in range(self.rows_a)
        ]
        exp = [(r, self.all_a + block * self.rows_e + r) for r in range(self.rows_e)]
        return attn, exp


def dot(left, right):
    return lax.dot_general(left, right, (((1,), (0,)), ((), ())), preferred_element_type=f32)


def call(kernel, args, outs, scratch=(), specs=None):
    whole = pl.BlockSpec(memory_space=pltpu.VMEM)
    return pl.pallas_call(
        kernel,
        in_specs=specs or [whole] * len(args),
        out_specs=[whole] * len(outs),
        out_shape=[jax.ShapeDtypeStruct(shape, dtype) for shape, dtype in outs],
        scratch_shapes=list(scratch),
        compiler_params=pltpu.CompilerParams(vmem_limit_bytes=48 * 1024 * 1024),
    )(*args)


def two_pieces(value):
    high = value.astype(bf16).astype(f32)
    return high, (value - high).astype(bf16).astype(f32)


def by_eights(value):
    return jnp.sum(value.reshape(-1, 8, LANES), axis=0)


STEPS = 4


def each(count, step, unrolled):
    if unrolled:
        for i in range(count):
            step(i)
    else:
        pl.loop(0, count)(step)


def terms_kernel(plan, act_a, dy_a, act_e, dy_e, full, send, act_a_v, dy_a_v, act_e_v, dy_e_v, sems):
    tile = plan.width // STEPS
    small = [
        pltpu.make_async_copy(act_a, act_a_v, sems.at[0]),
        pltpu.make_async_copy(act_e, act_e_v, sems.at[1]),
    ]
    big = []
    for t in range(STEPS):
        cols = pl.ds(t * tile, tile)
        big.append(pltpu.make_async_copy(dy_a.at[:, cols], dy_a_v.at[:, cols], sems.at[2 + 2 * t]))
        big.append(pltpu.make_async_copy(dy_e.at[:, cols], dy_e_v.at[:, cols], sems.at[3 + 2 * t]))
    for copy in small + big:
        copy.start()

    me = lax.axis_index("dp")

    def pick(groups, per_owner, count):
        shape = (groups * plan.n_dp, count)
        row = lax.broadcasted_iota(jnp.int32, shape, 0)
        col = lax.broadcasted_iota(jnp.int32, shape, 1)
        group, place = row // plan.n_dp, row % plan.n_dp
        owner = (2 * (place % plan.chips) + place // plan.chips) ^ me
        want = ((group // per_owner) * plan.n_dp + owner) * per_owner + group % per_owner
        return (want == col).astype(bf16)

    for copy in small:
        copy.wait()
    left_a = dot(pick(plan.n_expert * plan.rows_a, plan.rows_a, act_a.shape[0]), act_a_v[...]).astype(bf16)
    left_e = dot(pick(plan.rows_e, plan.rows_e, act_e.shape[0]), act_e_v[...]).astype(bf16)
    n_dp = plan.n_dp
    for t in range(STEPS):
        cols = pl.ds(t * tile, tile)
        big[2 * t].wait()
        terms_a = dot(left_a, dy_a_v[:, cols])
        big[2 * t + 1].wait()
        terms_e = dot(left_e, dy_e_v[:, cols])
        for b in range(tile // LANES):
            attn, exp = plan.places(t * (tile // LANES) + b)
            span = slice(b * LANES, (b + 1) * LANES)
            for terms, places in ((terms_a, attn), (terms_e, exp)):
                for group, start in places:
                    full[pl.ds(start, n_dp, stride=plan.chunk), :] = terms[group * n_dp : (group + 1) * n_dp, span]
    for c in range(plan.chips):
        send[pl.ds(c * plan.chunk, plan.chunk), :] = full[
            pl.ds((plan.chips + c) * plan.chunk, plan.chunk), :
        ].astype(bf16)


def make_terms(plan, *args):
    act_a, dy_a, act_e, dy_e = args
    half = plan.chips * plan.chunk
    return call(
        lambda *refs: terms_kernel(plan, *refs),
        args,
        [((2 * half, LANES), f32), ((half, LANES), bf16)],
        [
            pltpu.VMEM(act_a.shape, bf16),
            pltpu.VMEM(dy_a.shape, bf16),
            pltpu.VMEM(act_e.shape, bf16),
            pltpu.VMEM(dy_e.shape, bf16),
            pltpu.SemaphoreType.DMA((2 + 2 * STEPS,)),
        ],
        [pl.BlockSpec(memory_space=pltpu.HBM)] * len(args),
    )


def share_kernel(plan, *refs):
    own, got, (payload, g_exp) = refs[0], refs[1:-2], refs[-2:]
    total = own[...]
    for ref in got:
        total = total + ref[...].astype(f32)
    a = plan.all_a
    exp = total[a:]
    g_exp[...] = exp
    payload[:a, :] = total[:a].astype(bf16)
    payload[a:, :] = jnp.concatenate(two_pieces(by_eights(exp * exp)), axis=0).astype(bf16)


def pair_sum(plan, mine, other):
    a = plan.all_a
    attn = mine[:a, :].astype(f32) + other[:a, :].astype(f32)
    one, two = mine[a:, :].astype(f32), other[a:, :].astype(f32)
    return attn, (one[:8] + one[8:]) + (two[:8] + two[8:])


def again_kernel(plan, mine, other, payload):
    attn, square = pair_sum(plan, mine, other)
    a = plan.all_a
    payload[:a, :] = attn.astype(bf16)
    payload[a:, :] = jnp.concatenate(two_pieces(square), axis=0).astype(bf16)


def last_kernel(plan, mine, other, g_attn, square):
    attn, partial = pair_sum(plan, mine, other)
    g_attn[...] = attn
    square[...] = partial + by_eights(attn * attn)


def update_kernel(plan, limit, *refs):
    square, g_attn, g_exp, wa, ma, va, we, me, ve = refs[:9]
    states, wa_new, ma_new, va_new, we_new, me_new, ve_new, mine = refs[9:]
    norm = jnp.sqrt(jnp.sum(square[...], keepdims=True))
    factor = jnp.minimum(1.0, limit / (norm + 1e-06))
    place = lax.axis_index("expert")
    size = plan.size_a

    def rows(expert):
        return pl.ds(pl.multiple_of(expert * size, 16), size)

    wa_new[...], ma_new[...], va_new[...] = adamw(g_attn[rows(place), :], wa[...], ma[...], va[...], factor)
    for e in range(plan.n_expert):
        old = [states[e, pl.ds(i * size, size), :] for i in range(3)]
        weight, _, _ = adamw(g_attn[pl.ds(e * size, size), :], *old, factor)
        mine[pl.ds(e * size, size), :] = weight.astype(bf16)
    weight, moment, second = adamw(g_exp[...], we[...], me[...], ve[...], factor)
    we_new[...], me_new[...], ve_new[...] = weight, moment, second
    mine[plan.all_a :, :] = weight.astype(bf16)


def order_kernel(plan, *refs):
    n_dp = plan.n_dp
    parts, (attn, exp, rows, rows_a, rows_e) = refs[:n_dp], refs[n_dp:]
    me = lax.axis_index("dp")
    for i, part in enumerate(parts):
        owner = (2 * (i % plan.chips) + i // plan.chips) ^ me
        rows[pl.ds(pl.multiple_of(owner * plan.chunk, 16), plan.chunk), :] = part[...].astype(f32)
    count_a, count_e = attn.shape[0], exp.shape[1]

    def one(b):
        places_a, places_e = plan.places(b)
        span = pl.ds(b * LANES if isinstance(b, int) else pl.multiple_of(b * LANES, LANES), LANES)
        values = [rows[pl.ds(start, n_dp, stride=plan.chunk), :] for _, start in places_a]
        if plan.rows_a == 1:
            attn[:, span] = jnp.concatenate(values, axis=0).astype(bf16)
        else:
            for (group, _), value in zip(places_a, values):
                start = (group // plan.rows_a) * n_dp * plan.rows_a + group % plan.rows_a
                rows_a[pl.ds(start, n_dp, stride=plan.rows_a), :] = value
            attn[:, span] = rows_a[...].astype(bf16)
        for r, start in places_e:
            rows_e[pl.ds(b * count_e + r, n_dp, stride=plan.rows_e), :] = rows[
                pl.ds(start, n_dp, stride=plan.chunk), :
            ]

    each(plan.blocks, one, n_dp <= 8)
    for b in range(plan.blocks):
        exp[0, :, pl.ds(b * LANES, LANES)] = rows_e[pl.ds(b * count_e, count_e), :].astype(bf16)


def put_in_order(plan, parts):
    count_a = plan.n_expert * plan.n_dp * plan.rows_a
    count_e = plan.n_dp * plan.rows_e
    return call(
        lambda *refs: order_kernel(plan, *refs),
        parts,
        [((count_a, plan.width), bf16), ((1, count_e, plan.width), bf16)],
        [
            pltpu.VMEM((plan.n_dp * plan.chunk, LANES), f32),
            pltpu.VMEM((count_a, LANES), f32),
            pltpu.VMEM((plan.blocks * count_e, LANES), f32),
        ],
    )


def swap(value, axis, distance):
    size = lax.axis_size(axis)
    return lax.ppermute(value, axis, [(i, i ^ distance) for i in range(size)])


def to_blocks(value):
    rows, width = value.shape
    return value.reshape(rows, width // LANES, LANES).transpose(1, 0, 2).reshape(-1, LANES)


def from_blocks(value, rows):
    return value.reshape(-1, rows, LANES).transpose(1, 0, 2).reshape(rows, -1)


def body(act_attn, dy_attn, act_exp, dy_exp, w_attn, m_attn, v_attn, w_exp, m_exp, v_exp):
    width = w_attn.shape[1]
    n_expert = lax.axis_size("expert")
    n_dp = lax.axis_size("dp")
    rows_a, rows_e = w_attn.shape[0], w_exp.shape[1]
    plan = Plan(n_expert, n_dp, rows_a, rows_e, width)
    total_params = width * (act_attn.shape[1] + n_expert * act_exp.shape[2])
    limit = 0.5 * math.sqrt(total_params)
    chips, chunk = plan.chips, plan.chunk
    state_a = [to_blocks(value) for value in (w_attn, m_attn, v_attn)]
    state_e = [to_blocks(value[0]) for value in (w_exp, m_exp, v_exp)]

    held = [pltpu.with_memory_space_constraint(x, pltpu.HBM) for x in (act_attn.T, dy_attn, act_exp[0].T, dy_exp[0])]
    states = lax.all_gather(jnp.concatenate(state_a), "expert")
    full, send = make_terms(plan, *held)
    got = swap(send, "dp", 1)
    sums = [
        full[c * chunk : (c + 1) * chunk] + got[c * chunk : (c + 1) * chunk].astype(f32) for c in range(chips)
    ]
    got = [swap(sums[c].astype(bf16), "dp", 2 * c) for c in range(1, chips)]
    shared = ((plan.all_a + 16, LANES), bf16)
    payload, g_exp = call(
        lambda *refs: share_kernel(plan, *refs), [sums[0]] + got, [shared, ((plan.size_e, LANES), f32)]
    )
    distance = 1
    while 2 * distance < n_expert:
        other = swap(payload, "expert", distance)
        (payload,) = call(lambda *refs: again_kernel(plan, *refs), [payload, other], [shared])
        distance *= 2
    other = swap(payload, "expert", distance)
    g_attn, square = call(
        lambda *refs: last_kernel(plan, *refs), [payload, other], [((plan.all_a, LANES), f32), ((8, LANES), f32)]
    )
    distance = 1
    while distance < n_dp:
        square = square + swap(square, "dp", distance)
        distance *= 2
    block_a, block_e = ((plan.size_a, LANES), f32), ((plan.size_e, LANES), f32)
    wa, ma, va, we, me, ve, mine = call(
        lambda *refs: update_kernel(plan, limit, *refs),
        [square, g_attn, g_exp, *state_a, *state_e, states],
        [block_a] * 3 + [block_e] * 3 + [((chunk, LANES), bf16)],
    )
    near = [mine] + [swap(mine, "dp", 2 * c) for c in range(1, chips)]
    far = [swap(piece, "dp", 1) for piece in near]
    attn_full, expert_full = put_in_order(plan, near + far)
    new_a = [from_blocks(value, rows_a) for value in (wa, ma, va)]
    new_e = [from_blocks(value, rows_e)[None] for value in (we, me, ve)]
    return (*new_a, *new_e, attn_full, expert_full)


def solution(mesh):
    return jax.shard_map(
        body,
        mesh=mesh,
        in_specs=(
            P(("expert", "dp"), None),
            P(("expert", "dp"), None),
            P("expert", "dp", None),
            P("expert", "dp", None),
            P(("expert", "dp"), None),
            P(("expert", "dp"), None),
            P(("expert", "dp"), None),
            P("expert", "dp", None),
            P("expert", "dp", None),
            P("expert", "dp", None),
        ),
        out_specs=(
            P(("expert", "dp"), None),
            P(("expert", "dp"), None),
            P(("expert", "dp"), None),
            P("expert", "dp", None),
            P("expert", "dp", None),
            P("expert", "dp", None),
            P(),
            P("expert", None, None),
        ),
        check_vma=False,
    )
```

```python
import math

import jax
import jax.numpy as jnp
from jax import lax
from jax.experimental import pallas as pl
from jax.experimental.pallas import tpu as pltpu
from jax.sharding import PartitionSpec as P

beta_first = 0.9
beta_second = 0.95
bias_first = 1.0 - 0.9**10
bias_second = 1.0 - 0.95**10
learn_rate = 0.01
decay_rate = 0.1
adam_eps = 1e-08

LANES = 128
STEPS = 4
f32, bf16 = jnp.float32, jnp.bfloat16


def adamw(grad, weight, moment, second, factor):
    scaled = factor * grad
    moment_new = beta_first * moment + (1.0 - beta_first) * scaled
    second_new = beta_second * second + (1.0 - beta_second) * scaled * scaled
    update = moment_new / bias_first / (jnp.sqrt(second_new / bias_second) + adam_eps)
    weight_new = weight - learn_rate * (update + decay_rate * weight)
    return (weight_new, moment_new, second_new)


class Plan:
    def __init__(self, n_expert, n_dp, rows_a, rows_e, width):
        self.n_expert, self.n_dp, self.rows_a, self.rows_e = n_expert, n_dp, rows_a, rows_e
        self.width = width
        self.chips = n_dp // 2
        self.blocks = width // LANES
        self.size_a = self.blocks * rows_a
        self.size_e = self.blocks * rows_e
        self.all_a = n_expert * self.size_a
        self.chunk = self.all_a + self.size_e
        self.pair = 2 * self.chunk
        self.pack = 3 * (self.size_a + self.size_e)

    def places(self, block):
        attn = [
            (e * self.rows_a + r, e * self.size_a + block * self.rows_a + r)
            for e in range(self.n_expert)
            for r in range(self.rows_a)
        ]
        exp = [(r, self.all_a + block * self.rows_e + r) for r in range(self.rows_e)]
        return attn, exp


def dot(left, right):
    return lax.dot_general(left, right, (((1,), (0,)), ((), ())), preferred_element_type=f32)


def call(kernel, args, outs, scratch=(), in_specs=None, out_specs=None):
    whole = pl.BlockSpec(memory_space=pltpu.VMEM)
    return pl.pallas_call(
        kernel,
        in_specs=in_specs or [whole] * len(args),
        out_specs=out_specs or [whole] * len(outs),
        out_shape=[jax.ShapeDtypeStruct(shape, dtype) for shape, dtype in outs],
        scratch_shapes=list(scratch),
        compiler_params=pltpu.CompilerParams(vmem_limit_bytes=56 * 1024 * 1024),
    )(*args)


def two_pieces(value):
    high = value.astype(bf16).astype(f32)
    return jnp.concatenate([high, value - high], axis=0).astype(bf16)


def one_value(pieces):
    pieces = pieces.astype(f32)
    half = pieces.shape[0] // 2
    return pieces[:half] + pieces[half:]


def by_eights(value):
    return jnp.sum(value.reshape(-1, 8, LANES), axis=0)


def each(count, step, unrolled):
    if unrolled:
        for i in range(count):
            step(i)
    else:
        pl.loop(0, count)(step)


def aligned(index, unit):
    return index * unit if isinstance(index, int) else pl.multiple_of(index * unit, unit)


def terms_kernel(plan, act_a, dy_a, act_e, dy_e, wa, ma, va, we, me, ve, full, send, *scratch):
    act_a_v, dy_a_v, act_e_v, dy_e_v, state_a, state_e, sems = scratch
    tile = plan.width // STEPS
    small = [
        pltpu.make_async_copy(act_a, act_a_v, sems.at[0]),
        pltpu.make_async_copy(act_e, act_e_v, sems.at[1]),
    ]
    big = []
    for t in range(STEPS):
        cols = pl.ds(t * tile, tile)
        big.append(pltpu.make_async_copy(dy_a.at[:, cols], dy_a_v.at[:, cols], sems.at[2 + 2 * t]))
        big.append(pltpu.make_async_copy(dy_e.at[:, cols], dy_e_v.at[:, cols], sems.at[3 + 2 * t]))
    base = 2 + 2 * STEPS
    extra = [pltpu.make_async_copy(ref, state_a.at[i], sems.at[base + i]) for i, ref in enumerate((wa, ma, va))]
    extra += [pltpu.make_async_copy(ref, state_e.at[i], sems.at[base + 3 + i]) for i, ref in enumerate((we, me, ve))]
    for copy in small + big + extra:
        copy.start()

    chip = lax.axis_index("dp") // 2
    n_dp = plan.n_dp

    def pick(groups, per_owner, count):
        shape = (groups * n_dp, count)
        row = lax.broadcasted_iota(jnp.int32, shape, 0)
        col = lax.broadcasted_iota(jnp.int32, shape, 1)
        group, place = row // n_dp, row % n_dp
        owner = 2 * ((place // 2) ^ chip) + place % 2
        want = ((group // per_owner) * n_dp + owner) * per_owner + group % per_owner
        return (want == col).astype(bf16)

    pick_a = pick(plan.n_expert * plan.rows_a, plan.rows_a, act_a.shape[0])
    pick_e = pick(plan.rows_e, plan.rows_e, act_e.shape[0])
    for copy in small:
        copy.wait()
    left_a = dot(pick_a, act_a_v[...]).astype(bf16)
    left_e = dot(pick_e, act_e_v[...]).astype(bf16)
    for t in range(STEPS):
        cols = pl.ds(t * tile, tile)
        big[2 * t].wait()
        terms_a = dot(left_a, dy_a_v[:, cols])
        big[2 * t + 1].wait()
        terms_e = dot(left_e, dy_e_v[:, cols])
        for b in range(tile // LANES):
            attn, exp = plan.places(t * (tile // LANES) + b)
            span = slice(b * LANES, (b + 1) * LANES)
            for terms, places in ((terms_a, attn), (terms_e, exp)):
                for group, start in places:
                    full[pl.ds(start, n_dp, stride=plan.chunk), :] = terms[group * n_dp : (group + 1) * n_dp, span]
    for copy in extra:
        copy.wait()
    for i in range(3):
        send[pl.ds(i * plan.size_a, plan.size_a), :] = state_a[i].astype(bf16)
        send[pl.ds(3 * plan.size_a + i * plan.size_e, plan.size_e), :] = state_e[i].astype(bf16)

    def cast(p):
        send[pl.ds(plan.pack + aligned(p, plan.chunk), plan.chunk), :] = full[
            pl.ds(aligned(p, plan.chunk), plan.chunk), :
        ].astype(bf16)

    each(n_dp, cast, n_dp <= 8)


def make_terms(plan, args):
    act_a, dy_a, act_e, dy_e = args[:4]
    rows = n_rows = plan.n_dp * plan.chunk
    return call(
        lambda *refs: terms_kernel(plan, *refs),
        [pltpu.with_memory_space_constraint(arg, pltpu.HBM) for arg in args],
        [((rows, LANES), f32), ((plan.pack + n_rows, LANES), bf16)],
        [
            pltpu.VMEM(act_a.shape, bf16),
            pltpu.VMEM(dy_a.shape, bf16),
            pltpu.VMEM(act_e.shape, bf16),
            pltpu.VMEM(dy_e.shape, bf16),
            pltpu.VMEM((3, plan.size_a, LANES), f32),
            pltpu.VMEM((3, plan.size_e, LANES), f32),
            pltpu.SemaphoreType.DMA((8 + 2 * STEPS,)),
        ],
        in_specs=[pl.BlockSpec(memory_space=pltpu.HBM)] * len(args),
    )


def share_kernel(plan, *refs):
    own, got, (payload, g_exp) = refs[0], refs[1:-2], refs[-2:]
    square = jnp.zeros((8, LANES), f32)
    for k in range(2):
        a, e = plan.all_a, plan.size_e

        def total(start, size):
            value = own[pl.ds(start, size), :]
            for ref in got:
                value = value + ref[pl.ds(start, size), :].astype(f32)
            return value

        payload[pl.ds(k * a, a), :] = total(k * plan.chunk, a).astype(bf16)
        exp = total(k * plan.chunk + a, e)
        g_exp[pl.ds(k * e, e), :] = exp.astype(bf16)
        square = square + by_eights(exp * exp)
    payload[pl.ds(2 * plan.all_a, 16), :] = two_pieces(square)


def pair_sum(plan, mine, other):
    a = 2 * plan.all_a
    attn = mine[:a, :].astype(f32) + other[:a, :].astype(f32)
    return attn, one_value(mine[a:, :]) + one_value(other[a:, :])


def again_kernel(plan, mine, other, payload):
    attn, square = pair_sum(plan, mine, other)
    a = 2 * plan.all_a
    payload[:a, :] = attn.astype(bf16)
    payload[a:, :] = two_pieces(square)


def last_kernel(plan, mine, other, g_exp, rows):
    attn, square = pair_sum(plan, mine, other)
    square = square + by_eights(attn * attn)
    a, e = plan.all_a, plan.size_e
    for k in range(2):
        rows[pl.ds(k * plan.chunk, a), :] = attn[k * a : (k + 1) * a].astype(bf16)
        rows[pl.ds(k * plan.chunk + a, e), :] = g_exp[pl.ds(k * e, e), :]
    rows[pl.ds(plan.pair, 16), :] = two_pieces(square)


def state_kernel(plan, mine, other, *refs):
    packs, states = refs[:-1], refs[-1]
    place = lax.axis_index("expert")
    a, e = plan.size_a, plan.size_e
    for k, own in enumerate((mine, other)):
        for i in range(3):
            start = (k * 3 + i) * plan.chunk
            for q, pack in enumerate((None,) + packs):
                part = own[pl.ds(i * a, a), :] if pack is None else pack[pl.ds((k * 3 + i) * a, a), :]
                states[pl.ds(pl.multiple_of(start + (place ^ q) * a, 16), a), :] = part
            states[pl.ds(start + plan.all_a, e), :] = own[pl.ds(3 * a + i * e, e), :]


def tree_sum(values):
    while len(values) > 1:
        values = [values[i] + values[i + 1] for i in range(0, len(values), 2)]
    return values[0]


def update_kernel(plan, limit, *refs):
    chips, chunk = plan.chips, plan.chunk
    near_g, far_g, near_s, far_s = [refs[i * chips : (i + 1) * chips] for i in range(4)]
    refs = refs[4 * chips :]
    state, new, (attn, exp) = refs[:6], refs[6:12], refs[12:14]
    held, (rows, rows_a, rows_e, sems) = refs[14:20], refs[20:]
    me, place = lax.axis_index("dp"), lax.axis_index("expert")
    lead = (me % 2) == 1

    def grad(c, start, size):
        return jnp.where(lead, near_g[c][pl.ds(start, size), :], far_g[c][pl.ds(start, size), :])

    def old(c, start, size):
        return jnp.where(lead, far_s[c][pl.ds(start, size), :], near_s[c][pl.ds(start, size), :]).astype(f32)

    square = tree_sum([one_value(grad(c, plan.pair, 16)) for c in range(chips)])
    norm = jnp.sqrt(jnp.sum(square, keepdims=True))
    factor = jnp.minimum(1.0, limit / (norm + 1e-06))

    start = pl.multiple_of((me % 2) * chunk + place * plan.size_a, 16)
    own_a = grad(0, start, plan.size_a).astype(f32)
    start = pl.multiple_of((me % 2) * chunk + plan.all_a, 16)
    own_e = grad(0, start, plan.size_e).astype(f32)
    copies = []
    for b, own in enumerate((own_a, own_e)):
        values = adamw(own, *[ref[...] for ref in state[3 * b : 3 * b + 3]], factor)
        for i, value in enumerate(values):
            held[3 * b + i][...] = value
            copies.append(pltpu.make_async_copy(held[3 * b + i], new[3 * b + i], sems.at[3 * b + i]))
    for copy in copies:
        copy.start()

    piece = plan.size_a
    for c in range(chips):
        for k in range(2):
            owner = 2 * (c ^ (me // 2)) + k

            def one(p):
                weight, moment, second = [old(c, (k * 3 + i) * chunk + aligned(p, piece), piece) for i in range(3)]
                value = grad(c, k * chunk + aligned(p, piece), piece).astype(f32)
                weight, _, _ = adamw(value, weight, moment, second, factor)
                rows[pl.ds(pl.multiple_of(owner * chunk + aligned(p, piece), 16), piece), :] = weight

            each(chunk // piece, one, chips <= 4)

    count_e, n_dp = exp.shape[1], plan.n_dp

    def order(b):
        places_a, places_e = plan.places(b)
        span = pl.ds(aligned(b, LANES), LANES)
        values = [rows[pl.ds(start, n_dp, stride=chunk), :] for _, start in places_a]
        if plan.rows_a == 1:
            attn[:, span] = jnp.concatenate(values, axis=0).astype(bf16)
        else:
            for (group, _), value in zip(places_a, values):
                start = (group // plan.rows_a) * n_dp * plan.rows_a + group % plan.rows_a
                rows_a[pl.ds(start, n_dp, stride=plan.rows_a), :] = value
            attn[:, span] = rows_a[...].astype(bf16)
        for r, start in places_e:
            rows_e[pl.ds(b * count_e + r, n_dp, stride=plan.rows_e), :] = rows[pl.ds(start, n_dp, stride=chunk), :]

    each(plan.blocks, order, n_dp <= 8)
    for b in range(plan.blocks):
        exp[0, :, pl.ds(b * LANES, LANES)] = rows_e[pl.ds(b * count_e, count_e), :].astype(bf16)
    for copy in copies:
        copy.wait()


def update(plan, limit, gathered, state):
    count_a = plan.n_expert * plan.n_dp * plan.rows_a
    count_e = plan.n_dp * plan.rows_e
    vmem, hbm = pl.BlockSpec(memory_space=pltpu.VMEM), pl.BlockSpec(memory_space=pltpu.HBM)
    own = [((plan.size_a, LANES), f32)] * 3 + [((plan.size_e, LANES), f32)] * 3
    return call(
        lambda *refs: update_kernel(plan, limit, *refs),
        gathered + state,
        own + [((count_a, plan.width), bf16), ((1, count_e, plan.width), bf16)],
        [pltpu.VMEM(shape, dtype) for shape, dtype in own]
        + [
            pltpu.VMEM((plan.n_dp * plan.chunk, LANES), f32),
            pltpu.VMEM((count_a, LANES), f32),
            pltpu.VMEM((plan.blocks * count_e, LANES), f32),
            pltpu.SemaphoreType.DMA((6,)),
        ],
        out_specs=[hbm] * 6 + [vmem] * 2,
    )


def swap(value, axis, distance, cores=(0, 1)):
    size = lax.axis_size(axis)
    if axis == "dp":
        return lax.ppermute(value, axis, [(i, i ^ distance) for i in range(size) if i % 2 in cores])
    n_dp = lax.axis_size("dp")
    pairs = [(i * n_dp + j, (i ^ distance) * n_dp + j) for i in range(size) for j in range(n_dp) if j % 2 in cores]
    return lax.ppermute(value, ("expert", "dp"), pairs)


def to_blocks(value):
    rows, width = value.shape
    return value.reshape(rows, width // LANES, LANES).transpose(1, 0, 2).reshape(-1, LANES)


def from_blocks(value, rows):
    return value.reshape(-1, rows, LANES).transpose(1, 0, 2).reshape(rows, -1)


EVEN, ODD = (0,), (1,)


def body(act_attn, dy_attn, act_exp, dy_exp, w_attn, m_attn, v_attn, w_exp, m_exp, v_exp):
    width = w_attn.shape[1]
    n_expert = lax.axis_size("expert")
    n_dp = lax.axis_size("dp")
    rows_a, rows_e = w_attn.shape[0], w_exp.shape[1]
    plan = Plan(n_expert, n_dp, rows_a, rows_e, width)
    total_params = width * (act_attn.shape[1] + n_expert * act_exp.shape[2])
    limit = 0.5 * math.sqrt(total_params)
    chips, pair, size_a = plan.chips, plan.pair, plan.size_a
    state = [to_blocks(value) for value in (w_attn, m_attn, v_attn)]
    state += [to_blocks(value[0]) for value in (w_exp, m_exp, v_exp)]

    full, send = make_terms(plan, [act_attn.T, dy_attn, act_exp[0].T, dy_exp[0], *state])
    got = swap(send, "dp", 1)

    sums = [
        full[c * pair : (c + 1) * pair] + got[plan.pack + c * pair : plan.pack + (c + 1) * pair].astype(f32)
        for c in range(chips)
    ]
    parts = [swap(sums[c].astype(bf16), "dp", 2 * c, ODD) for c in range(1, chips)]
    shared = ((2 * plan.all_a + 16, LANES), bf16)
    payload, g_exp = call(
        lambda *refs: share_kernel(plan, *refs), [sums[0]] + parts, [shared, ((2 * plan.size_e, LANES), bf16)]
    )
    distance = 1
    while 2 * distance < n_expert:
        other = swap(payload, "expert", distance, ODD)
        (payload,) = call(lambda *refs: again_kernel(plan, *refs), [payload, other], [shared])
        distance *= 2
    other = swap(payload, "expert", distance, ODD)
    (grads,) = call(
        lambda *refs: last_kernel(plan, *refs), [payload, other, g_exp], [((pair + 16, LANES), bf16)]
    )
    near_g = [grads] + [swap(grads, "dp", 2 * c, ODD) for c in range(1, chips)]
    far_g = [swap(value, "dp", 1, ODD) for value in near_g]

    mine, other = send[: plan.pack], got[: plan.pack]
    packs = jnp.concatenate([mine[: 3 * size_a], other[: 3 * size_a]])
    packs = [swap(packs, "expert", q, EVEN) for q in range(1, n_expert)]
    (states,) = call(
        lambda *refs: state_kernel(plan, *refs), [mine, other, *packs], [((3 * pair, LANES), bf16)]
    )
    near_s = [states] + [swap(states, "dp", 2 * c, EVEN) for c in range(1, chips)]
    far_s = [swap(value, "dp", 1, EVEN) for value in near_s]

    *new, attn_full, expert_full = update(plan, limit, near_g + far_g + near_s + far_s, state)
    new_a = [from_blocks(value, rows_a) for value in new[:3]]
    new_e = [from_blocks(value, rows_e)[None] for value in new[3:]]
    return (*new_a, *new_e, attn_full, expert_full)


def solution(mesh):
    return jax.shard_map(
        body,
        mesh=mesh,
        in_specs=(
            P(("expert", "dp"), None),
            P(("expert", "dp"), None),
            P("expert", "dp", None),
            P("expert", "dp", None),
            P(("expert", "dp"), None),
            P(("expert", "dp"), None),
            P(("expert", "dp"), None),
            P("expert", "dp", None),
            P("expert", "dp", None),
            P("expert", "dp", None),
        ),
        out_specs=(
            P(("expert", "dp"), None),
            P(("expert", "dp"), None),
            P(("expert", "dp"), None),
            P("expert", "dp", None),
            P("expert", "dp", None),
            P("expert", "dp", None),
            P(),
            P("expert", None, None),
        ),
        check_vma=False,
    )
```

```python
import math

import jax
import jax.numpy as jnp
from jax import lax
from jax.experimental import pallas as pl
from jax.experimental.pallas import tpu as pltpu
from jax.sharding import PartitionSpec as P

beta_first = 0.9
beta_second = 0.95
bias_first = 1.0 - 0.9**10
bias_second = 1.0 - 0.95**10
learn_rate = 0.01
decay_rate = 0.1
adam_eps = 1e-08

LANES = 128
STEPS = 4
f32, bf16 = jnp.float32, jnp.bfloat16


def adamw(grad, weight, moment, second, factor):
    scaled = factor * grad
    moment_new = beta_first * moment + (1.0 - beta_first) * scaled
    second_new = beta_second * second + (1.0 - beta_second) * scaled * scaled
    update = moment_new / bias_first / (jnp.sqrt(second_new / bias_second) + adam_eps)
    weight_new = weight - learn_rate * (update + decay_rate * weight)
    return (weight_new, moment_new, second_new)


class Plan:
    def __init__(self, n_expert, n_dp, rows_a, rows_e, width):
        self.n_expert, self.n_dp, self.rows_a, self.rows_e = n_expert, n_dp, rows_a, rows_e
        self.width = width
        self.chips = n_dp // 2
        self.blocks = width // LANES
        self.size_a = self.blocks * rows_a
        self.size_e = self.blocks * rows_e
        self.all_a = n_expert * self.size_a
        self.chunk = self.all_a + self.size_e
        self.pair = 2 * self.chunk
        self.pack = 3 * (self.size_a + self.size_e)

    def places(self, block):
        attn = [
            (e * self.rows_a + r, e * self.size_a + block * self.rows_a + r)
            for e in range(self.n_expert)
            for r in range(self.rows_a)
        ]
        exp = [(r, self.all_a + block * self.rows_e + r) for r in range(self.rows_e)]
        return attn, exp


def dot(left, right):
    return lax.dot_general(left, right, (((1,), (0,)), ((), ())), preferred_element_type=f32)


def size_of(shape, dtype):
    return math.prod(shape) * jnp.dtype(dtype).itemsize


def call(kernel, args, outs, scratch=(), in_specs=None, out_specs=None):
    whole = pl.BlockSpec(memory_space=pltpu.VMEM)
    held = sum(size_of(arg.shape, arg.dtype) for arg in args if not in_specs)
    held += sum(size_of(*out) for out in outs) + sum(size_of(*buffer) for buffer in scratch)
    semaphores = [] if not scratch else [pltpu.SemaphoreType.DMA((64,))]
    return pl.pallas_call(
        kernel,
        in_specs=in_specs or [whole] * len(args),
        out_specs=out_specs or [whole] * len(outs),
        out_shape=[jax.ShapeDtypeStruct(shape, dtype) for shape, dtype in outs],
        scratch_shapes=[pltpu.VMEM(*buffer) for buffer in scratch] + semaphores,
        compiler_params=pltpu.CompilerParams(vmem_limit_bytes=held + 4 * 1024 * 1024),
    )(*args)


def two_pieces(value):
    high = value.astype(bf16).astype(f32)
    return jnp.concatenate([high, value - high], axis=0).astype(bf16)


def one_value(pieces):
    pieces = pieces.astype(f32)
    half = pieces.shape[0] // 2
    return pieces[:half] + pieces[half:]


def by_eights(value):
    return jnp.sum(value.reshape(-1, 8, LANES), axis=0)


def each(count, step, unrolled):
    if unrolled:
        for i in range(count):
            step(i)
    else:
        pl.loop(0, count)(step)


def aligned(index, unit):
    return index * unit if isinstance(index, int) else pl.multiple_of(index * unit, unit)


def terms_kernel(plan, act_a, dy_a, act_e, dy_e, wa, ma, va, we, me, ve, full, send, *scratch):
    act_a_v, dy_a_v, act_e_v, dy_e_v, state_a, state_e, sems = scratch
    tile = plan.width // STEPS
    small = [
        pltpu.make_async_copy(act_a, act_a_v, sems.at[0]),
        pltpu.make_async_copy(act_e, act_e_v, sems.at[1]),
    ]
    big = []
    for t in range(STEPS):
        cols = pl.ds(t * tile, tile)
        big.append(pltpu.make_async_copy(dy_a.at[:, cols], dy_a_v.at[:, cols], sems.at[2 + 2 * t]))
        big.append(pltpu.make_async_copy(dy_e.at[:, cols], dy_e_v.at[:, cols], sems.at[3 + 2 * t]))
    base = 2 + 2 * STEPS
    extra = [pltpu.make_async_copy(ref, state_a.at[i], sems.at[base + i]) for i, ref in enumerate((wa, ma, va))]
    extra += [pltpu.make_async_copy(ref, state_e.at[i], sems.at[base + 3 + i]) for i, ref in enumerate((we, me, ve))]
    for copy in small + big + extra:
        copy.start()

    chip = lax.axis_index("dp") // 2
    n_dp = plan.n_dp

    def pick(groups, per_owner, count):
        shape = (groups * n_dp, count)
        row = lax.broadcasted_iota(jnp.int32, shape, 0)
        col = lax.broadcasted_iota(jnp.int32, shape, 1)
        group, place = row // n_dp, row % n_dp
        owner = 2 * ((place // 2) ^ chip) + place % 2
        want = ((group // per_owner) * n_dp + owner) * per_owner + group % per_owner
        return (want == col).astype(bf16)

    pick_a = pick(plan.n_expert * plan.rows_a, plan.rows_a, act_a.shape[0])
    pick_e = pick(plan.rows_e, plan.rows_e, act_e.shape[0])
    for copy in small:
        copy.wait()
    left_a = dot(pick_a, act_a_v[...]).astype(bf16)
    left_e = dot(pick_e, act_e_v[...]).astype(bf16)
    for t in range(STEPS):
        cols = pl.ds(t * tile, tile)
        big[2 * t].wait()
        terms_a = dot(left_a, dy_a_v[:, cols])
        big[2 * t + 1].wait()
        terms_e = dot(left_e, dy_e_v[:, cols])
        for b in range(tile // LANES):
            attn, exp = plan.places(t * (tile // LANES) + b)
            span = slice(b * LANES, (b + 1) * LANES)
            for terms, places in ((terms_a, attn), (terms_e, exp)):
                for group, start in places:
                    full[pl.ds(start, n_dp, stride=plan.chunk), :] = terms[group * n_dp : (group + 1) * n_dp, span]
    for copy in extra:
        copy.wait()
    for i in range(3):
        send[pl.ds(i * plan.size_a, plan.size_a), :] = state_a[i].astype(bf16)
        send[pl.ds(3 * plan.size_a + i * plan.size_e, plan.size_e), :] = state_e[i].astype(bf16)

    def cast(p):
        send[pl.ds(plan.pack + aligned(p, plan.chunk), plan.chunk), :] = full[
            pl.ds(aligned(p, plan.chunk), plan.chunk), :
        ].astype(bf16)

    each(n_dp, cast, n_dp <= 8)


def make_terms(plan, args):
    act_a, dy_a, act_e, dy_e = args[:4]
    rows = n_rows = plan.n_dp * plan.chunk
    return call(
        lambda *refs: terms_kernel(plan, *refs),
        [pltpu.with_memory_space_constraint(arg, pltpu.HBM) for arg in args],
        [((rows, LANES), f32), ((plan.pack + n_rows, LANES), bf16)],
        [
            (act_a.shape, bf16),
            (dy_a.shape, bf16),
            (act_e.shape, bf16),
            (dy_e.shape, bf16),
            ((3, plan.size_a, LANES), f32),
            ((3, plan.size_e, LANES), f32),
        ],
        in_specs=[pl.BlockSpec(memory_space=pltpu.HBM)] * len(args),
    )


def share_kernel(plan, *refs):
    own, got, (payload, g_exp) = refs[0], refs[1:-2], refs[-2:]
    square = jnp.zeros((8, LANES), f32)
    for k in range(2):
        a, e = plan.all_a, plan.size_e

        def total(start, size):
            value = own[pl.ds(start, size), :]
            for ref in got:
                value = value + ref[pl.ds(start, size), :].astype(f32)
            return value

        payload[pl.ds(k * a, a), :] = total(k * plan.chunk, a).astype(bf16)
        exp = total(k * plan.chunk + a, e)
        g_exp[pl.ds(k * e, e), :] = exp.astype(bf16)
        square = square + by_eights(exp * exp)
    payload[pl.ds(2 * plan.all_a, 16), :] = two_pieces(square)


def pair_sum(plan, mine, other):
    a = 2 * plan.all_a
    attn = mine[:a, :].astype(f32) + other[:a, :].astype(f32)
    return attn, one_value(mine[a:, :]) + one_value(other[a:, :])


def again_kernel(plan, mine, other, payload):
    attn, square = pair_sum(plan, mine, other)
    a = 2 * plan.all_a
    payload[:a, :] = attn.astype(bf16)
    payload[a:, :] = two_pieces(square)


def last_kernel(plan, mine, other, g_exp, rows):
    attn, square = pair_sum(plan, mine, other)
    square = square + by_eights(attn * attn)
    a, e = plan.all_a, plan.size_e
    for k in range(2):
        rows[pl.ds(k * plan.chunk, a), :] = attn[k * a : (k + 1) * a].astype(bf16)
        rows[pl.ds(k * plan.chunk + a, e), :] = g_exp[pl.ds(k * e, e), :]
    rows[pl.ds(plan.pair, 16), :] = two_pieces(square)


def packs_kernel(plan, mine, other, both):
    size = 3 * plan.size_a
    both[:size, :] = mine[:size, :]
    both[size:, :] = other[:size, :]


def state_kernel(plan, mine, other, both, *refs):
    packs, states = (both,) + refs[:-1], refs[-1]
    place = lax.axis_index("expert")
    a, e = plan.size_a, plan.size_e
    for k, own in enumerate((mine, other)):
        for i in range(3):
            start = (k * 3 + i) * plan.chunk
            for q, pack in enumerate(packs):
                rows = pl.ds(pl.multiple_of(start + (place ^ q) * a, 16), a)
                states[rows, :] = pack[pl.ds((k * 3 + i) * a, a), :]
            states[pl.ds(start + plan.all_a, e), :] = own[pl.ds(3 * a + i * e, e), :]


def tree_sum(values):
    while len(values) > 1:
        values = [values[i] + values[i + 1] for i in range(0, len(values), 2)]
    return values[0]


def update_kernel(plan, limit, *refs):
    chips, chunk = plan.chips, plan.chunk
    near_g, far_g, near_s, far_s = [refs[i * chips : (i + 1) * chips] for i in range(4)]
    refs = refs[4 * chips :]
    state, new, (attn, exp) = refs[:6], refs[6:12], refs[12:14]
    held, (rows, rows_a, rows_e, sems) = refs[14:20], refs[20:]
    me, place = lax.axis_index("dp"), lax.axis_index("expert")
    lead = (me % 2) == 1

    def grad(c, start, size):
        return jnp.where(lead, near_g[c][pl.ds(start, size), :], far_g[c][pl.ds(start, size), :])

    def old(c, start, size):
        return jnp.where(lead, far_s[c][pl.ds(start, size), :], near_s[c][pl.ds(start, size), :]).astype(f32)

    square = tree_sum([one_value(grad(c, plan.pair, 16)) for c in range(chips)])
    norm = jnp.sqrt(jnp.sum(square, keepdims=True))
    factor = jnp.minimum(1.0, limit / (norm + 1e-06))

    start = pl.multiple_of((me % 2) * chunk + place * plan.size_a, 16)
    own_a = grad(0, start, plan.size_a).astype(f32)
    start = pl.multiple_of((me % 2) * chunk + plan.all_a, 16)
    own_e = grad(0, start, plan.size_e).astype(f32)
    copies = []
    for b, own in enumerate((own_a, own_e)):
        values = adamw(own, *[ref[...] for ref in state[3 * b : 3 * b + 3]], factor)
        for i, value in enumerate(values):
            held[3 * b + i][...] = value
            copies.append(pltpu.make_async_copy(held[3 * b + i], new[3 * b + i], sems.at[3 * b + i]))
    for copy in copies:
        copy.start()

    piece = plan.size_a
    for c in range(chips):
        for k in range(2):
            owner = 2 * (c ^ (me // 2)) + k

            def one(p):
                weight, moment, second = [old(c, (k * 3 + i) * chunk + aligned(p, piece), piece) for i in range(3)]
                value = grad(c, k * chunk + aligned(p, piece), piece).astype(f32)
                weight, _, _ = adamw(value, weight, moment, second, factor)
                rows[pl.ds(pl.multiple_of(owner * chunk + aligned(p, piece), 16), piece), :] = weight

            each(chunk // piece, one, chips <= 4)

    count_e, n_dp = exp.shape[1], plan.n_dp

    def order(b):
        places_a, places_e = plan.places(b)
        span = pl.ds(aligned(b, LANES), LANES)
        values = [rows[pl.ds(start, n_dp, stride=chunk), :] for _, start in places_a]
        if plan.rows_a == 1:
            attn[:, span] = jnp.concatenate(values, axis=0).astype(bf16)
        else:
            for (group, _), value in zip(places_a, values):
                start = (group // plan.rows_a) * n_dp * plan.rows_a + group % plan.rows_a
                rows_a[pl.ds(start, n_dp, stride=plan.rows_a), :] = value
            attn[:, span] = rows_a[...].astype(bf16)
        for r, start in places_e:
            rows_e[pl.ds(b * count_e + r, n_dp, stride=plan.rows_e), :] = rows[pl.ds(start, n_dp, stride=chunk), :]

    each(plan.blocks, order, n_dp <= 8)
    for b in range(plan.blocks):
        exp[0, :, pl.ds(b * LANES, LANES)] = rows_e[pl.ds(b * count_e, count_e), :].astype(bf16)
    for copy in copies:
        copy.wait()


def update(plan, limit, gathered, state):
    count_a = plan.n_expert * plan.n_dp * plan.rows_a
    count_e = plan.n_dp * plan.rows_e
    vmem, hbm = pl.BlockSpec(memory_space=pltpu.VMEM), pl.BlockSpec(memory_space=pltpu.HBM)
    own = [((plan.size_a, LANES), f32)] * 3 + [((plan.size_e, LANES), f32)] * 3
    return call(
        lambda *refs: update_kernel(plan, limit, *refs),
        gathered + state,
        own + [((count_a, plan.width), bf16), ((1, count_e, plan.width), bf16)],
        own
        + [
            ((plan.n_dp * plan.chunk, LANES), f32),
            ((count_a, LANES), f32),
            ((plan.blocks * count_e, LANES), f32),
        ],
        out_specs=[hbm] * 6 + [vmem] * 2,
    )


def swap(value, axis, distance, cores=(0, 1)):
    size, n_dp = lax.axis_size(axis), lax.axis_size("dp")
    if axis == "dp":
        return lax.ppermute(value, axis, [(i, i ^ distance if i % 2 in cores else i) for i in range(size)])
    pairs = [
        (i * n_dp + j, (i ^ distance if j % 2 in cores else i) * n_dp + j) for i in range(size) for j in range(n_dp)
    ]
    return lax.ppermute(value, ("expert", "dp"), pairs)


def to_blocks(value):
    rows, width = value.shape
    return value.reshape(rows, width // LANES, LANES).transpose(1, 0, 2).reshape(-1, LANES)


def from_blocks(value, rows):
    return value.reshape(-1, rows, LANES).transpose(1, 0, 2).reshape(rows, -1)


EVEN, ODD = (0,), (1,)


def body(act_attn, dy_attn, act_exp, dy_exp, w_attn, m_attn, v_attn, w_exp, m_exp, v_exp):
    width = w_attn.shape[1]
    n_expert = lax.axis_size("expert")
    n_dp = lax.axis_size("dp")
    rows_a, rows_e = w_attn.shape[0], w_exp.shape[1]
    plan = Plan(n_expert, n_dp, rows_a, rows_e, width)
    total_params = width * (act_attn.shape[1] + n_expert * act_exp.shape[2])
    limit = 0.5 * math.sqrt(total_params)
    chips, pair, size_a = plan.chips, plan.pair, plan.size_a
    state = [to_blocks(value) for value in (w_attn, m_attn, v_attn)]
    state += [to_blocks(value[0]) for value in (w_exp, m_exp, v_exp)]

    full, send = make_terms(plan, [act_attn.T, dy_attn, act_exp[0].T, dy_exp[0], *state])
    got = swap(send, "dp", 1)

    sums = [
        full[c * pair : (c + 1) * pair] + got[plan.pack + c * pair : plan.pack + (c + 1) * pair].astype(f32)
        for c in range(chips)
    ]
    parts = [swap(sums[c].astype(bf16), "dp", 2 * c, ODD) for c in range(1, chips)]
    shared = ((2 * plan.all_a + 16, LANES), bf16)
    payload, g_exp = call(
        lambda *refs: share_kernel(plan, *refs), [sums[0]] + parts, [shared, ((2 * plan.size_e, LANES), bf16)]
    )
    distance = 1
    while 2 * distance < n_expert:
        other = swap(payload, "expert", distance, ODD)
        (payload,) = call(lambda *refs: again_kernel(plan, *refs), [payload, other], [shared])
        distance *= 2
    other = swap(payload, "expert", distance, ODD)
    (grads,) = call(
        lambda *refs: last_kernel(plan, *refs), [payload, other, g_exp], [((pair + 16, LANES), bf16)]
    )
    near_g = [grads] + [swap(grads, "dp", 2 * c, ODD) for c in range(1, chips)]
    far_g = [swap(value, "dp", 1) for value in near_g]

    (both,) = call(lambda *refs: packs_kernel(plan, *refs), [send, got], [((6 * size_a, LANES), bf16)])
    packs = [swap(both, "expert", q, EVEN) for q in range(1, n_expert)]
    (states,) = call(
        lambda *refs: state_kernel(plan, *refs), [send, got, both, *packs], [((3 * pair, LANES), bf16)]
    )
    near_s = [states] + [swap(states, "dp", 2 * c, EVEN) for c in range(1, chips)]
    far_s = [swap(value, "dp", 1) for value in near_s]

    *new, attn_full, expert_full = update(plan, limit, near_g + far_g + near_s + far_s, state)
    new_a = [from_blocks(value, rows_a) for value in new[:3]]
    new_e = [from_blocks(value, rows_e)[None] for value in new[3:]]
    return (*new_a, *new_e, attn_full, expert_full)


def solution(mesh):
    return jax.shard_map(
        body,
        mesh=mesh,
        in_specs=(
            P(("expert", "dp"), None),
            P(("expert", "dp"), None),
            P("expert", "dp", None),
            P("expert", "dp", None),
            P(("expert", "dp"), None),
            P(("expert", "dp"), None),
            P(("expert", "dp"), None),
            P("expert", "dp", None),
            P("expert", "dp", None),
            P("expert", "dp", None),
        ),
        out_specs=(
            P(("expert", "dp"), None),
            P(("expert", "dp"), None),
            P(("expert", "dp"), None),
            P("expert", "dp", None),
            P("expert", "dp", None),
            P("expert", "dp", None),
            P(),
            P("expert", None, None),
        ),
        check_vma=False,
    )
```

```python
import math

import jax
import jax.numpy as jnp
from jax import lax
from jax.experimental import pallas as pl
from jax.experimental.pallas import tpu as pltpu
from jax.sharding import PartitionSpec as P

beta_first = 0.9
beta_second = 0.95
bias_first = 1.0 - 0.9**10
bias_second = 1.0 - 0.95**10
learn_rate = 0.01
decay_rate = 0.1
adam_eps = 1e-08

LANES = 128
f32, bf16 = jnp.float32, jnp.bfloat16


def adamw(grad, weight, moment, second, factor):
    scaled = factor * grad
    moment_new = beta_first * moment + (1.0 - beta_first) * scaled
    second_new = beta_second * second + (1.0 - beta_second) * scaled * scaled
    update = moment_new / bias_first / (jnp.sqrt(second_new / bias_second) + adam_eps)
    weight_new = weight - learn_rate * (update + decay_rate * weight)
    return (weight_new, moment_new, second_new)


class Plan:
    def __init__(self, n_expert, n_dp, rows_a, rows_e, width):
        self.n_expert, self.n_dp, self.rows_a, self.rows_e = n_expert, n_dp, rows_a, rows_e
        self.width = width
        self.chips = n_dp // 2
        self.blocks = width // LANES
        self.size_a = self.blocks * rows_a
        self.size_e = self.blocks * rows_e
        self.all_a = n_expert * self.size_a
        self.chunk = self.all_a + self.size_e

    def places(self, block):
        attn = [
            (e * self.rows_a + r, e * self.size_a + block * self.rows_a + r)
            for e in range(self.n_expert)
            for r in range(self.rows_a)
        ]
        exp = [(r, self.all_a + block * self.rows_e + r) for r in range(self.rows_e)]
        return attn, exp


def dot(left, right):
    return lax.dot_general(left, right, (((1,), (0,)), ((), ())), preferred_element_type=f32)


def size_of(shape, dtype):
    return math.prod(shape) * jnp.dtype(dtype).itemsize


def call(kernel, args, outs, scratch=(), in_specs=None):
    whole = pl.BlockSpec(memory_space=pltpu.VMEM)
    held = sum(size_of(arg.shape, arg.dtype) for arg in args if not in_specs)
    held += sum(size_of(*out) for out in outs) + sum(size_of(*buffer) for buffer in scratch)
    semaphores = [pltpu.SemaphoreType.DMA((16,))] if in_specs else []
    return pl.pallas_call(
        kernel,
        in_specs=in_specs or [whole] * len(args),
        out_specs=[whole] * len(outs),
        out_shape=[jax.ShapeDtypeStruct(shape, dtype) for shape, dtype in outs],
        scratch_shapes=[pltpu.VMEM(*buffer) for buffer in scratch] + semaphores,
        compiler_params=pltpu.CompilerParams(vmem_limit_bytes=held + 4 * 1024 * 1024),
    )(*args)


def two_pieces(value):
    high = value.astype(bf16).astype(f32)
    return high, (value - high).astype(bf16).astype(f32)


def by_eights(value):
    return jnp.sum(value.reshape(-1, 8, LANES), axis=0)


STEPS = 4


def each(count, step, unrolled):
    if unrolled:
        for i in range(count):
            step(i)
    else:
        pl.loop(0, count)(step)


def terms_kernel(plan, act_a, dy_a, act_e, dy_e, w, m, v, full, send, pack, act_a_v, dy_a_v, act_e_v, dy_e_v, state, sems):
    tile = plan.width // STEPS
    small = [
        pltpu.make_async_copy(act_a, act_a_v, sems.at[0]),
        pltpu.make_async_copy(act_e, act_e_v, sems.at[1]),
    ]
    big = []
    for t in range(STEPS):
        cols = pl.ds(t * tile, tile)
        big.append(pltpu.make_async_copy(dy_a.at[:, cols], dy_a_v.at[:, cols], sems.at[2 + 2 * t]))
        big.append(pltpu.make_async_copy(dy_e.at[:, cols], dy_e_v.at[:, cols], sems.at[3 + 2 * t]))
    extra = [pltpu.make_async_copy(ref, state.at[i], sems.at[2 + 2 * STEPS + i]) for i, ref in enumerate((w, m, v))]
    for copy in small + big[:4]:
        copy.start()

    me = lax.axis_index("dp")

    def pick(groups, per_owner, count):
        shape = (groups * plan.n_dp, count)
        row = lax.broadcasted_iota(jnp.int32, shape, 0)
        col = lax.broadcasted_iota(jnp.int32, shape, 1)
        group, place = row // plan.n_dp, row % plan.n_dp
        owner = (2 * (place % plan.chips) + place // plan.chips) ^ me
        want = ((group // per_owner) * plan.n_dp + owner) * per_owner + group % per_owner
        return (want == col).astype(bf16)

    for copy in small:
        copy.wait()
    left_a = dot(pick(plan.n_expert * plan.rows_a, plan.rows_a, act_a.shape[0]), act_a_v[...]).astype(bf16)
    left_e = dot(pick(plan.rows_e, plan.rows_e, act_e.shape[0]), act_e_v[...]).astype(bf16)
    n_dp = plan.n_dp
    for t in range(STEPS):
        cols = pl.ds(t * tile, tile)
        big[2 * t].wait()
        terms_a = dot(left_a, dy_a_v[:, cols])
        big[2 * t + 1].wait()
        for copy in big[2 * t + 4 : 2 * t + 6] if t + 2 < STEPS else extra if t + 2 == STEPS else []:
            copy.start()
        terms_e = dot(left_e, dy_e_v[:, cols])
        for b in range(tile // LANES):
            attn, exp = plan.places(t * (tile // LANES) + b)
            span = slice(b * LANES, (b + 1) * LANES)
            for terms, places in ((terms_a, attn), (terms_e, exp)):
                for group, start in places:
                    full[pl.ds(start, n_dp, stride=plan.chunk), :] = terms[group * n_dp : (group + 1) * n_dp, span]
    for c in range(plan.chips):
        send[pl.ds(c * plan.chunk, plan.chunk), :] = full[
            pl.ds((plan.chips + c) * plan.chunk, plan.chunk), :
        ].astype(bf16)
    for copy in extra:
        copy.wait()
    size = plan.size_a
    high, low = two_pieces(state[0])
    for i, value in enumerate((high, low, state[1], state[2])):
        pack[pl.ds(i * size, size), :] = value.astype(bf16)


def make_terms(plan, act_a, dy_a, act_e, dy_e, w, m, v):
    args = (act_a, dy_a, act_e, dy_e, w, m, v)
    half = plan.chips * plan.chunk
    return call(
        lambda *refs: terms_kernel(plan, *refs),
        args,
        [((2 * half, LANES), f32), ((half, LANES), bf16), ((4 * plan.size_a, LANES), bf16)],
        [
            (act_a.shape, bf16),
            (dy_a.shape, bf16),
            (act_e.shape, bf16),
            (dy_e.shape, bf16),
            ((3,) + w.shape, f32),
        ],
        [pl.BlockSpec(memory_space=pltpu.HBM)] * len(args),
    )


def share_kernel(plan, *refs):
    own, got, (payload, g_exp) = refs[0], refs[1:-2], refs[-2:]
    total = own[...]
    for ref in got:
        total = total + ref[...].astype(f32)
    a = plan.all_a
    exp = total[a:]
    g_exp[...] = exp
    payload[:a, :] = total[:a].astype(bf16)
    payload[a:, :] = jnp.concatenate(two_pieces(by_eights(exp * exp)), axis=0).astype(bf16)


def pair_sum(plan, mine, other):
    a = plan.all_a
    attn = mine[:a, :].astype(f32) + other[:a, :].astype(f32)
    one, two = mine[a:, :].astype(f32), other[a:, :].astype(f32)
    return attn, (one[:8] + one[8:]) + (two[:8] + two[8:])


def again_kernel(plan, distance, mine, other, held, far, payload, both):
    attn, square = pair_sum(plan, mine, other)
    a = plan.all_a
    payload[:a, :] = attn.astype(bf16)
    payload[a:, :] = jnp.concatenate(two_pieces(square), axis=0).astype(bf16)
    bit = (lax.axis_index("expert") // distance) % 2
    size = held.shape[0]
    both[pl.ds(pl.multiple_of(bit * size, 16), size), :] = held[...]
    both[pl.ds(pl.multiple_of((1 - bit) * size, 16), size), :] = far[...]


def last_kernel(plan, mine, other, g_attn, square):
    attn, partial = pair_sum(plan, mine, other)
    g_attn[...] = attn
    square[...] = jnp.broadcast_to((partial + by_eights(attn * attn))[None], square.shape)


def clip_factor(limit, square):
    norm = jnp.sqrt(jnp.sum(jnp.sum(square[...], axis=0), keepdims=True))
    return jnp.minimum(1.0, limit / (norm + 1e-06))


def rows_kernel(plan, limit, square, g_attn, g_exp, we, me, ve, held, far, mine):
    factor = clip_factor(limit, square)
    size, half = plan.size_a, plan.n_expert // 2
    bit = (lax.axis_index("expert") // half) % 2
    for side, states in enumerate((held, far)):
        for i in range(half):
            rows = pl.ds(pl.multiple_of((((bit + side) % 2) * half + i) * size, 16), size)
            high, low, moment, second = [
                states[pl.ds((i * 4 + j) * size, size), :].astype(f32) for j in range(4)
            ]
            weight, _, _ = adamw(g_attn[rows, :], high + low, moment, second, factor)
            mine[rows, :] = weight.astype(bf16)
    weight, _, _ = adamw(g_exp[...], we[...], me[...], ve[...], factor)
    mine[plan.all_a :, :] = weight.astype(bf16)


def own_kernel(plan, limit, *refs):
    square, g_attn, g_exp = refs[:3]
    state, new = refs[3:9], refs[9:]
    factor = clip_factor(limit, square)
    rows = pl.ds(pl.multiple_of(lax.axis_index("expert") * plan.size_a, 16), plan.size_a)
    for b, grad in enumerate((g_attn[rows, :], g_exp[...])):
        values = adamw(grad, *[ref[...] for ref in state[3 * b : 3 * b + 3]], factor)
        for ref, value in zip(new[3 * b : 3 * b + 3], values):
            ref[...] = value


def order_kernel(plan, *refs):
    n_dp = plan.n_dp
    parts, (attn, exp, rows, rows_a, rows_e) = refs[:n_dp], refs[n_dp:]
    me = lax.axis_index("dp")
    for i, part in enumerate(parts):
        owner = (2 * (i % plan.chips) + i // plan.chips) ^ me
        rows[pl.ds(pl.multiple_of(owner * plan.chunk, 16), plan.chunk), :] = part[...].astype(f32)
    count_a, count_e = attn.shape[0], exp.shape[1]

    def one(b):
        places_a, places_e = plan.places(b)
        span = pl.ds(b * LANES if isinstance(b, int) else pl.multiple_of(b * LANES, LANES), LANES)
        values = [rows[pl.ds(start, n_dp, stride=plan.chunk), :] for _, start in places_a]
        if plan.rows_a == 1:
            attn[:, span] = jnp.concatenate(values, axis=0).astype(bf16)
        else:
            for (group, _), value in zip(places_a, values):
                start = (group // plan.rows_a) * n_dp * plan.rows_a + group % plan.rows_a
                rows_a[pl.ds(start, n_dp, stride=plan.rows_a), :] = value
            attn[:, span] = rows_a[...].astype(bf16)
        for r, start in places_e:
            rows_e[pl.ds(b * count_e + r, n_dp, stride=plan.rows_e), :] = rows[
                pl.ds(start, n_dp, stride=plan.chunk), :
            ]

    each(plan.blocks, one, n_dp <= 8)
    for b in range(plan.blocks):
        exp[0, :, pl.ds(b * LANES, LANES)] = rows_e[pl.ds(b * count_e, count_e), :].astype(bf16)


def put_in_order(plan, parts):
    count_a = plan.n_expert * plan.n_dp * plan.rows_a
    count_e = plan.n_dp * plan.rows_e
    return call(
        lambda *refs: order_kernel(plan, *refs),
        parts,
        [((count_a, plan.width), bf16), ((1, count_e, plan.width), bf16)],
        [
            ((plan.n_dp * plan.chunk, LANES), f32),
            ((count_a, LANES), f32),
            ((plan.blocks * count_e, LANES), f32),
        ],
    )


def swap(value, axis, distance):
    size = lax.axis_size(axis)
    return lax.ppermute(value, axis, [(i, i ^ distance) for i in range(size)])


def to_blocks(value):
    rows, width = value.shape
    return value.reshape(rows, width // LANES, LANES).transpose(1, 0, 2).reshape(-1, LANES)


def from_blocks(value, rows):
    return value.reshape(-1, rows, LANES).transpose(1, 0, 2).reshape(rows, -1)


def body(act_attn, dy_attn, act_exp, dy_exp, w_attn, m_attn, v_attn, w_exp, m_exp, v_exp):
    width = w_attn.shape[1]
    n_expert = lax.axis_size("expert")
    n_dp = lax.axis_size("dp")
    rows_a, rows_e = w_attn.shape[0], w_exp.shape[1]
    plan = Plan(n_expert, n_dp, rows_a, rows_e, width)
    total_params = width * (act_attn.shape[1] + n_expert * act_exp.shape[2])
    limit = 0.5 * math.sqrt(total_params)
    chips, chunk = plan.chips, plan.chunk
    state_a = [to_blocks(value) for value in (w_attn, m_attn, v_attn)]
    state_e = [to_blocks(value[0]) for value in (w_exp, m_exp, v_exp)]

    held = [pltpu.with_memory_space_constraint(x, pltpu.HBM) for x in (act_attn.T, dy_attn, act_exp[0].T, dy_exp[0])]
    full, send, pack = make_terms(plan, *held, *[pltpu.with_memory_space_constraint(x, pltpu.HBM) for x in state_a])
    got = swap(send, "dp", 1)
    sums = [
        full[c * chunk : (c + 1) * chunk] + got[c * chunk : (c + 1) * chunk].astype(f32) for c in range(chips)
    ]
    got = [swap(sums[c].astype(bf16), "dp", 2 * c) for c in range(1, chips)]
    shared = ((plan.all_a + 16, LANES), bf16)
    payload, g_exp = call(
        lambda *refs: share_kernel(plan, *refs), [sums[0]] + got, [shared, ((plan.size_e, LANES), f32)]
    )
    distance = 1
    while 2 * distance < n_expert:
        other, far = swap(payload, "expert", distance), swap(pack, "expert", distance)
        payload, pack = call(
            lambda *refs: again_kernel(plan, distance, *refs),
            [payload, other, pack, far],
            [shared, ((8 * distance * plan.size_a, LANES), bf16)],
        )
        distance *= 2
    other, far = swap(payload, "expert", distance), swap(pack, "expert", distance)
    g_attn, square = call(
        lambda *refs: last_kernel(plan, *refs), [payload, other], [((plan.all_a, LANES), f32), ((n_dp, 8, LANES), f32)]
    )
    square = lax.all_to_all(square, "dp", 0, 0, tiled=True)
    block_a, block_e = ((plan.size_a, LANES), f32), ((plan.size_e, LANES), f32)
    (mine,) = call(
        lambda *refs: rows_kernel(plan, limit, *refs),
        [square, g_attn, g_exp, *state_e, pack, far],
        [((chunk, LANES), bf16)],
    )
    wa, ma, va, we, me, ve = call(
        lambda *refs: own_kernel(plan, limit, *refs),
        [square, g_attn, g_exp, *state_a, *state_e],
        [block_a] * 3 + [block_e] * 3,
    )
    near = [mine] + [swap(mine, "dp", 2 * c) for c in range(1, chips)]
    far = [swap(piece, "dp", 1) for piece in near]
    attn_full, expert_full = put_in_order(plan, near + far)
    new_a = [from_blocks(value, rows_a) for value in (wa, ma, va)]
    new_e = [from_blocks(value, rows_e)[None] for value in (we, me, ve)]
    return (*new_a, *new_e, attn_full, expert_full)


def solution(mesh):
    return jax.shard_map(
        body,
        mesh=mesh,
        in_specs=(
            P(("expert", "dp"), None),
            P(("expert", "dp"), None),
            P("expert", "dp", None),
            P("expert", "dp", None),
            P(("expert", "dp"), None),
            P(("expert", "dp"), None),
            P(("expert", "dp"), None),
            P("expert", "dp", None),
            P("expert", "dp", None),
            P("expert", "dp", None),
        ),
        out_specs=(
            P(("expert", "dp"), None),
            P(("expert", "dp"), None),
            P(("expert", "dp"), None),
            P("expert", "dp", None),
            P("expert", "dp", None),
            P("expert", "dp", None),
            P(),
            P("expert", None, None),
        ),
        check_vma=False,
    )
```

```python
import math

import jax
import jax.numpy as jnp
from jax import lax
from jax.experimental import pallas as pl
from jax.experimental.pallas import tpu as pltpu
from jax.sharding import PartitionSpec as P

beta_first = 0.9
beta_second = 0.95
bias_first = 1.0 - 0.9**10
bias_second = 1.0 - 0.95**10
learn_rate = 0.01
decay_rate = 0.1
adam_eps = 1e-08

LANES = 128
f32, bf16 = jnp.float32, jnp.bfloat16


def adamw(grad, weight, moment, second, factor):
    scaled = factor * grad
    moment_new = beta_first * moment + (1.0 - beta_first) * scaled
    second_new = beta_second * second + (1.0 - beta_second) * scaled * scaled
    update = moment_new / bias_first / (jnp.sqrt(second_new / bias_second) + adam_eps)
    weight_new = weight - learn_rate * (update + decay_rate * weight)
    return (weight_new, moment_new, second_new)


class Plan:
    def __init__(self, n_expert, n_dp, rows_a, rows_e, width):
        self.n_expert, self.n_dp, self.rows_a, self.rows_e = n_expert, n_dp, rows_a, rows_e
        self.width = width
        self.chips = n_dp // 2
        self.blocks = width // LANES
        self.size_a = self.blocks * rows_a
        self.size_e = self.blocks * rows_e
        self.all_a = n_expert * self.size_a
        self.chunk = self.all_a + self.size_e

    def places(self, block):
        attn = [
            (e * self.rows_a + r, e * self.size_a + block * self.rows_a + r)
            for e in range(self.n_expert)
            for r in range(self.rows_a)
        ]
        exp = [(r, self.all_a + block * self.rows_e + r) for r in range(self.rows_e)]
        return attn, exp


def dot(left, right):
    return lax.dot_general(left, right, (((1,), (0,)), ((), ())), preferred_element_type=f32)


def size_of(shape, dtype):
    return math.prod(shape) * jnp.dtype(dtype).itemsize


def call(kernel, args, outs, scratch=(), in_space=pltpu.VMEM, out_space=pltpu.VMEM, copies=False):
    held = sum(size_of(arg.shape, arg.dtype) for arg in args if in_space is pltpu.VMEM)
    held += sum(size_of(*out) for out in outs) + sum(size_of(*buffer) for buffer in scratch)
    semaphores = [pltpu.SemaphoreType.DMA((16,))] if copies else []
    return pl.pallas_call(
        kernel,
        in_specs=[pl.BlockSpec(memory_space=in_space)] * len(args),
        out_specs=[pl.BlockSpec(memory_space=out_space)] * len(outs),
        out_shape=[jax.ShapeDtypeStruct(shape, dtype) for shape, dtype in outs],
        scratch_shapes=[pltpu.VMEM(*buffer) for buffer in scratch] + semaphores,
        compiler_params=pltpu.CompilerParams(vmem_limit_bytes=held + 4 * 1024 * 1024),
    )(*args)


def two_pieces(value):
    high = value.astype(bf16).astype(f32)
    return high, (value - high).astype(bf16).astype(f32)


def by_eights(value):
    return jnp.sum(value.reshape(-1, 8, LANES), axis=0)


STEPS = 4


def each(count, step, unrolled):
    if unrolled:
        for i in range(count):
            step(i)
    else:
        pl.loop(0, count)(step)


def terms_kernel(plan, act_a, dy_a, act_e, dy_e, w, m, v, full, send, pack, act_a_v, dy_a_v, act_e_v, dy_e_v, state, sems):
    tile = plan.width // STEPS
    small = [
        pltpu.make_async_copy(act_a, act_a_v, sems.at[0]),
        pltpu.make_async_copy(act_e, act_e_v, sems.at[1]),
    ]
    big = []
    for t in range(STEPS):
        cols = pl.ds(t * tile, tile)
        big.append(pltpu.make_async_copy(dy_a.at[:, cols], dy_a_v.at[:, cols], sems.at[2 + 2 * t]))
        big.append(pltpu.make_async_copy(dy_e.at[:, cols], dy_e_v.at[:, cols], sems.at[3 + 2 * t]))
    extra = [pltpu.make_async_copy(ref, state.at[i], sems.at[2 + 2 * STEPS + i]) for i, ref in enumerate((w, m, v))]
    for copy in small + big + extra:
        copy.start()

    me = lax.axis_index("dp")

    def pick(groups, per_owner, count):
        shape = (groups * plan.n_dp, count)
        row = lax.broadcasted_iota(jnp.int32, shape, 0)
        col = lax.broadcasted_iota(jnp.int32, shape, 1)
        group, place = row // plan.n_dp, row % plan.n_dp
        owner = (2 * (place % plan.chips) + place // plan.chips) ^ me
        want = ((group // per_owner) * plan.n_dp + owner) * per_owner + group % per_owner
        return (want == col).astype(bf16)

    for copy in small:
        copy.wait()
    left_a = dot(pick(plan.n_expert * plan.rows_a, plan.rows_a, act_a.shape[0]), act_a_v[...]).astype(bf16)
    left_e = dot(pick(plan.rows_e, plan.rows_e, act_e.shape[0]), act_e_v[...]).astype(bf16)
    n_dp = plan.n_dp
    for t in range(STEPS):
        cols = pl.ds(t * tile, tile)
        big[2 * t].wait()
        terms_a = dot(left_a, dy_a_v[:, cols])
        big[2 * t + 1].wait()
        terms_e = dot(left_e, dy_e_v[:, cols])
        for b in range(tile // LANES):
            attn, exp = plan.places(t * (tile // LANES) + b)
            span = slice(b * LANES, (b + 1) * LANES)
            for terms, places in ((terms_a, attn), (terms_e, exp)):
                for group, start in places:
                    full[pl.ds(start, n_dp, stride=plan.chunk), :] = terms[group * n_dp : (group + 1) * n_dp, span]
    for c in range(plan.chips):
        send[pl.ds(c * plan.chunk, plan.chunk), :] = full[
            pl.ds((plan.chips + c) * plan.chunk, plan.chunk), :
        ].astype(bf16)
    for copy in extra:
        copy.wait()
    size = plan.size_a
    for i in range(3):
        pack[pl.ds(i * size, size), :] = state[i].astype(bf16)


def make_terms(plan, act_a, dy_a, act_e, dy_e, w, m, v):
    args = (act_a, dy_a, act_e, dy_e, w, m, v)
    half = plan.chips * plan.chunk
    return call(
        lambda *refs: terms_kernel(plan, *refs),
        args,
        [((2 * half, LANES), f32), ((half, LANES), bf16), ((3 * plan.size_a, LANES), bf16)],
        [
            (act_a.shape, bf16),
            (dy_a.shape, bf16),
            (act_e.shape, bf16),
            (dy_e.shape, bf16),
            ((3,) + w.shape, f32),
        ],
        in_space=pltpu.HBM,
        copies=True,
    )


def share_kernel(plan, *refs):
    held, far, own, got, (payload, g_exp, both) = *refs[:3], refs[3:-3], refs[-3:]
    both[0], both[1] = held[...], far[...]
    total = own[...]
    for ref in got:
        total = total + ref[...].astype(f32)
    a = plan.all_a
    exp = total[a:]
    g_exp[...] = exp
    payload[:a, :] = total[:a].astype(bf16)
    payload[a:, :] = jnp.concatenate(two_pieces(by_eights(exp * exp)), axis=0).astype(bf16)


def pair_sum(plan, mine, other):
    a = plan.all_a
    attn = mine[:a, :].astype(f32) + other[:a, :].astype(f32)
    one, two = mine[a:, :].astype(f32), other[a:, :].astype(f32)
    return attn, (one[:8] + one[8:]) + (two[:8] + two[8:])


def again_kernel(plan, mine, other, payload):
    attn, square = pair_sum(plan, mine, other)
    a = plan.all_a
    payload[:a, :] = attn.astype(bf16)
    payload[a:, :] = jnp.concatenate(two_pieces(square), axis=0).astype(bf16)


def last_kernel(plan, mine, other, g_attn, square):
    attn, partial = pair_sum(plan, mine, other)
    g_attn[...] = attn
    square[...] = jnp.broadcast_to((partial + by_eights(attn * attn))[None], square.shape)


def clip_factor(limit, square):
    norm = jnp.sqrt(jnp.sum(jnp.sum(square[...], axis=0), keepdims=True))
    return jnp.minimum(1.0, limit / (norm + 1e-06))


def rows_kernel(plan, limit, square, g_attn, g_exp, we, me, ve, both, *refs):
    far, mine = refs[:-1], refs[-1]
    factor = clip_factor(limit, square)
    size, place = plan.size_a, lax.axis_index("expert")
    for q, states in enumerate([both.at[0], both.at[1], *far]):
        rows = pl.ds(pl.multiple_of((place ^ q) * size, 16), size)
        old = [states[pl.ds(i * size, size), :].astype(f32) for i in range(3)]
        weight, _, _ = adamw(g_attn[rows, :], *old, factor)
        mine[rows, :] = weight.astype(bf16)
    weight, _, _ = adamw(g_exp[...], we[...], me[...], ve[...], factor)
    mine[plan.all_a :, :] = weight.astype(bf16)


def own_kernel(plan, limit, *refs):
    square, g_attn, g_exp = refs[:3]
    state, new = refs[3:9], refs[9:]
    factor = clip_factor(limit, square)
    rows = pl.ds(pl.multiple_of(lax.axis_index("expert") * plan.size_a, 16), plan.size_a)
    for b, grad in enumerate((g_attn[rows, :], g_exp[...])):
        values = adamw(grad, *[ref[...] for ref in state[3 * b : 3 * b + 3]], factor)
        for ref, value in zip(new[3 * b : 3 * b + 3], values):
            ref[...] = value


PARTS = 2


def order_kernel(plan, *refs):
    n_dp = plan.n_dp
    parts, (attn, exp, rows, rows_a, rows_e, attn_v, exp_v, sems) = refs[:n_dp], refs[n_dp:]
    me = lax.axis_index("dp")
    for i, part in enumerate(parts):
        owner = (2 * (-i % plan.chips) + i // plan.chips) ^ me
        rows[pl.ds(pl.multiple_of(owner * plan.chunk, 16), plan.chunk), :] = part[...].astype(f32)
    count_e = exp.shape[1]

    def lanes(b):
        return pl.ds(b * LANES if isinstance(b, int) else pl.multiple_of(b * LANES, LANES), LANES)

    def gather(b):
        places_a, places_e = plan.places(b)
        values = [rows[pl.ds(start, n_dp, stride=plan.chunk), :] for _, start in places_a]
        if plan.rows_a == 1:
            attn_v[:, lanes(b)] = jnp.concatenate(values, axis=0).astype(bf16)
        else:
            for (group, _), value in zip(places_a, values):
                start = (group // plan.rows_a) * n_dp * plan.rows_a + group % plan.rows_a
                rows_a[pl.ds(start, n_dp, stride=plan.rows_a), :] = value
            attn_v[:, lanes(b)] = rows_a[...].astype(bf16)
        for r, start in places_e:
            rows_e[pl.ds(b * count_e + r, n_dp, stride=plan.rows_e), :] = rows[
                pl.ds(start, n_dp, stride=plan.chunk), :
            ]

    def finish(b):
        exp_v[:, lanes(b)] = rows_e[pl.ds(b * count_e, count_e), :].astype(bf16)

    copies = []
    count = plan.blocks // PARTS
    for part in range(PARTS):
        each(count, lambda b: gather(part * count + b), n_dp <= 8)
        each(count, lambda b: finish(part * count + b), True)
        cols = pl.ds(part * count * LANES, count * LANES)
        copies.append(pltpu.make_async_copy(attn_v.at[:, cols], attn.at[:, cols], sems.at[2 * part]))
        copies.append(pltpu.make_async_copy(exp_v.at[:, cols], exp.at[0, :, cols], sems.at[2 * part + 1]))
        for copy in copies[-2:]:
            copy.start()
    for copy in copies:
        copy.wait()


def put_in_order(plan, parts):
    count_a = plan.n_expert * plan.n_dp * plan.rows_a
    count_e = plan.n_dp * plan.rows_e
    return call(
        lambda *refs: order_kernel(plan, *refs),
        parts,
        [((count_a, plan.width), bf16), ((1, count_e, plan.width), bf16)],
        [
            ((plan.n_dp * plan.chunk, LANES), f32),
            ((count_a, LANES), f32),
            ((plan.blocks * count_e, LANES), f32),
            ((count_a, plan.width), bf16),
            ((count_e, plan.width), bf16),
        ],
        out_space=pltpu.HBM,
        copies=True,
    )


def swap(value, axis, distance):
    size = lax.axis_size(axis)
    return lax.ppermute(value, axis, [(i, i ^ distance) for i in range(size)])


def to_blocks(value):
    rows, width = value.shape
    return value.reshape(rows, width // LANES, LANES).transpose(1, 0, 2).reshape(-1, LANES)


def from_blocks(value, rows):
    return value.reshape(-1, rows, LANES).transpose(1, 0, 2).reshape(rows, -1)


def body(act_attn, dy_attn, act_exp, dy_exp, w_attn, m_attn, v_attn, w_exp, m_exp, v_exp):
    width = w_attn.shape[1]
    n_expert = lax.axis_size("expert")
    n_dp = lax.axis_size("dp")
    rows_a, rows_e = w_attn.shape[0], w_exp.shape[1]
    plan = Plan(n_expert, n_dp, rows_a, rows_e, width)
    total_params = width * (act_attn.shape[1] + n_expert * act_exp.shape[2])
    limit = 0.5 * math.sqrt(total_params)
    chips, chunk = plan.chips, plan.chunk
    state_a = [to_blocks(value) for value in (w_attn, m_attn, v_attn)]
    state_e = [to_blocks(value[0]) for value in (w_exp, m_exp, v_exp)]

    held = [pltpu.with_memory_space_constraint(x, pltpu.HBM) for x in (act_attn.T, dy_attn, act_exp[0].T, dy_exp[0])]
    full, send, pack = make_terms(plan, *held, *[pltpu.with_memory_space_constraint(x, pltpu.HBM) for x in state_a])
    got = swap(send, "dp", 1)
    sums = [
        full[c * chunk : (c + 1) * chunk] + got[c * chunk : (c + 1) * chunk].astype(f32) for c in range(chips)
    ]
    got = [swap(sums[c].astype(bf16), "dp", 2 * c) for c in reversed(range(1, chips))]
    shared = ((plan.all_a + 16, LANES), bf16)
    payload, g_exp, both = call(
        lambda *refs: share_kernel(plan, *refs),
        [pack, swap(pack, "expert", 1), sums[0]] + got,
        [shared, ((plan.size_e, LANES), f32), ((2,) + pack.shape, bf16)],
    )
    distance = 1
    while 2 * distance < n_expert:
        other = swap(payload, "expert", distance)
        (payload,) = call(lambda *refs: again_kernel(plan, *refs), [payload, other], [shared])
        distance *= 2
    other = swap(payload, "expert", distance)
    far = [swap(pack, "expert", q) for q in range(2, n_expert)]
    g_attn, square = call(
        lambda *refs: last_kernel(plan, *refs), [payload, other], [((plan.all_a, LANES), f32), ((n_dp, 8, LANES), f32)]
    )
    square = lax.all_to_all(square, "dp", 0, 0, tiled=True)
    block_a, block_e = ((plan.size_a, LANES), f32), ((plan.size_e, LANES), f32)
    (mine,) = call(
        lambda *refs: rows_kernel(plan, limit, *refs),
        [square, g_attn, g_exp, *state_e, both, *far],
        [((chunk, LANES), bf16)],
    )
    wa, ma, va, we, me, ve = call(
        lambda *refs: own_kernel(plan, limit, *refs),
        [square, g_attn, g_exp, *state_a, *state_e],
        [block_a] * 3 + [block_e] * 3,
    )
    near = [mine] + [swap(mine, "dp", 2 * c) for c in reversed(range(1, chips))]
    far = [swap(piece, "dp", 1) for piece in near]
    attn_full, expert_full = put_in_order(plan, near + far)
    new_a = [from_blocks(value, rows_a) for value in (wa, ma, va)]
    new_e = [from_blocks(value, rows_e)[None] for value in (we, me, ve)]
    return (*new_a, *new_e, attn_full, expert_full)


def solution(mesh):
    return jax.shard_map(
        body,
        mesh=mesh,
        in_specs=(
            P(("expert", "dp"), None),
            P(("expert", "dp"), None),
            P("expert", "dp", None),
            P("expert", "dp", None),
            P(("expert", "dp"), None),
            P(("expert", "dp"), None),
            P(("expert", "dp"), None),
            P("expert", "dp", None),
            P("expert", "dp", None),
            P("expert", "dp", None),
        ),
        out_specs=(
            P(("expert", "dp"), None),
            P(("expert", "dp"), None),
            P(("expert", "dp"), None),
            P("expert", "dp", None),
            P("expert", "dp", None),
            P("expert", "dp", None),
            P(),
            P("expert", None, None),
        ),
        check_vma=False,
    )
```

```python
import math

import jax
import jax.numpy as jnp
from jax import lax
from jax.experimental import pallas as pl
from jax.experimental.pallas import tpu as pltpu
from jax.sharding import PartitionSpec as P

beta_first = 0.9
beta_second = 0.95
bias_first = 1.0 - 0.9**10
bias_second = 1.0 - 0.95**10
learn_rate = 0.01
decay_rate = 0.1
adam_eps = 1e-08

LANES = 128
f32, bf16 = jnp.float32, jnp.bfloat16


def adamw(grad, weight, moment, second, factor):
    scaled = factor * grad
    moment_new = beta_first * moment + (1.0 - beta_first) * scaled
    second_new = beta_second * second + (1.0 - beta_second) * scaled * scaled
    update = moment_new / bias_first / (jnp.sqrt(second_new / bias_second) + adam_eps)
    weight_new = weight - learn_rate * (update + decay_rate * weight)
    return (weight_new, moment_new, second_new)


def role_of(chip, core, expert):
    return core ^ ((chip ^ expert ^ (expert // 2)) % 2)


class Plan:
    def __init__(self, n_expert, n_dp, rows_a, rows_e, width):
        self.n_expert, self.n_dp, self.rows_a, self.rows_e = n_expert, n_dp, rows_a, rows_e
        self.width = width
        self.chips = n_dp // 2
        self.blocks = width // LANES
        self.size_a = self.blocks * rows_a
        self.size_e = self.blocks * rows_e
        self.all_a = n_expert * self.size_a
        self.chunk = self.all_a + self.size_e

    def places(self, block):
        attn = [
            (e * self.rows_a + r, e * self.size_a + block * self.rows_a + r)
            for e in range(self.n_expert)
            for r in range(self.rows_a)
        ]
        exp = [(r, self.all_a + block * self.rows_e + r) for r in range(self.rows_e)]
        return attn, exp


def dot(left, right):
    return lax.dot_general(left, right, (((1,), (0,)), ((), ())), preferred_element_type=f32)


def size_of(shape, dtype):
    return math.prod(shape) * jnp.dtype(dtype).itemsize


def call(kernel, args, outs, scratch=(), in_space=pltpu.VMEM, out_space=pltpu.VMEM, copies=False):
    held = sum(size_of(arg.shape, arg.dtype) for arg in args if in_space is pltpu.VMEM)
    held += sum(size_of(*out) for out in outs) + sum(size_of(*buffer) for buffer in scratch)
    semaphores = [pltpu.SemaphoreType.DMA((16,))] if copies else []
    return pl.pallas_call(
        kernel,
        in_specs=[pl.BlockSpec(memory_space=in_space)] * len(args),
        out_specs=[pl.BlockSpec(memory_space=out_space)] * len(outs),
        out_shape=[jax.ShapeDtypeStruct(shape, dtype) for shape, dtype in outs],
        scratch_shapes=[pltpu.VMEM(*buffer) for buffer in scratch] + semaphores,
        compiler_params=pltpu.CompilerParams(vmem_limit_bytes=held + 4 * 1024 * 1024),
    )(*args)


def two_pieces(value):
    high = value.astype(bf16).astype(f32)
    return high, (value - high).astype(bf16).astype(f32)


def by_eights(value):
    return jnp.sum(value.reshape(-1, 8, LANES), axis=0)


STEPS = 4


def each(count, step, unrolled):
    if unrolled:
        for i in range(count):
            step(i)
    else:
        pl.loop(0, count)(step)


def terms_kernel(plan, act_a, dy_a, act_e, dy_e, w, m, v, full, send, pack, act_a_v, dy_a_v, act_e_v, dy_e_v, state, sems):
    tile = plan.width // STEPS
    small = [
        pltpu.make_async_copy(act_a, act_a_v, sems.at[0]),
        pltpu.make_async_copy(act_e, act_e_v, sems.at[1]),
    ]
    big = []
    for t in range(STEPS):
        cols = pl.ds(t * tile, tile)
        big.append(pltpu.make_async_copy(dy_a.at[:, cols], dy_a_v.at[:, cols], sems.at[2 + 2 * t]))
        big.append(pltpu.make_async_copy(dy_e.at[:, cols], dy_e_v.at[:, cols], sems.at[3 + 2 * t]))
    extra = [pltpu.make_async_copy(ref, state.at[i], sems.at[2 + 2 * STEPS + i]) for i, ref in enumerate((w, m, v))]
    for copy in small + big + extra:
        copy.start()

    me, me_ex = lax.axis_index("dp"), lax.axis_index("expert")
    my_role = role_of(me // 2, me % 2, me_ex)

    def pick(groups, per_owner, count, expert):
        shape = (groups * plan.n_dp, count)
        row = lax.broadcasted_iota(jnp.int32, shape, 0)
        col = lax.broadcasted_iota(jnp.int32, shape, 1)
        group, place = row // plan.n_dp, row % plan.n_dp
        chip, role = (place % plan.chips) ^ (me // 2), (place // plan.chips) ^ my_role
        if expert is None:
            expert, base = group // per_owner, (group // per_owner) * plan.n_dp
        else:
            base = 0
        owner = 2 * chip + role_of(chip, role, expert)
        want = (base + owner) * per_owner + group % per_owner
        return (want == col).astype(bf16)

    for copy in small:
        copy.wait()
    left_a = dot(pick(plan.n_expert * plan.rows_a, plan.rows_a, act_a.shape[0], None), act_a_v[...]).astype(bf16)
    left_e = dot(pick(plan.rows_e, plan.rows_e, act_e.shape[0], me_ex), act_e_v[...]).astype(bf16)
    n_dp = plan.n_dp
    for t in range(STEPS):
        cols = pl.ds(t * tile, tile)
        big[2 * t].wait()
        terms_a = dot(left_a, dy_a_v[:, cols])
        big[2 * t + 1].wait()
        terms_e = dot(left_e, dy_e_v[:, cols])
        for b in range(tile // LANES):
            attn, exp = plan.places(t * (tile // LANES) + b)
            span = slice(b * LANES, (b + 1) * LANES)
            for terms, places in ((terms_a, attn), (terms_e, exp)):
                for group, start in places:
                    full[pl.ds(start, n_dp, stride=plan.chunk), :] = terms[group * n_dp : (group + 1) * n_dp, span]
    for c in range(plan.chips):
        send[pl.ds(c * plan.chunk, plan.chunk), :] = full[
            pl.ds((plan.chips + c) * plan.chunk, plan.chunk), :
        ].astype(bf16)
    for copy in extra:
        copy.wait()
    size = plan.size_a
    for i in range(3):
        pack[pl.ds(i * size, size), :] = state[i].astype(bf16)


def make_terms(plan, act_a, dy_a, act_e, dy_e, w, m, v):
    args = (act_a, dy_a, act_e, dy_e, w, m, v)
    half = plan.chips * plan.chunk
    return call(
        lambda *refs: terms_kernel(plan, *refs),
        args,
        [((2 * half, LANES), f32), ((half, LANES), bf16), ((3 * plan.size_a, LANES), bf16)],
        [
            (act_a.shape, bf16),
            (dy_a.shape, bf16),
            (act_e.shape, bf16),
            (dy_e.shape, bf16),
            ((3,) + w.shape, f32),
        ],
        in_space=pltpu.HBM,
        copies=True,
    )


def share_kernel(plan, *refs):
    held, far, own, got, (payload, g_exp, both) = *refs[:3], refs[3:-3], refs[-3:]
    both[0], both[1] = held[...], far[...]
    total = own[...]
    for ref in got:
        total = total + ref[...].astype(f32)
    a = plan.all_a
    exp = total[a:]
    g_exp[...] = exp
    payload[:a, :] = total[:a].astype(bf16)
    payload[a:, :] = jnp.concatenate(two_pieces(by_eights(exp * exp)), axis=0).astype(bf16)


def pair_sum(plan, mine, other):
    a = plan.all_a
    attn = mine[:a, :].astype(f32) + other[:a, :].astype(f32)
    one, two = mine[a:, :].astype(f32), other[a:, :].astype(f32)
    return attn, (one[:8] + one[8:]) + (two[:8] + two[8:])


def again_kernel(plan, mine, other, payload):
    attn, square = pair_sum(plan, mine, other)
    a = plan.all_a
    payload[:a, :] = attn.astype(bf16)
    payload[a:, :] = jnp.concatenate(two_pieces(square), axis=0).astype(bf16)


def last_kernel(plan, mine, other, g_attn, square):
    attn, partial = pair_sum(plan, mine, other)
    g_attn[...] = attn
    square[...] = partial + by_eights(attn * attn)


def clip_factor(limit, squares):
    values = [squares[-i % len(squares)][...] for i in range(len(squares))]
    while len(values) > 1:
        values = [values[i] + values[i + 1] for i in range(0, len(values), 2)]
    norm = jnp.sqrt(jnp.sum(values[0], keepdims=True))
    return jnp.minimum(1.0, limit / (norm + 1e-06))


def rows_kernel(plan, limit, *refs):
    factor = clip_factor(limit, refs[: plan.chips])
    g_attn, g_exp, we, me, ve, both, *far, mine = refs[plan.chips :]
    size, place = plan.size_a, lax.axis_index("expert")
    for q, states in enumerate([both.at[0], both.at[1], *far]):
        rows = pl.ds(pl.multiple_of((place ^ q) * size, 16), size)
        old = [states[pl.ds(i * size, size), :].astype(f32) for i in range(3)]
        weight, _, _ = adamw(g_attn[rows, :], *old, factor)
        mine[rows, :] = weight.astype(bf16)
    weight, _, _ = adamw(g_exp[...], we[...], me[...], ve[...], factor)
    mine[plan.all_a :, :] = weight.astype(bf16)


def own_kernel(plan, limit, *refs):
    factor = clip_factor(limit, refs[: plan.chips])
    g_attn, g_exp = refs[plan.chips : plan.chips + 2]
    state, new = refs[plan.chips + 2 : plan.chips + 8], refs[plan.chips + 8 :]
    rows = pl.ds(pl.multiple_of(lax.axis_index("expert") * plan.size_a, 16), plan.size_a)
    for b, grad in enumerate((g_attn[rows, :], g_exp[...])):
        values = adamw(grad, *[ref[...] for ref in state[3 * b : 3 * b + 3]], factor)
        for ref, value in zip(new[3 * b : 3 * b + 3], values):
            ref[...] = value


PARTS = 2


def order_kernel(plan, *refs):
    n_dp = plan.n_dp
    parts, (attn, exp, rows, rows_a, rows_e, attn_v, exp_v, sems) = refs[:n_dp], refs[n_dp:]
    me = lax.axis_index("dp")
    me_ex = lax.axis_index("expert")
    my_role = role_of(me // 2, me % 2, me_ex)
    for i, part in enumerate(parts):
        chip, role = (-i % plan.chips) ^ (me // 2), (i // plan.chips) ^ my_role
        blocks = [(e, e * plan.size_a, plan.size_a) for e in range(plan.n_expert)]
        for expert, start, size in blocks + [(me_ex, plan.all_a, plan.size_e)]:
            owner = 2 * chip + role_of(chip, role, expert)
            to = pl.multiple_of(owner * plan.chunk + start, 16)
            rows[pl.ds(to, size), :] = part[pl.ds(start, size), :].astype(f32)
    count_e = exp.shape[1]

    def lanes(b):
        return pl.ds(b * LANES if isinstance(b, int) else pl.multiple_of(b * LANES, LANES), LANES)

    def gather(b):
        places_a, places_e = plan.places(b)
        values = [rows[pl.ds(start, n_dp, stride=plan.chunk), :] for _, start in places_a]
        if plan.rows_a == 1:
            attn_v[:, lanes(b)] = jnp.concatenate(values, axis=0).astype(bf16)
        else:
            for (group, _), value in zip(places_a, values):
                start = (group // plan.rows_a) * n_dp * plan.rows_a + group % plan.rows_a
                rows_a[pl.ds(start, n_dp, stride=plan.rows_a), :] = value
            attn_v[:, lanes(b)] = rows_a[...].astype(bf16)
        for r, start in places_e:
            rows_e[pl.ds(b * count_e + r, n_dp, stride=plan.rows_e), :] = rows[
                pl.ds(start, n_dp, stride=plan.chunk), :
            ]

    def finish(b):
        exp_v[:, lanes(b)] = rows_e[pl.ds(b * count_e, count_e), :].astype(bf16)

    copies = []
    count = plan.blocks // PARTS
    for part in range(PARTS):
        each(count, lambda b: gather(part * count + b), n_dp <= 8)
        each(count, lambda b: finish(part * count + b), True)
        cols = pl.ds(part * count * LANES, count * LANES)
        copies.append(pltpu.make_async_copy(attn_v.at[:, cols], attn.at[:, cols], sems.at[2 * part]))
        copies.append(pltpu.make_async_copy(exp_v.at[:, cols], exp.at[0, :, cols], sems.at[2 * part + 1]))
        for copy in copies[-2:]:
            copy.start()
    for copy in copies:
        copy.wait()


def put_in_order(plan, parts):
    count_a = plan.n_expert * plan.n_dp * plan.rows_a
    count_e = plan.n_dp * plan.rows_e
    return call(
        lambda *refs: order_kernel(plan, *refs),
        parts,
        [((count_a, plan.width), bf16), ((1, count_e, plan.width), bf16)],
        [
            ((plan.n_dp * plan.chunk, LANES), f32),
            ((count_a, LANES), f32),
            ((plan.blocks * count_e, LANES), f32),
            ((count_a, plan.width), bf16),
            ((count_e, plan.width), bf16),
        ],
        out_space=pltpu.HBM,
        copies=True,
    )


def swap(value, chips=0, experts=0):
    n_expert, n_dp = lax.axis_size("expert"), lax.axis_size("dp")
    pairs = []
    for e in range(n_expert):
        for j in range(n_dp):
            role = role_of(j // 2, j % 2, e)
            chip, expert = (j // 2) ^ chips, e ^ experts
            pairs.append((e * n_dp + j, expert * n_dp + 2 * chip + role_of(chip, role, expert)))
    return lax.ppermute(value, ("expert", "dp"), pairs)


def swap_cores(value):
    return lax.ppermute(value, "dp", [(i, i ^ 1) for i in range(lax.axis_size("dp"))])


def to_blocks(value):
    rows, width = value.shape
    return value.reshape(rows, width // LANES, LANES).transpose(1, 0, 2).reshape(-1, LANES)


def from_blocks(value, rows):
    return value.reshape(-1, rows, LANES).transpose(1, 0, 2).reshape(rows, -1)


def body(act_attn, dy_attn, act_exp, dy_exp, w_attn, m_attn, v_attn, w_exp, m_exp, v_exp):
    width = w_attn.shape[1]
    n_expert = lax.axis_size("expert")
    n_dp = lax.axis_size("dp")
    rows_a, rows_e = w_attn.shape[0], w_exp.shape[1]
    plan = Plan(n_expert, n_dp, rows_a, rows_e, width)
    total_params = width * (act_attn.shape[1] + n_expert * act_exp.shape[2])
    limit = 0.5 * math.sqrt(total_params)
    chips, chunk = plan.chips, plan.chunk
    state_a = [to_blocks(value) for value in (w_attn, m_attn, v_attn)]
    state_e = [to_blocks(value[0]) for value in (w_exp, m_exp, v_exp)]

    held = [pltpu.with_memory_space_constraint(x, pltpu.HBM) for x in (act_attn.T, dy_attn, act_exp[0].T, dy_exp[0])]
    full, send, pack = make_terms(plan, *held, *[pltpu.with_memory_space_constraint(x, pltpu.HBM) for x in state_a])
    got = swap_cores(send)
    sums = [
        full[c * chunk : (c + 1) * chunk] + got[c * chunk : (c + 1) * chunk].astype(f32) for c in range(chips)
    ]
    got = [swap(sums[c].astype(bf16), chips=c) for c in reversed(range(1, chips))]
    shared = ((plan.all_a + 16, LANES), bf16)
    payload, g_exp, both = call(
        lambda *refs: share_kernel(plan, *refs),
        [pack, swap(pack, experts=1), sums[0]] + got,
        [shared, ((plan.size_e, LANES), f32), ((2,) + pack.shape, bf16)],
    )
    distance = 1
    while 2 * distance < n_expert:
        other = swap(payload, experts=distance)
        (payload,) = call(lambda *refs: again_kernel(plan, *refs), [payload, other], [shared])
        distance *= 2
    other = swap(payload, experts=distance)
    far = [swap(pack, experts=q) for q in range(2, n_expert)]
    g_attn, square = call(
        lambda *refs: last_kernel(plan, *refs), [payload, other], [((plan.all_a, LANES), f32), ((8, LANES), f32)]
    )
    square = square + swap_cores(square)
    squares = [square] + [swap(square, chips=c) for c in reversed(range(1, chips))]
    block_a, block_e = ((plan.size_a, LANES), f32), ((plan.size_e, LANES), f32)
    (mine,) = call(
        lambda *refs: rows_kernel(plan, limit, *refs),
        [*squares, g_attn, g_exp, *state_e, both, *far],
        [((chunk, LANES), bf16)],
    )
    wa, ma, va, we, me, ve = call(
        lambda *refs: own_kernel(plan, limit, *refs),
        [*squares, g_attn, g_exp, *state_a, *state_e],
        [block_a] * 3 + [block_e] * 3,
    )
    near = [mine] + [swap(mine, chips=c) for c in reversed(range(1, chips))]
    far = [swap_cores(piece) for piece in near]
    attn_full, expert_full = put_in_order(plan, near + far)
    new_a = [from_blocks(value, rows_a) for value in (wa, ma, va)]
    new_e = [from_blocks(value, rows_e)[None] for value in (we, me, ve)]
    return (*new_a, *new_e, attn_full, expert_full)


def solution(mesh):
    return jax.shard_map(
        body,
        mesh=mesh,
        in_specs=(
            P(("expert", "dp"), None),
            P(("expert", "dp"), None),
            P("expert", "dp", None),
            P("expert", "dp", None),
            P(("expert", "dp"), None),
            P(("expert", "dp"), None),
            P(("expert", "dp"), None),
            P("expert", "dp", None),
            P("expert", "dp", None),
            P("expert", "dp", None),
        ),
        out_specs=(
            P(("expert", "dp"), None),
            P(("expert", "dp"), None),
            P(("expert", "dp"), None),
            P("expert", "dp", None),
            P("expert", "dp", None),
            P("expert", "dp", None),
            P(),
            P("expert", None, None),
        ),
        check_vma=False,
    )
```

```python
import math

import jax
import jax.numpy as jnp
from jax import lax
from jax.experimental import pallas as pl
from jax.experimental.pallas import tpu as pltpu
from jax.sharding import PartitionSpec as P

beta_first = 0.9
beta_second = 0.95
bias_first = 1.0 - 0.9**10
bias_second = 1.0 - 0.95**10
learn_rate = 0.01
decay_rate = 0.1
adam_eps = 1e-08

LANES = 128
f32, bf16 = jnp.float32, jnp.bfloat16


def adamw(grad, weight, moment, second, factor):
    scaled = factor * grad
    moment_new = beta_first * moment + (1.0 - beta_first) * scaled
    second_new = beta_second * second + (1.0 - beta_second) * scaled * scaled
    update = moment_new / bias_first / (jnp.sqrt(second_new / bias_second) + adam_eps)
    weight_new = weight - learn_rate * (update + decay_rate * weight)
    return (weight_new, moment_new, second_new)


def role_of(chip, core, expert):
    return core ^ ((chip ^ expert ^ (expert // 2)) % 2)


class Plan:
    def __init__(self, n_expert, n_dp, rows_a, rows_e, width):
        self.n_expert, self.n_dp, self.rows_a, self.rows_e = n_expert, n_dp, rows_a, rows_e
        self.width = width
        self.chips = n_dp // 2
        self.blocks = width // LANES
        self.size_a = self.blocks * rows_a
        self.size_e = self.blocks * rows_e
        self.all_a = n_expert * self.size_a
        self.chunk = self.all_a + self.size_e
        self.turned = n_dp == 8 and rows_a == 1

    def places(self, block):
        attn = [
            (e * self.rows_a + r, e * self.size_a + block * self.rows_a + r)
            for e in range(self.n_expert)
            for r in range(self.rows_a)
        ]
        exp = [(r, self.all_a + block * self.rows_e + r) for r in range(self.rows_e)]
        return attn, exp


def dot(left, right):
    return lax.dot_general(left, right, (((1,), (0,)), ((), ())), preferred_element_type=f32)


def size_of(shape, dtype):
    return math.prod(shape) * jnp.dtype(dtype).itemsize


def call(kernel, args, outs, scratch=(), in_space=pltpu.VMEM, out_space=pltpu.VMEM, copies=False):
    held = sum(size_of(arg.shape, arg.dtype) for arg in args if in_space is pltpu.VMEM)
    held += sum(size_of(*out) for out in outs) + sum(size_of(*buffer) for buffer in scratch)
    semaphores = [pltpu.SemaphoreType.DMA((16,))] if copies else []
    return pl.pallas_call(
        kernel,
        in_specs=[pl.BlockSpec(memory_space=in_space)] * len(args),
        out_specs=[pl.BlockSpec(memory_space=out_space)] * len(outs),
        out_shape=[jax.ShapeDtypeStruct(shape, dtype) for shape, dtype in outs],
        scratch_shapes=[pltpu.VMEM(*buffer) for buffer in scratch] + semaphores,
        compiler_params=pltpu.CompilerParams(vmem_limit_bytes=held + 4 * 1024 * 1024),
    )(*args)


def two_pieces(value):
    high = value.astype(bf16).astype(f32)
    return high, (value - high).astype(bf16).astype(f32)


def by_eights(value):
    return jnp.sum(value.reshape(-1, 8, LANES), axis=0)


STEPS = 4


def each(count, step, unrolled):
    if unrolled:
        for i in range(count):
            step(i)
    else:
        pl.loop(0, count)(step)


def terms_kernel(plan, act_a, dy_a, act_e, dy_e, w, m, v, full, send, pack, act_a_v, dy_a_v, act_e_v, dy_e_v, state, sems):
    tile = plan.width // STEPS
    small = [
        pltpu.make_async_copy(act_a, act_a_v, sems.at[0]),
        pltpu.make_async_copy(act_e, act_e_v, sems.at[1]),
    ]
    big = []
    for t in range(STEPS):
        cols = pl.ds(t * tile, tile)
        big.append(pltpu.make_async_copy(dy_a.at[:, cols], dy_a_v.at[:, cols], sems.at[2 + 2 * t]))
        big.append(pltpu.make_async_copy(dy_e.at[:, cols], dy_e_v.at[:, cols], sems.at[3 + 2 * t]))
    extra = [pltpu.make_async_copy(ref, state.at[i], sems.at[2 + 2 * STEPS + i]) for i, ref in enumerate((w, m, v))]
    for copy in small + big + extra:
        copy.start()

    me, me_ex = lax.axis_index("dp"), lax.axis_index("expert")
    my_role = role_of(me // 2, me % 2, me_ex)

    def pick(groups, per_owner, count, expert):
        shape = (groups * plan.n_dp, count)
        row = lax.broadcasted_iota(jnp.int32, shape, 0)
        col = lax.broadcasted_iota(jnp.int32, shape, 1)
        group, place = row // plan.n_dp, row % plan.n_dp
        chip, role = (place % plan.chips) ^ (me // 2), (place // plan.chips) ^ my_role
        if expert is None:
            expert, base = group // per_owner, (group // per_owner) * plan.n_dp
        else:
            base = 0
        owner = 2 * chip + role_of(chip, role, expert)
        want = (base + owner) * per_owner + group % per_owner
        return (want == col).astype(bf16)

    for copy in small:
        copy.wait()
    left_a = dot(pick(plan.n_expert * plan.rows_a, plan.rows_a, act_a.shape[0], None), act_a_v[...]).astype(bf16)
    left_e = dot(pick(plan.rows_e, plan.rows_e, act_e.shape[0], me_ex), act_e_v[...]).astype(bf16)
    n_dp = plan.n_dp
    for t in range(STEPS):
        cols = pl.ds(t * tile, tile)
        big[2 * t].wait()
        terms_a = dot(left_a, dy_a_v[:, cols])
        big[2 * t + 1].wait()
        terms_e = dot(left_e, dy_e_v[:, cols])
        for b in range(tile // LANES):
            attn, exp = plan.places(t * (tile // LANES) + b)
            span = slice(b * LANES, (b + 1) * LANES)
            for terms, places in ((terms_a, attn), (terms_e, exp)):
                for group, start in places:
                    full[pl.ds(start, n_dp, stride=plan.chunk), :] = terms[group * n_dp : (group + 1) * n_dp, span]
    for c in range(plan.chips):
        send[pl.ds(c * plan.chunk, plan.chunk), :] = full[
            pl.ds((plan.chips + c) * plan.chunk, plan.chunk), :
        ].astype(bf16)
    for copy in extra:
        copy.wait()
    size = plan.size_a
    for i in range(3):
        pack[pl.ds(i * size, size), :] = state[i].astype(bf16)


def make_terms(plan, act_a, dy_a, act_e, dy_e, w, m, v):
    args = (act_a, dy_a, act_e, dy_e, w, m, v)
    half = plan.chips * plan.chunk
    return call(
        lambda *refs: terms_kernel(plan, *refs),
        args,
        [((2 * half, LANES), f32), ((half, LANES), bf16), ((3 * plan.size_a, LANES), bf16)],
        [
            (act_a.shape, bf16),
            (dy_a.shape, bf16),
            (act_e.shape, bf16),
            (dy_e.shape, bf16),
            ((3,) + w.shape, f32),
        ],
        in_space=pltpu.HBM,
        copies=True,
    )


def share_kernel(plan, *refs):
    held, far, own, got, (payload, g_exp, both) = *refs[:3], refs[3:-3], refs[-3:]
    both[0], both[1] = held[...], far[...]
    total = own[...]
    for ref in got:
        total = total + ref[...].astype(f32)
    a = plan.all_a
    exp = total[a:]
    g_exp[...] = exp
    payload[:a, :] = total[:a].astype(bf16)
    payload[a:, :] = jnp.concatenate(two_pieces(by_eights(exp * exp)), axis=0).astype(bf16)


def pair_sum(plan, mine, other):
    a = plan.all_a
    attn = mine[:a, :].astype(f32) + other[:a, :].astype(f32)
    one, two = mine[a:, :].astype(f32), other[a:, :].astype(f32)
    return attn, (one[:8] + one[8:]) + (two[:8] + two[8:])


def again_kernel(plan, mine, other, payload):
    attn, square = pair_sum(plan, mine, other)
    a = plan.all_a
    payload[:a, :] = attn.astype(bf16)
    payload[a:, :] = jnp.concatenate(two_pieces(square), axis=0).astype(bf16)


def last_kernel(plan, mine, other, g_attn, square):
    attn, partial = pair_sum(plan, mine, other)
    g_attn[...] = attn
    square[...] = partial + by_eights(attn * attn)


def square_order(chips):
    return [0, *reversed(range(1, chips - 1)), chips - 1]


def clip_factor(limit, squares):
    order = square_order(len(squares))
    values = [squares[order.index(c)][...] for c in range(len(squares))]
    while len(values) > 1:
        values = [values[i] + values[i + 1] for i in range(0, len(values), 2)]
    norm = jnp.sqrt(jnp.sum(values[0], keepdims=True))
    return jnp.minimum(1.0, limit / (norm + 1e-06))


def rows_kernel(plan, limit, *refs):
    factor = clip_factor(limit, refs[: plan.chips])
    g_attn, g_exp, we, me, ve, both, *far, mine = refs[plan.chips :]
    size, place = plan.size_a, lax.axis_index("expert")
    for q, states in enumerate([both.at[0], both.at[1], *far]):
        rows = pl.ds(pl.multiple_of((place ^ q) * size, 16), size)
        old = [states[pl.ds(i * size, size), :].astype(f32) for i in range(3)]
        weight, _, _ = adamw(g_attn[rows, :], *old, factor)
        mine[rows, :] = weight.astype(bf16)
    weight, _, _ = adamw(g_exp[...], we[...], me[...], ve[...], factor)
    mine[plan.all_a :, :] = weight.astype(bf16)


def own_kernel(plan, limit, *refs):
    factor = clip_factor(limit, refs[: plan.chips])
    g_attn, g_exp = refs[plan.chips : plan.chips + 2]
    state, new = refs[plan.chips + 2 : plan.chips + 8], refs[plan.chips + 8 :]
    rows = pl.ds(pl.multiple_of(lax.axis_index("expert") * plan.size_a, 16), plan.size_a)
    for b, grad in enumerate((g_attn[rows, :], g_exp[...])):
        values = adamw(grad, *[ref[...] for ref in state[3 * b : 3 * b + 3]], factor)
        for ref, value in zip(new[3 * b : 3 * b + 3], values):
            ref[...] = value


PARTS = 2


def order_kernel(plan, *refs):
    n_dp = plan.n_dp
    parts, (attn, exp, rows, rows_a, rows_e, attn_v, exp_v, sems) = refs[:n_dp], refs[n_dp:]
    me = lax.axis_index("dp")
    me_ex = lax.axis_index("expert")
    my_role = role_of(me // 2, me % 2, me_ex)
    for i, part in enumerate(parts):
        chip, role = (-i % plan.chips) ^ (me // 2), (i // plan.chips) ^ my_role
        blocks = [(e, e * plan.size_a, plan.size_a) for e in range(plan.n_expert)]
        for expert, start, size in blocks + [(me_ex, plan.all_a, plan.size_e)]:
            owner = 2 * chip + role_of(chip, role, expert)
            to = pl.multiple_of(owner * plan.chunk + start, 16)
            rows[pl.ds(to, size), :] = part[pl.ds(start, size), :].astype(f32)
    count_e = exp.shape[1]

    def lanes(b):
        return pl.ds(b * LANES if isinstance(b, int) else pl.multiple_of(b * LANES, LANES), LANES)

    def turn(part):
        for e in range(plan.n_expert):
            first = e * plan.size_a + part * count
            value = jnp.stack([rows[pl.ds(j * plan.chunk + first, count), :] for j in range(n_dp)])
            value = value.transpose(1, 0, 2)
            for b in range(count):
                rows_a[pl.ds(e * n_dp, n_dp), lanes(b)] = value[b]
        first = plan.all_a + part * count * plan.rows_e
        value = jnp.stack([rows[pl.ds(j * plan.chunk + first, count * plan.rows_e), :] for j in range(n_dp)])
        value = value.transpose(1, 0, 2)
        for b in range(count):
            for r in range(plan.rows_e):
                start = (part * count + b) * count_e + r
                rows_e[pl.ds(start, n_dp, stride=plan.rows_e), :] = value[b * plan.rows_e + r]
        attn_v[:, pl.ds(part * count * LANES, count * LANES)] = rows_a[...].astype(bf16)

    def gather(b):
        places_a, places_e = plan.places(b)
        values = [rows[pl.ds(start, n_dp, stride=plan.chunk), :] for _, start in places_a]
        if plan.rows_a == 1:
            attn_v[:, lanes(b)] = jnp.concatenate(values, axis=0).astype(bf16)
        else:
            for (group, _), value in zip(places_a, values):
                start = (group // plan.rows_a) * n_dp * plan.rows_a + group % plan.rows_a
                rows_a[pl.ds(start, n_dp, stride=plan.rows_a), :] = value
            attn_v[:, lanes(b)] = rows_a[...].astype(bf16)
        for r, start in places_e:
            rows_e[pl.ds(b * count_e + r, n_dp, stride=plan.rows_e), :] = rows[
                pl.ds(start, n_dp, stride=plan.chunk), :
            ]

    def finish(b):
        exp_v[:, lanes(b)] = rows_e[pl.ds(b * count_e, count_e), :].astype(bf16)

    copies = []
    count = plan.blocks // PARTS
    for part in range(PARTS):
        if plan.turned:
            turn(part)
        else:
            each(count, lambda b: gather(part * count + b), n_dp <= 8)
        each(count, lambda b: finish(part * count + b), True)
        cols = pl.ds(part * count * LANES, count * LANES)
        copies.append(pltpu.make_async_copy(attn_v.at[:, cols], attn.at[:, cols], sems.at[2 * part]))
        copies.append(pltpu.make_async_copy(exp_v.at[:, cols], exp.at[0, :, cols], sems.at[2 * part + 1]))
        for copy in copies[-2:]:
            copy.start()
    for copy in copies:
        copy.wait()


def put_in_order(plan, parts):
    count_a = plan.n_expert * plan.n_dp * plan.rows_a
    count_e = plan.n_dp * plan.rows_e
    return call(
        lambda *refs: order_kernel(plan, *refs),
        parts,
        [((count_a, plan.width), bf16), ((1, count_e, plan.width), bf16)],
        [
            ((plan.n_dp * plan.chunk, LANES), f32),
            ((count_a, plan.width // PARTS if plan.turned else LANES), f32),
            ((plan.blocks * count_e, LANES), f32),
            ((count_a, plan.width), bf16),
            ((count_e, plan.width), bf16),
        ],
        out_space=pltpu.HBM,
        copies=True,
    )


def swap(value, chips=0, experts=0):
    n_expert, n_dp = lax.axis_size("expert"), lax.axis_size("dp")
    pairs = []
    for e in range(n_expert):
        for j in range(n_dp):
            role = role_of(j // 2, j % 2, e)
            chip, expert = (j // 2) ^ chips, e ^ experts
            pairs.append((e * n_dp + j, expert * n_dp + 2 * chip + role_of(chip, role, expert)))
    return lax.ppermute(value, ("expert", "dp"), pairs)


def swap_cores(value):
    return lax.ppermute(value, "dp", [(i, i ^ 1) for i in range(lax.axis_size("dp"))])


def to_blocks(value):
    rows, width = value.shape
    return value.reshape(rows, width // LANES, LANES).transpose(1, 0, 2).reshape(-1, LANES)


def from_blocks(value, rows):
    return value.reshape(-1, rows, LANES).transpose(1, 0, 2).reshape(rows, -1)


def body(act_attn, dy_attn, act_exp, dy_exp, w_attn, m_attn, v_attn, w_exp, m_exp, v_exp):
    width = w_attn.shape[1]
    n_expert = lax.axis_size("expert")
    n_dp = lax.axis_size("dp")
    rows_a, rows_e = w_attn.shape[0], w_exp.shape[1]
    plan = Plan(n_expert, n_dp, rows_a, rows_e, width)
    total_params = width * (act_attn.shape[1] + n_expert * act_exp.shape[2])
    limit = 0.5 * math.sqrt(total_params)
    chips, chunk = plan.chips, plan.chunk
    state_a = [to_blocks(value) for value in (w_attn, m_attn, v_attn)]
    state_e = [to_blocks(value[0]) for value in (w_exp, m_exp, v_exp)]

    held = [pltpu.with_memory_space_constraint(x, pltpu.HBM) for x in (act_attn.T, dy_attn, act_exp[0].T, dy_exp[0])]
    full, send, pack = make_terms(plan, *held, *[pltpu.with_memory_space_constraint(x, pltpu.HBM) for x in state_a])
    got = swap_cores(send)
    sums = [
        full[c * chunk : (c + 1) * chunk] + got[c * chunk : (c + 1) * chunk].astype(f32) for c in range(chips)
    ]
    got = [swap(sums[c].astype(bf16), chips=c) for c in reversed(range(1, chips))]
    shared = ((plan.all_a + 16, LANES), bf16)
    packs = [pack, swap(pack, experts=1)]
    payload, g_exp, both = call(
        lambda *refs: share_kernel(plan, *refs),
        packs + [sums[0]] + got,
        [shared, ((plan.size_e, LANES), f32), ((2,) + pack.shape, bf16)],
    )
    distance = 1
    while 2 * distance < n_expert:
        other = swap(payload, experts=distance)
        (payload,) = call(lambda *refs: again_kernel(plan, *refs), [payload, other], [shared])
        distance *= 2
    other = swap(payload, experts=distance)
    far = []
    for step in (2**i for i in range(1, n_expert.bit_length() - 1)):
        far += [swap(value, experts=step) for value in packs + far]
    g_attn, square = call(
        lambda *refs: last_kernel(plan, *refs), [payload, other], [((plan.all_a, LANES), f32), ((8, LANES), f32)]
    )
    square = square + swap_cores(square)
    squares = [square] + [swap(square, chips=c) for c in square_order(chips)[1:]]
    block_a, block_e = ((plan.size_a, LANES), f32), ((plan.size_e, LANES), f32)
    (mine,) = call(
        lambda *refs: rows_kernel(plan, limit, *refs),
        [*squares, g_attn, g_exp, *state_e, both, *far],
        [((chunk, LANES), bf16)],
    )
    wa, ma, va, we, me, ve = call(
        lambda *refs: own_kernel(plan, limit, *refs),
        [*squares, g_attn, g_exp, *state_a, *state_e],
        [block_a] * 3 + [block_e] * 3,
    )
    near = [mine] + [swap(mine, chips=c) for c in reversed(range(1, chips))]
    far = [swap_cores(piece) for piece in near]
    attn_full, expert_full = put_in_order(plan, near + far)
    new_a = [from_blocks(value, rows_a) for value in (wa, ma, va)]
    new_e = [from_blocks(value, rows_e)[None] for value in (we, me, ve)]
    return (*new_a, *new_e, attn_full, expert_full)


def solution(mesh):
    return jax.shard_map(
        body,
        mesh=mesh,
        in_specs=(
            P(("expert", "dp"), None),
            P(("expert", "dp"), None),
            P("expert", "dp", None),
            P("expert", "dp", None),
            P(("expert", "dp"), None),
            P(("expert", "dp"), None),
            P(("expert", "dp"), None),
            P("expert", "dp", None),
            P("expert", "dp", None),
            P("expert", "dp", None),
        ),
        out_specs=(
            P(("expert", "dp"), None),
            P(("expert", "dp"), None),
            P(("expert", "dp"), None),
            P("expert", "dp", None),
            P("expert", "dp", None),
            P("expert", "dp", None),
            P(),
            P("expert", None, None),
        ),
        check_vma=False,
    )
```

```python
import math

import jax
import jax.numpy as jnp
from jax import lax
from jax.experimental import pallas as pl
from jax.experimental.pallas import tpu as pltpu
from jax.sharding import PartitionSpec as P

beta_first = 0.9
beta_second = 0.95
bias_first = 1.0 - 0.9**10
bias_second = 1.0 - 0.95**10
learn_rate = 0.01
decay_rate = 0.1
adam_eps = 1e-08

LANES = 128
f32, bf16 = jnp.float32, jnp.bfloat16


def adamw(grad, weight, moment, second, factor):
    scaled = factor * grad
    moment_new = beta_first * moment + (1.0 - beta_first) * scaled
    second_new = beta_second * second + (1.0 - beta_second) * scaled * scaled
    update = moment_new / bias_first / (jnp.sqrt(second_new / bias_second) + adam_eps)
    weight_new = weight - learn_rate * (update + decay_rate * weight)
    return (weight_new, moment_new, second_new)


def role_of(chip, core, expert):
    bits = chip ^ expert
    for shift in (4, 2, 1):
        bits = bits ^ (bits >> shift)
    return core ^ (bits & 1)


class Plan:
    def __init__(self, n_expert, n_dp, rows_a, rows_e, width):
        self.n_expert, self.n_dp, self.rows_a, self.rows_e = n_expert, n_dp, rows_a, rows_e
        self.width = width
        self.chips = n_dp // 2
        self.blocks = width // LANES
        self.size_a = self.blocks * rows_a
        self.size_e = self.blocks * rows_e
        self.all_a = n_expert * self.size_a
        self.chunk = self.all_a + self.size_e
        self.turned = n_dp == 8 and rows_a == 1

    def places(self, block):
        attn = [
            (e * self.rows_a + r, e * self.size_a + block * self.rows_a + r)
            for e in range(self.n_expert)
            for r in range(self.rows_a)
        ]
        exp = [(r, self.all_a + block * self.rows_e + r) for r in range(self.rows_e)]
        return attn, exp


def dot(left, right):
    return lax.dot_general(left, right, (((1,), (0,)), ((), ())), preferred_element_type=f32)


def size_of(shape, dtype):
    return math.prod(shape) * jnp.dtype(dtype).itemsize


def call(kernel, args, outs, scratch=(), in_space=pltpu.VMEM, out_space=pltpu.VMEM, copies=False):
    held = sum(size_of(arg.shape, arg.dtype) for arg in args if in_space is pltpu.VMEM)
    held += sum(size_of(*out) for out in outs) + sum(size_of(*buffer) for buffer in scratch)
    semaphores = [pltpu.SemaphoreType.DMA((16,))] if copies else []
    return pl.pallas_call(
        kernel,
        in_specs=[pl.BlockSpec(memory_space=in_space)] * len(args),
        out_specs=[pl.BlockSpec(memory_space=out_space)] * len(outs),
        out_shape=[jax.ShapeDtypeStruct(shape, dtype) for shape, dtype in outs],
        scratch_shapes=[pltpu.VMEM(*buffer) for buffer in scratch] + semaphores,
        compiler_params=pltpu.CompilerParams(vmem_limit_bytes=held + 4 * 1024 * 1024),
    )(*args)


def two_pieces(value):
    high = value.astype(bf16).astype(f32)
    return high, (value - high).astype(bf16).astype(f32)


def by_eights(value):
    return jnp.sum(value.reshape(-1, 8, LANES), axis=0)


STEPS = (4, 4, 4, 2, 2)


def each(count, step, unrolled):
    if unrolled:
        for i in range(count):
            step(i)
    else:
        pl.loop(0, count)(step)


def terms_kernel(plan, act_a, dy_a, act_e, dy_e, w, m, v, full, send, pack, act_a_v, dy_a_v, act_e_v, dy_e_v, state, sems):
    unit = plan.blocks // sum(STEPS)
    tiles = [(sum(STEPS[:t]) * unit, STEPS[t] * unit) for t in range(len(STEPS))]
    small = [
        pltpu.make_async_copy(act_a, act_a_v, sems.at[0]),
        pltpu.make_async_copy(act_e, act_e_v, sems.at[1]),
    ]
    big = []
    for t, (first, count) in enumerate(tiles):
        cols = pl.ds(first * LANES, count * LANES)
        big.append(pltpu.make_async_copy(dy_a.at[:, cols], dy_a_v.at[:, cols], sems.at[2 + 2 * t]))
        big.append(pltpu.make_async_copy(dy_e.at[:, cols], dy_e_v.at[:, cols], sems.at[3 + 2 * t]))
    extra = [pltpu.make_async_copy(ref, state.at[i], sems.at[2 + 2 * len(STEPS) + i]) for i, ref in enumerate((w, m, v))]
    for copy in small + big + extra:
        copy.start()

    me, me_ex = lax.axis_index("dp"), lax.axis_index("expert")
    my_role = role_of(me // 2, me % 2, me_ex)

    def pick(groups, per_owner, count, expert):
        shape = (groups * plan.n_dp, count)
        row = lax.broadcasted_iota(jnp.int32, shape, 0)
        col = lax.broadcasted_iota(jnp.int32, shape, 1)
        group, place = row // plan.n_dp, row % plan.n_dp
        chip, role = (place % plan.chips) ^ (me // 2), (place // plan.chips) ^ my_role
        if expert is None:
            expert, base = group // per_owner, (group // per_owner) * plan.n_dp
        else:
            base = 0
        owner = 2 * chip + role_of(chip, role, expert)
        want = (base + owner) * per_owner + group % per_owner
        return (want == col).astype(bf16)

    for copy in small:
        copy.wait()
    left_a = dot(pick(plan.n_expert * plan.rows_a, plan.rows_a, act_a.shape[0], None), act_a_v[...]).astype(bf16)
    left_e = dot(pick(plan.rows_e, plan.rows_e, act_e.shape[0], me_ex), act_e_v[...]).astype(bf16)
    n_dp = plan.n_dp
    for t, (first, count) in enumerate(tiles):
        cols = pl.ds(first * LANES, count * LANES)
        big[2 * t].wait()
        terms_a = dot(left_a, dy_a_v[:, cols])
        big[2 * t + 1].wait()
        terms_e = dot(left_e, dy_e_v[:, cols])
        for b in range(count):
            attn, exp = plan.places(first + b)
            span = slice(b * LANES, (b + 1) * LANES)
            for terms, places in ((terms_a, attn), (terms_e, exp)):
                for group, start in places:
                    full[pl.ds(start, n_dp, stride=plan.chunk), :] = terms[group * n_dp : (group + 1) * n_dp, span]
    for c in range(plan.chips):
        send[pl.ds(c * plan.chunk, plan.chunk), :] = full[
            pl.ds((plan.chips + c) * plan.chunk, plan.chunk), :
        ].astype(bf16)
    for copy in extra:
        copy.wait()
    size = plan.size_a
    for i in range(3):
        pack[pl.ds(i * size, size), :] = state[i].astype(bf16)


def make_terms(plan, act_a, dy_a, act_e, dy_e, w, m, v):
    args = (act_a, dy_a, act_e, dy_e, w, m, v)
    half = plan.chips * plan.chunk
    return call(
        lambda *refs: terms_kernel(plan, *refs),
        args,
        [((2 * half, LANES), f32), ((half, LANES), bf16), ((3 * plan.size_a, LANES), bf16)],
        [
            (act_a.shape, bf16),
            (dy_a.shape, bf16),
            (act_e.shape, bf16),
            (dy_e.shape, bf16),
            ((3,) + w.shape, f32),
        ],
        in_space=pltpu.HBM,
        copies=True,
    )


def share_kernel(plan, *refs):
    held, own, got, (payload, g_exp, both) = refs[:3], refs[3], refs[4:-3], refs[-3:]
    for i, pack in enumerate(held):
        both[i] = pack[...]
    total = own[...]
    for ref in got:
        total = total + ref[...].astype(f32)
    a = plan.all_a
    exp = total[a:]
    g_exp[...] = exp
    payload[:a, :] = total[:a].astype(bf16)
    payload[a:, :] = jnp.concatenate(two_pieces(by_eights(exp * exp)), axis=0).astype(bf16)


def pair_sum(plan, mine, other):
    a = plan.all_a
    attn = mine[:a, :].astype(f32) + other[:a, :].astype(f32)
    one, two = mine[a:, :].astype(f32), other[a:, :].astype(f32)
    return attn, (one[:8] + one[8:]) + (two[:8] + two[8:])


def again_kernel(plan, mine, other, payload):
    attn, square = pair_sum(plan, mine, other)
    a = plan.all_a
    payload[:a, :] = attn.astype(bf16)
    payload[a:, :] = jnp.concatenate(two_pieces(square), axis=0).astype(bf16)


def last_kernel(plan, mine, other, g_attn, square):
    attn, partial = pair_sum(plan, mine, other)
    g_attn[...] = attn
    square[...] = partial + by_eights(attn * attn)


def square_order(chips):
    return [0, *range(1, chips - 2), chips - 1, chips - 2]


def clip_factor(limit, squares):
    order = square_order(len(squares))
    values = [squares[order.index(c)][...] for c in range(len(squares))]
    while len(values) > 1:
        values = [values[i] + values[i + 1] for i in range(0, len(values), 2)]
    norm = jnp.sqrt(jnp.sum(values[0], keepdims=True))
    return jnp.minimum(1.0, limit / (norm + 1e-06))


def rows_kernel(plan, limit, *refs):
    factor = clip_factor(limit, refs[: plan.chips])
    g_attn, g_exp, we, me, ve, both, far, mine = refs[plan.chips :]
    size, place = plan.size_a, lax.axis_index("expert")
    for q, states in enumerate([both.at[0], both.at[1], both.at[2], far]):
        rows = pl.ds(pl.multiple_of((place ^ q) * size, 16), size)
        old = [states[pl.ds(i * size, size), :].astype(f32) for i in range(3)]
        weight, _, _ = adamw(g_attn[rows, :], *old, factor)
        mine[rows, :] = weight.astype(bf16)
    weight, _, _ = adamw(g_exp[...], we[...], me[...], ve[...], factor)
    mine[plan.all_a :, :] = weight.astype(bf16)


def own_kernel(plan, limit, *refs):
    factor = clip_factor(limit, refs[: plan.chips])
    g_attn, g_exp = refs[plan.chips : plan.chips + 2]
    state, new = refs[plan.chips + 2 : plan.chips + 8], refs[plan.chips + 8 :]
    rows = pl.ds(pl.multiple_of(lax.axis_index("expert") * plan.size_a, 16), plan.size_a)
    for b, grad in enumerate((g_attn[rows, :], g_exp[...])):
        values = adamw(grad, *[ref[...] for ref in state[3 * b : 3 * b + 3]], factor)
        for ref, value in zip(new[3 * b : 3 * b + 3], values):
            ref[...] = value


PARTS = 2


def order_kernel(plan, *refs):
    n_dp = plan.n_dp
    parts, (attn, exp, rows, rows_a, rows_e, attn_v, exp_v, sems) = refs[:n_dp], refs[n_dp:]
    me = lax.axis_index("dp")
    me_ex = lax.axis_index("expert")
    my_role = role_of(me // 2, me % 2, me_ex)
    for i, part in enumerate(parts):
        chip, role = (-i % plan.chips) ^ (me // 2), (i // plan.chips) ^ my_role
        blocks = [(e, e * plan.size_a, plan.size_a) for e in range(plan.n_expert)]
        for expert, start, size in blocks + [(me_ex, plan.all_a, plan.size_e)]:
            owner = 2 * chip + role_of(chip, role, expert)
            to = pl.multiple_of(owner * plan.chunk + start, 16)
            rows[pl.ds(to, size), :] = part[pl.ds(start, size), :].astype(f32)
    count_e = exp.shape[1]

    def lanes(b):
        return pl.ds(b * LANES if isinstance(b, int) else pl.multiple_of(b * LANES, LANES), LANES)

    def turn(part):
        for e in range(plan.n_expert):
            first = e * plan.size_a + part * count
            value = jnp.stack([rows[pl.ds(j * plan.chunk + first, count), :] for j in range(n_dp)])
            value = value.transpose(1, 0, 2)
            for b in range(count):
                rows_a[pl.ds(e * n_dp, n_dp), lanes(b)] = value[b]
        first = plan.all_a + part * count * plan.rows_e
        value = jnp.stack([rows[pl.ds(j * plan.chunk + first, count * plan.rows_e), :] for j in range(n_dp)])
        value = value.transpose(1, 0, 2)
        for b in range(count):
            for r in range(plan.rows_e):
                start = (part * count + b) * count_e + r
                rows_e[pl.ds(start, n_dp, stride=plan.rows_e), :] = value[b * plan.rows_e + r]
        attn_v[:, pl.ds(part * count * LANES, count * LANES)] = rows_a[...].astype(bf16)

    def gather(b):
        places_a, places_e = plan.places(b)
        values = [rows[pl.ds(start, n_dp, stride=plan.chunk), :] for _, start in places_a]
        if plan.rows_a == 1:
            attn_v[:, lanes(b)] = jnp.concatenate(values, axis=0).astype(bf16)
        else:
            for (group, _), value in zip(places_a, values):
                start = (group // plan.rows_a) * n_dp * plan.rows_a + group % plan.rows_a
                rows_a[pl.ds(start, n_dp, stride=plan.rows_a), :] = value
            attn_v[:, lanes(b)] = rows_a[...].astype(bf16)
        for r, start in places_e:
            rows_e[pl.ds(b * count_e + r, n_dp, stride=plan.rows_e), :] = rows[
                pl.ds(start, n_dp, stride=plan.chunk), :
            ]

    def finish(b):
        exp_v[:, lanes(b)] = rows_e[pl.ds(b * count_e, count_e), :].astype(bf16)

    copies = []
    count = plan.blocks // PARTS
    for part in range(PARTS):
        if plan.turned:
            turn(part)
        else:
            each(count, lambda b: gather(part * count + b), n_dp <= 8)
        each(count, lambda b: finish(part * count + b), True)
        cols = pl.ds(part * count * LANES, count * LANES)
        copies.append(pltpu.make_async_copy(attn_v.at[:, cols], attn.at[:, cols], sems.at[2 * part]))
        copies.append(pltpu.make_async_copy(exp_v.at[:, cols], exp.at[0, :, cols], sems.at[2 * part + 1]))
        for copy in copies[-2:]:
            copy.start()
    for copy in copies:
        copy.wait()


def put_in_order(plan, parts):
    count_a = plan.n_expert * plan.n_dp * plan.rows_a
    count_e = plan.n_dp * plan.rows_e
    return call(
        lambda *refs: order_kernel(plan, *refs),
        parts,
        [((count_a, plan.width), bf16), ((1, count_e, plan.width), bf16)],
        [
            ((plan.n_dp * plan.chunk, LANES), f32),
            ((count_a, plan.width // PARTS if plan.turned else LANES), f32),
            ((plan.blocks * count_e, LANES), f32),
            ((count_a, plan.width), bf16),
            ((count_e, plan.width), bf16),
        ],
        out_space=pltpu.HBM,
        copies=True,
    )


def swap(value, chips=0, experts=0):
    n_expert, n_dp = lax.axis_size("expert"), lax.axis_size("dp")
    pairs = []
    for e in range(n_expert):
        for j in range(n_dp):
            role = role_of(j // 2, j % 2, e)
            chip, expert = (j // 2) ^ chips, e ^ experts
            pairs.append((e * n_dp + j, expert * n_dp + 2 * chip + role_of(chip, role, expert)))
    return lax.ppermute(value, ("expert", "dp"), pairs)


def swap_cores(value):
    return lax.ppermute(value, "dp", [(i, i ^ 1) for i in range(lax.axis_size("dp"))])


def to_blocks(value):
    rows, width = value.shape
    return value.reshape(rows, width // LANES, LANES).transpose(1, 0, 2).reshape(-1, LANES)


def from_blocks(value, rows):
    return value.reshape(-1, rows, LANES).transpose(1, 0, 2).reshape(rows, -1)


def body(act_attn, dy_attn, act_exp, dy_exp, w_attn, m_attn, v_attn, w_exp, m_exp, v_exp):
    width = w_attn.shape[1]
    n_expert = lax.axis_size("expert")
    n_dp = lax.axis_size("dp")
    rows_a, rows_e = w_attn.shape[0], w_exp.shape[1]
    plan = Plan(n_expert, n_dp, rows_a, rows_e, width)
    total_params = width * (act_attn.shape[1] + n_expert * act_exp.shape[2])
    limit = 0.5 * math.sqrt(total_params)
    chips, chunk = plan.chips, plan.chunk
    state_a = [to_blocks(value) for value in (w_attn, m_attn, v_attn)]
    state_e = [to_blocks(value[0]) for value in (w_exp, m_exp, v_exp)]

    held = [pltpu.with_memory_space_constraint(x, pltpu.HBM) for x in (act_attn.T, dy_attn, act_exp[0].T, dy_exp[0])]
    full, send, pack = make_terms(plan, *held, *[pltpu.with_memory_space_constraint(x, pltpu.HBM) for x in state_a])
    got = swap_cores(send)
    sums = [
        full[c * chunk : (c + 1) * chunk] + got[c * chunk : (c + 1) * chunk].astype(f32) for c in range(chips)
    ]
    got = [swap(sums[c].astype(bf16), chips=c) for c in reversed(range(1, chips))]
    shared = ((plan.all_a + 16, LANES), bf16)
    packs = [pack, swap(pack, experts=1), swap(pack, experts=2)]
    payload, g_exp, both = call(
        lambda *refs: share_kernel(plan, *refs),
        packs + [sums[0]] + got,
        [shared, ((plan.size_e, LANES), f32), ((3,) + pack.shape, bf16)],
    )
    distance = 1
    while 2 * distance < n_expert:
        other = swap(payload, experts=distance)
        (payload,) = call(lambda *refs: again_kernel(plan, *refs), [payload, other], [shared])
        distance *= 2
    other = swap(payload, experts=distance)
    far = swap(packs[1], experts=2)
    g_attn, square = call(
        lambda *refs: last_kernel(plan, *refs), [payload, other], [((plan.all_a, LANES), f32), ((8, LANES), f32)]
    )
    square = square + swap_cores(square)
    squares = [square] + [swap(square, chips=c) for c in square_order(chips)[1:]]
    block_a, block_e = ((plan.size_a, LANES), f32), ((plan.size_e, LANES), f32)
    (mine,) = call(
        lambda *refs: rows_kernel(plan, limit, *refs),
        [*squares, g_attn, g_exp, *state_e, both, far],
        [((chunk, LANES), bf16)],
    )
    wa, ma, va, we, me, ve = call(
        lambda *refs: own_kernel(plan, limit, *refs),
        [*squares, g_attn, g_exp, *state_a, *state_e],
        [block_a] * 3 + [block_e] * 3,
    )
    near = [mine] + [swap(mine, chips=c) for c in reversed(range(1, chips))]
    far = [swap_cores(piece) for piece in near]
    attn_full, expert_full = put_in_order(plan, near + far)
    new_a = [from_blocks(value, rows_a) for value in (wa, ma, va)]
    new_e = [from_blocks(value, rows_e)[None] for value in (we, me, ve)]
    return (*new_a, *new_e, attn_full, expert_full)


def solution(mesh):
    return jax.shard_map(
        body,
        mesh=mesh,
        in_specs=(
            P(("expert", "dp"), None),
            P(("expert", "dp"), None),
            P("expert", "dp", None),
            P("expert", "dp", None),
            P(("expert", "dp"), None),
            P(("expert", "dp"), None),
            P(("expert", "dp"), None),
            P("expert", "dp", None),
            P("expert", "dp", None),
            P("expert", "dp", None),
        ),
        out_specs=(
            P(("expert", "dp"), None),
            P(("expert", "dp"), None),
            P(("expert", "dp"), None),
            P("expert", "dp", None),
            P("expert", "dp", None),
            P("expert", "dp", None),
            P(),
            P("expert", None, None),
        ),
        check_vma=False,
    )
```

```python
import math

import jax
import jax.numpy as jnp
from jax import lax
from jax.experimental import pallas as pl
from jax.experimental.pallas import tpu as pltpu
from jax.sharding import PartitionSpec as P

beta_first = 0.9
beta_second = 0.95
bias_first = 1.0 - 0.9**10
bias_second = 1.0 - 0.95**10
learn_rate = 0.01
decay_rate = 0.1
adam_eps = 1e-08

LANES = 128
f32, bf16 = jnp.float32, jnp.bfloat16


def adamw(grad, weight, moment, second, factor):
    scaled = factor * grad
    moment_new = beta_first * moment + (1.0 - beta_first) * scaled
    second_new = beta_second * second + (1.0 - beta_second) * scaled * scaled
    update = moment_new / bias_first / (jnp.sqrt(second_new / bias_second) + adam_eps)
    weight_new = weight - learn_rate * (update + decay_rate * weight)
    return (weight_new, moment_new, second_new)


def role_of(chip, core, expert):
    return core ^ ((chip ^ expert ^ (expert // 2)) % 2)


class Plan:
    def __init__(self, n_expert, n_dp, rows_a, rows_e, width):
        self.n_expert, self.n_dp, self.rows_a, self.rows_e = n_expert, n_dp, rows_a, rows_e
        self.width = width
        self.chips = n_dp // 2
        self.blocks = width // LANES
        self.size_a = self.blocks * rows_a
        self.size_e = self.blocks * rows_e
        self.all_a = n_expert * self.size_a
        self.chunk = self.all_a + self.size_e
        self.turned = n_dp == 8 and rows_a == 1

    def places(self, block):
        attn = [
            (e * self.rows_a + r, e * self.size_a + block * self.rows_a + r)
            for e in range(self.n_expert)
            for r in range(self.rows_a)
        ]
        exp = [(r, self.all_a + block * self.rows_e + r) for r in range(self.rows_e)]
        return attn, exp


def dot(left, right):
    return lax.dot_general(left, right, (((1,), (0,)), ((), ())), preferred_element_type=f32)


def size_of(shape, dtype):
    return math.prod(shape) * jnp.dtype(dtype).itemsize


def call(kernel, args, outs, scratch=(), in_space=pltpu.VMEM, out_space=pltpu.VMEM, copies=False):
    held = sum(size_of(arg.shape, arg.dtype) for arg in args if in_space is pltpu.VMEM)
    held += sum(size_of(*out) for out in outs) + sum(size_of(*buffer) for buffer in scratch)
    semaphores = [pltpu.SemaphoreType.DMA((16,))] if copies else []
    return pl.pallas_call(
        kernel,
        in_specs=[pl.BlockSpec(memory_space=in_space)] * len(args),
        out_specs=[pl.BlockSpec(memory_space=out_space)] * len(outs),
        out_shape=[jax.ShapeDtypeStruct(shape, dtype) for shape, dtype in outs],
        scratch_shapes=[pltpu.VMEM(*buffer) for buffer in scratch] + semaphores,
        compiler_params=pltpu.CompilerParams(vmem_limit_bytes=held + 4 * 1024 * 1024),
    )(*args)


def two_pieces(value):
    high = value.astype(bf16).astype(f32)
    return high, (value - high).astype(bf16).astype(f32)


def by_eights(value):
    return jnp.sum(value.reshape(-1, 8, LANES), axis=0)


STEPS = 3


def each(count, step, unrolled):
    if unrolled:
        for i in range(count):
            step(i)
    else:
        pl.loop(0, count)(step)


def terms_kernel(plan, act_a, dy_a, act_e, dy_e, w, m, v, full, send, pack, act_a_v, dy_a_v, act_e_v, dy_e_v, state, sems):
    tile = plan.width // STEPS
    small = [
        pltpu.make_async_copy(act_a, act_a_v, sems.at[0]),
        pltpu.make_async_copy(act_e, act_e_v, sems.at[1]),
    ]
    big = []
    for t in range(STEPS):
        cols = pl.ds(t * tile, tile)
        big.append(pltpu.make_async_copy(dy_a.at[:, cols], dy_a_v.at[:, cols], sems.at[2 + 2 * t]))
        big.append(pltpu.make_async_copy(dy_e.at[:, cols], dy_e_v.at[:, cols], sems.at[3 + 2 * t]))
    extra = [pltpu.make_async_copy(ref, state.at[i], sems.at[2 + 2 * STEPS + i]) for i, ref in enumerate((w, m, v))]
    for copy in small + big + extra:
        copy.start()

    me, me_ex = lax.axis_index("dp"), lax.axis_index("expert")
    my_role = role_of(me // 2, me % 2, me_ex)

    def pick(groups, per_owner, count, expert):
        shape = (groups * plan.n_dp, count)
        row = lax.broadcasted_iota(jnp.int32, shape, 0)
        col = lax.broadcasted_iota(jnp.int32, shape, 1)
        group, place = row // plan.n_dp, row % plan.n_dp
        chip, role = (place % plan.chips) ^ (me // 2), (place // plan.chips) ^ my_role
        if expert is None:
            expert, base = group // per_owner, (group // per_owner) * plan.n_dp
        else:
            base = 0
        owner = 2 * chip + role_of(chip, role, expert)
        want = (base + owner) * per_owner + group % per_owner
        return (want == col).astype(bf16)

    for copy in small:
        copy.wait()
    left_a = dot(pick(plan.n_expert * plan.rows_a, plan.rows_a, act_a.shape[0], None), act_a_v[...]).astype(bf16)
    left_e = dot(pick(plan.rows_e, plan.rows_e, act_e.shape[0], me_ex), act_e_v[...]).astype(bf16)
    n_dp = plan.n_dp

    def turn(start, pieces):
        value = jnp.stack(pieces).transpose(1, 0, 2)
        for c in range(plan.chips):
            rows = pl.ds(c * plan.chunk + start, len(pieces))
            full[rows, :] = value[c]
            send[rows, :] = value[plan.chips + c].astype(bf16)

    for t in range(STEPS):
        cols = pl.ds(t * tile, tile)
        big[2 * t].wait()
        terms_a = dot(left_a, dy_a_v[:, cols])
        big[2 * t + 1].wait()
        terms_e = dot(left_e, dy_e_v[:, cols])
        count = tile // LANES
        if plan.turned:
            blocks = [slice(b * LANES, (b + 1) * LANES) for b in range(count)]
            for e in range(plan.n_expert):
                turn(e * plan.size_a + t * count, [terms_a[e * n_dp : (e + 1) * n_dp, span] for span in blocks])
            pieces = [
                terms_e[r * n_dp : (r + 1) * n_dp, span] for span in blocks for r in range(plan.rows_e)
            ]
            turn(plan.all_a + t * count * plan.rows_e, pieces)
            continue
        for b in range(count):
            attn, exp = plan.places(t * count + b)
            span = slice(b * LANES, (b + 1) * LANES)
            for terms, places in ((terms_a, attn), (terms_e, exp)):
                for group, start in places:
                    full[pl.ds(start, n_dp, stride=plan.chunk), :] = terms[group * n_dp : (group + 1) * n_dp, span]
    for c in range(0 if plan.turned else plan.chips):
        send[pl.ds(c * plan.chunk, plan.chunk), :] = full[
            pl.ds((plan.chips + c) * plan.chunk, plan.chunk), :
        ].astype(bf16)
    for copy in extra:
        copy.wait()
    size = plan.size_a
    for i in range(3):
        pack[pl.ds(i * size, size), :] = state[i].astype(bf16)


def make_terms(plan, act_a, dy_a, act_e, dy_e, w, m, v):
    args = (act_a, dy_a, act_e, dy_e, w, m, v)
    half = plan.chips * plan.chunk
    return call(
        lambda *refs: terms_kernel(plan, *refs),
        args,
        [((half if plan.turned else 2 * half, LANES), f32), ((half, LANES), bf16), ((3 * plan.size_a, LANES), bf16)],
        [
            (act_a.shape, bf16),
            (dy_a.shape, bf16),
            (act_e.shape, bf16),
            (dy_e.shape, bf16),
            ((3,) + w.shape, f32),
        ],
        in_space=pltpu.HBM,
        copies=True,
    )


def share_kernel(plan, *refs):
    held, far, own, got, (payload, g_exp, both) = *refs[:3], refs[3:-3], refs[-3:]
    both[0], both[1] = held[...], far[...]
    total = own[...]
    for ref in got:
        total = total + ref[...].astype(f32)
    a = plan.all_a
    exp = total[a:]
    g_exp[...] = exp
    payload[:a, :] = total[:a].astype(bf16)
    payload[a:, :] = jnp.concatenate(two_pieces(by_eights(exp * exp)), axis=0).astype(bf16)


def pair_sum(plan, mine, other):
    a = plan.all_a
    attn = mine[:a, :].astype(f32) + other[:a, :].astype(f32)
    one, two = mine[a:, :].astype(f32), other[a:, :].astype(f32)
    return attn, (one[:8] + one[8:]) + (two[:8] + two[8:])


def again_kernel(plan, mine, other, payload):
    attn, square = pair_sum(plan, mine, other)
    a = plan.all_a
    payload[:a, :] = attn.astype(bf16)
    payload[a:, :] = jnp.concatenate(two_pieces(square), axis=0).astype(bf16)


def last_kernel(plan, mine, other, g_attn, square):
    attn, partial = pair_sum(plan, mine, other)
    g_attn[...] = attn
    square[...] = partial + by_eights(attn * attn)


def square_order(chips):
    return [0, *reversed(range(1, chips - 1)), chips - 1]


def clip_factor(limit, squares):
    order = square_order(len(squares))
    values = [squares[order.index(c)][...] for c in range(len(squares))]
    while len(values) > 1:
        values = [values[i] + values[i + 1] for i in range(0, len(values), 2)]
    norm = jnp.sqrt(jnp.sum(values[0], keepdims=True))
    return jnp.minimum(1.0, limit / (norm + 1e-06))


def rows_kernel(plan, limit, *refs):
    factor = clip_factor(limit, refs[: plan.chips])
    g_attn, g_exp, we, me, ve, both, *far, mine = refs[plan.chips :]
    size, place = plan.size_a, lax.axis_index("expert")
    for q, states in enumerate([both.at[0], both.at[1], *far]):
        rows = pl.ds(pl.multiple_of((place ^ q) * size, 16), size)
        old = [states[pl.ds(i * size, size), :].astype(f32) for i in range(3)]
        weight, _, _ = adamw(g_attn[rows, :], *old, factor)
        mine[rows, :] = weight.astype(bf16)
    weight, _, _ = adamw(g_exp[...], we[...], me[...], ve[...], factor)
    mine[plan.all_a :, :] = weight.astype(bf16)


def own_kernel(plan, limit, *refs):
    factor = clip_factor(limit, refs[: plan.chips])
    g_attn, g_exp = refs[plan.chips : plan.chips + 2]
    state, new = refs[plan.chips + 2 : plan.chips + 8], refs[plan.chips + 8 :]
    rows = pl.ds(pl.multiple_of(lax.axis_index("expert") * plan.size_a, 16), plan.size_a)
    for b, grad in enumerate((g_attn[rows, :], g_exp[...])):
        values = adamw(grad, *[ref[...] for ref in state[3 * b : 3 * b + 3]], factor)
        for ref, value in zip(new[3 * b : 3 * b + 3], values):
            ref[...] = value


PARTS = 2


def order_kernel(plan, *refs):
    n_dp = plan.n_dp
    parts, (attn, exp, rows, rows_a, rows_e, attn_v, exp_v, sems) = refs[:n_dp], refs[n_dp:]
    me = lax.axis_index("dp")
    me_ex = lax.axis_index("expert")
    my_role = role_of(me // 2, me % 2, me_ex)
    for i, part in enumerate(parts):
        chip, role = (i % plan.chips) ^ (me // 2), (i // plan.chips) ^ my_role
        blocks = [(e, e * plan.size_a, plan.size_a) for e in range(plan.n_expert)]
        for expert, start, size in blocks + [(me_ex, plan.all_a, plan.size_e)]:
            owner = 2 * chip + role_of(chip, role, expert)
            to = pl.multiple_of(owner * plan.chunk + start, 16)
            rows[pl.ds(to, size), :] = part[pl.ds(start, size), :].astype(f32)
    count_e = exp.shape[1]

    def lanes(b):
        return pl.ds(b * LANES if isinstance(b, int) else pl.multiple_of(b * LANES, LANES), LANES)

    def turn(part):
        for e in range(plan.n_expert):
            first = e * plan.size_a + part * count
            value = jnp.stack([rows[pl.ds(j * plan.chunk + first, count), :] for j in range(n_dp)])
            value = value.transpose(1, 0, 2)
            for b in range(count):
                rows_a[pl.ds(e * n_dp, n_dp), lanes(b)] = value[b]
        first = plan.all_a + part * count * plan.rows_e
        value = jnp.stack([rows[pl.ds(j * plan.chunk + first, count * plan.rows_e), :] for j in range(n_dp)])
        value = value.transpose(1, 0, 2)
        for b in range(count):
            for r in range(plan.rows_e):
                start = (part * count + b) * count_e + r
                rows_e[pl.ds(start, n_dp, stride=plan.rows_e), :] = value[b * plan.rows_e + r]
        attn_v[:, pl.ds(part * count * LANES, count * LANES)] = rows_a[...].astype(bf16)

    def gather(b):
        places_a, places_e = plan.places(b)
        values = [rows[pl.ds(start, n_dp, stride=plan.chunk), :] for _, start in places_a]
        if plan.rows_a == 1:
            attn_v[:, lanes(b)] = jnp.concatenate(values, axis=0).astype(bf16)
        else:
            for (group, _), value in zip(places_a, values):
                start = (group // plan.rows_a) * n_dp * plan.rows_a + group % plan.rows_a
                rows_a[pl.ds(start, n_dp, stride=plan.rows_a), :] = value
            attn_v[:, lanes(b)] = rows_a[...].astype(bf16)
        for r, start in places_e:
            rows_e[pl.ds(b * count_e + r, n_dp, stride=plan.rows_e), :] = rows[
                pl.ds(start, n_dp, stride=plan.chunk), :
            ]

    def finish(b):
        exp_v[:, lanes(b)] = rows_e[pl.ds(b * count_e, count_e), :].astype(bf16)

    copies = []
    count = plan.blocks // PARTS
    for part in range(PARTS):
        if plan.turned:
            turn(part)
        else:
            each(count, lambda b: gather(part * count + b), n_dp <= 8)
        each(count, lambda b: finish(part * count + b), True)
        cols = pl.ds(part * count * LANES, count * LANES)
        copies.append(pltpu.make_async_copy(attn_v.at[:, cols], attn.at[:, cols], sems.at[2 * part]))
        copies.append(pltpu.make_async_copy(exp_v.at[:, cols], exp.at[0, :, cols], sems.at[2 * part + 1]))
        for copy in copies[-2:]:
            copy.start()
    for copy in copies:
        copy.wait()


def put_in_order(plan, parts):
    count_a = plan.n_expert * plan.n_dp * plan.rows_a
    count_e = plan.n_dp * plan.rows_e
    return call(
        lambda *refs: order_kernel(plan, *refs),
        parts,
        [((count_a, plan.width), bf16), ((1, count_e, plan.width), bf16)],
        [
            ((plan.n_dp * plan.chunk, LANES), f32),
            ((count_a, plan.width // PARTS if plan.turned else LANES), f32),
            ((plan.blocks * count_e, LANES), f32),
            ((count_a, plan.width), bf16),
            ((count_e, plan.width), bf16),
        ],
        out_space=pltpu.HBM,
        copies=True,
    )


def swap(value, chips=0, experts=0):
    n_expert, n_dp = lax.axis_size("expert"), lax.axis_size("dp")
    pairs = []
    for e in range(n_expert):
        for j in range(n_dp):
            role = role_of(j // 2, j % 2, e)
            chip, expert = (j // 2) ^ chips, e ^ experts
            pairs.append((e * n_dp + j, expert * n_dp + 2 * chip + role_of(chip, role, expert)))
    return lax.ppermute(value, ("expert", "dp"), pairs)


def swap_cores(value):
    return lax.ppermute(value, "dp", [(i, i ^ 1) for i in range(lax.axis_size("dp"))])


def to_blocks(value):
    rows, width = value.shape
    return value.reshape(rows, width // LANES, LANES).transpose(1, 0, 2).reshape(-1, LANES)


def from_blocks(value, rows):
    return value.reshape(-1, rows, LANES).transpose(1, 0, 2).reshape(rows, -1)


def body(act_attn, dy_attn, act_exp, dy_exp, w_attn, m_attn, v_attn, w_exp, m_exp, v_exp):
    width = w_attn.shape[1]
    n_expert = lax.axis_size("expert")
    n_dp = lax.axis_size("dp")
    rows_a, rows_e = w_attn.shape[0], w_exp.shape[1]
    plan = Plan(n_expert, n_dp, rows_a, rows_e, width)
    total_params = width * (act_attn.shape[1] + n_expert * act_exp.shape[2])
    limit = 0.5 * math.sqrt(total_params)
    chips, chunk = plan.chips, plan.chunk
    state_a = [to_blocks(value) for value in (w_attn, m_attn, v_attn)]
    state_e = [to_blocks(value[0]) for value in (w_exp, m_exp, v_exp)]

    held = [pltpu.with_memory_space_constraint(x, pltpu.HBM) for x in (act_attn.T, dy_attn, act_exp[0].T, dy_exp[0])]
    full, send, pack = make_terms(plan, *held, *[pltpu.with_memory_space_constraint(x, pltpu.HBM) for x in state_a])
    got = swap_cores(send)
    sums = [
        full[c * chunk : (c + 1) * chunk] + got[c * chunk : (c + 1) * chunk].astype(f32) for c in range(chips)
    ]
    got = [swap(sums[c].astype(bf16), chips=c) for c in reversed(range(1, chips))]
    shared = ((plan.all_a + 16, LANES), bf16)
    packs = [pack, swap(pack, experts=1)]
    payload, g_exp, both = call(
        lambda *refs: share_kernel(plan, *refs),
        packs + [sums[0]] + got,
        [shared, ((plan.size_e, LANES), f32), ((2,) + pack.shape, bf16)],
    )
    distance = 1
    while 2 * distance < n_expert:
        other = swap(payload, experts=distance)
        (payload,) = call(lambda *refs: again_kernel(plan, *refs), [payload, other], [shared])
        distance *= 2
    other = swap(payload, experts=distance)
    far = [swap(pack, experts=q) for q in range(2, n_expert)]
    g_attn, square = call(
        lambda *refs: last_kernel(plan, *refs), [payload, other], [((plan.all_a, LANES), f32), ((8, LANES), f32)]
    )
    square = square + swap_cores(square)
    squares = [square] + [swap(square, chips=c) for c in square_order(chips)[1:]]
    block_a, block_e = ((plan.size_a, LANES), f32), ((plan.size_e, LANES), f32)
    (mine,) = call(
        lambda *refs: rows_kernel(plan, limit, *refs),
        [*squares, g_attn, g_exp, *state_e, both, *far],
        [((chunk, LANES), bf16)],
    )
    wa, ma, va, we, me, ve = call(
        lambda *refs: own_kernel(plan, limit, *refs),
        [*squares, g_attn, g_exp, *state_a, *state_e],
        [block_a] * 3 + [block_e] * 3,
    )
    near = [mine] + [swap(mine, chips=c) for c in range(1, chips)]
    far = [swap_cores(piece) for piece in near]
    attn_full, expert_full = put_in_order(plan, near + far)
    new_a = [from_blocks(value, rows_a) for value in (wa, ma, va)]
    new_e = [from_blocks(value, rows_e)[None] for value in (we, me, ve)]
    return (*new_a, *new_e, attn_full, expert_full)


def solution(mesh):
    return jax.shard_map(
        body,
        mesh=mesh,
        in_specs=(
            P(("expert", "dp"), None),
            P(("expert", "dp"), None),
            P("expert", "dp", None),
            P("expert", "dp", None),
            P(("expert", "dp"), None),
            P(("expert", "dp"), None),
            P(("expert", "dp"), None),
            P("expert", "dp", None),
            P("expert", "dp", None),
            P("expert", "dp", None),
        ),
        out_specs=(
            P(("expert", "dp"), None),
            P(("expert", "dp"), None),
            P(("expert", "dp"), None),
            P("expert", "dp", None),
            P("expert", "dp", None),
            P("expert", "dp", None),
            P(),
            P("expert", None, None),
        ),
        check_vma=False,
    )
```

```python
import math

import jax
import jax.numpy as jnp
from jax import lax
from jax.experimental import pallas as pl
from jax.experimental.pallas import tpu as pltpu
from jax.sharding import PartitionSpec as P

beta_first = 0.9
beta_second = 0.95
bias_first = 1.0 - 0.9**10
bias_second = 1.0 - 0.95**10
learn_rate = 0.01
decay_rate = 0.1
adam_eps = 1e-08

LANES = 128
f32, bf16 = jnp.float32, jnp.bfloat16


def adamw(grad, weight, moment, second, factor):
    scaled = factor * grad
    moment_new = beta_first * moment + (1.0 - beta_first) * scaled
    second_new = beta_second * second + (1.0 - beta_second) * scaled * scaled
    update = moment_new / bias_first / (jnp.sqrt(second_new / bias_second) + adam_eps)
    weight_new = weight - learn_rate * (update + decay_rate * weight)
    return (weight_new, moment_new, second_new)


def role_of(chip, core, expert):
    return core ^ ((chip ^ expert ^ (expert // 2)) % 2)


class Plan:
    def __init__(self, n_expert, n_dp, rows_a, rows_e, width):
        self.n_expert, self.n_dp, self.rows_a, self.rows_e = n_expert, n_dp, rows_a, rows_e
        self.width = width
        self.chips = n_dp // 2
        self.blocks = width // LANES
        self.size_a = self.blocks * rows_a
        self.size_e = self.blocks * rows_e
        self.all_a = n_expert * self.size_a
        self.chunk = self.all_a + self.size_e
        self.turned = n_dp == 8 and rows_a == 1

    def places(self, block):
        attn = [
            (e * self.rows_a + r, e * self.size_a + block * self.rows_a + r)
            for e in range(self.n_expert)
            for r in range(self.rows_a)
        ]
        exp = [(r, self.all_a + block * self.rows_e + r) for r in range(self.rows_e)]
        return attn, exp


def dot(left, right):
    return lax.dot_general(left, right, (((1,), (0,)), ((), ())), preferred_element_type=f32)


def size_of(shape, dtype):
    return math.prod(shape) * jnp.dtype(dtype).itemsize


def call(kernel, args, outs, scratch=(), in_space=pltpu.VMEM, out_space=pltpu.VMEM, copies=False):
    held = sum(size_of(arg.shape, arg.dtype) for arg in args if in_space is pltpu.VMEM)
    held += sum(size_of(*out) for out in outs) + sum(size_of(*buffer) for buffer in scratch)
    semaphores = [pltpu.SemaphoreType.DMA((16,))] if copies else []
    return pl.pallas_call(
        kernel,
        in_specs=[pl.BlockSpec(memory_space=in_space)] * len(args),
        out_specs=[pl.BlockSpec(memory_space=out_space)] * len(outs),
        out_shape=[jax.ShapeDtypeStruct(shape, dtype) for shape, dtype in outs],
        scratch_shapes=[pltpu.VMEM(*buffer) for buffer in scratch] + semaphores,
        compiler_params=pltpu.CompilerParams(vmem_limit_bytes=held + 4 * 1024 * 1024),
    )(*args)


def two_pieces(value):
    high = value.astype(bf16).astype(f32)
    return high, (value - high).astype(bf16).astype(f32)


def by_eights(value):
    return jnp.sum(value.reshape(-1, 8, LANES), axis=0)


STEPS = 2


def each(count, step, unrolled):
    if unrolled:
        for i in range(count):
            step(i)
    else:
        pl.loop(0, count)(step)


def terms_kernel(plan, act_a, dy_a, act_e, dy_e, w, m, v, full, send, pack, act_a_v, dy_a_v, act_e_v, dy_e_v, state, sems):
    tile = plan.width // STEPS
    small = [
        pltpu.make_async_copy(act_a, act_a_v, sems.at[0]),
        pltpu.make_async_copy(act_e, act_e_v, sems.at[1]),
    ]
    big = []
    for t in range(STEPS):
        cols = pl.ds(t * tile, tile)
        big.append(pltpu.make_async_copy(dy_a.at[:, cols], dy_a_v.at[:, cols], sems.at[2 + 2 * t]))
        big.append(pltpu.make_async_copy(dy_e.at[:, cols], dy_e_v.at[:, cols], sems.at[3 + 2 * t]))
    extra = [pltpu.make_async_copy(ref, state.at[i], sems.at[2 + 2 * STEPS + i]) for i, ref in enumerate((w, m, v))]
    for copy in small + big + extra:
        copy.start()

    me, me_ex = lax.axis_index("dp"), lax.axis_index("expert")
    my_role = role_of(me // 2, me % 2, me_ex)

    def pick(groups, per_owner, count, expert):
        shape = (groups * plan.n_dp, count)
        row = lax.broadcasted_iota(jnp.int32, shape, 0)
        col = lax.broadcasted_iota(jnp.int32, shape, 1)
        group, place = row // plan.n_dp, row % plan.n_dp
        chip, role = (place % plan.chips) ^ (me // 2), (place // plan.chips) ^ my_role
        if expert is None:
            expert, base = group // per_owner, (group // per_owner) * plan.n_dp
        else:
            base = 0
        owner = 2 * chip + role_of(chip, role, expert)
        want = (base + owner) * per_owner + group % per_owner
        return (want == col).astype(bf16)

    for copy in small:
        copy.wait()
    left_a = dot(pick(plan.n_expert * plan.rows_a, plan.rows_a, act_a.shape[0], None), act_a_v[...]).astype(bf16)
    left_e = dot(pick(plan.rows_e, plan.rows_e, act_e.shape[0], me_ex), act_e_v[...]).astype(bf16)
    n_dp = plan.n_dp

    def turn(start, pieces):
        value = jnp.stack(pieces).transpose(1, 0, 2)
        for c in range(plan.chips):
            rows = pl.ds(c * plan.chunk + start, len(pieces))
            full[rows, :] = value[c]
            send[rows, :] = value[plan.chips + c].astype(bf16)

    for t in range(STEPS):
        cols = pl.ds(t * tile, tile)
        big[2 * t].wait()
        terms_a = dot(left_a, dy_a_v[:, cols])
        big[2 * t + 1].wait()
        terms_e = dot(left_e, dy_e_v[:, cols])
        count = tile // LANES
        if plan.turned:
            blocks = [slice(b * LANES, (b + 1) * LANES) for b in range(count)]
            for e in range(plan.n_expert):
                turn(e * plan.size_a + t * count, [terms_a[e * n_dp : (e + 1) * n_dp, span] for span in blocks])
            pieces = [
                terms_e[r * n_dp : (r + 1) * n_dp, span] for span in blocks for r in range(plan.rows_e)
            ]
            turn(plan.all_a + t * count * plan.rows_e, pieces)
            continue
        for b in range(count):
            attn, exp = plan.places(t * count + b)
            span = slice(b * LANES, (b + 1) * LANES)
            for terms, places in ((terms_a, attn), (terms_e, exp)):
                for group, start in places:
                    full[pl.ds(start, n_dp, stride=plan.chunk), :] = terms[group * n_dp : (group + 1) * n_dp, span]
    for c in range(0 if plan.turned else plan.chips):
        send[pl.ds(c * plan.chunk, plan.chunk), :] = full[
            pl.ds((plan.chips + c) * plan.chunk, plan.chunk), :
        ].astype(bf16)
    for copy in extra:
        copy.wait()
    size = plan.size_a
    for i in range(3):
        pack[pl.ds(i * size, size), :] = state[i].astype(bf16)


def make_terms(plan, act_a, dy_a, act_e, dy_e, w, m, v):
    args = (act_a, dy_a, act_e, dy_e, w, m, v)
    half = plan.chips * plan.chunk
    return call(
        lambda *refs: terms_kernel(plan, *refs),
        args,
        [((half if plan.turned else 2 * half, LANES), f32), ((half, LANES), bf16), ((3 * plan.size_a, LANES), bf16)],
        [
            (act_a.shape, bf16),
            (dy_a.shape, bf16),
            (act_e.shape, bf16),
            (dy_e.shape, bf16),
            ((3,) + w.shape, f32),
        ],
        in_space=pltpu.HBM,
        copies=True,
    )


def share_kernel(plan, *refs):
    own, got, (payload, g_exp) = refs[0], refs[1:-2], refs[-2:]
    total = own[...]
    for ref in got:
        total = total + ref[...].astype(f32)
    a = plan.all_a
    exp = total[a:]
    g_exp[...] = exp
    payload[:a, :] = total[:a].astype(bf16)
    payload[a:, :] = jnp.concatenate(two_pieces(by_eights(exp * exp)), axis=0).astype(bf16)


def pair_sum(plan, mine, other):
    a = plan.all_a
    attn = mine[:a, :].astype(f32) + other[:a, :].astype(f32)
    one, two = mine[a:, :].astype(f32), other[a:, :].astype(f32)
    return attn, (one[:8] + one[8:]) + (two[:8] + two[8:])


def again_kernel(plan, mine, other, pack, payload, held):
    held[...] = pack[...]
    attn, square = pair_sum(plan, mine, other)
    a = plan.all_a
    payload[:a, :] = attn.astype(bf16)
    payload[a:, :] = jnp.concatenate(two_pieces(square), axis=0).astype(bf16)


def last_kernel(plan, mine, other, g_attn, square):
    attn, partial = pair_sum(plan, mine, other)
    g_attn[...] = attn
    square[...] = partial + by_eights(attn * attn)


def square_order(chips):
    return [0, *reversed(range(1, chips - 1)), chips - 1]


def clip_factor(limit, squares):
    order = square_order(len(squares))
    values = [squares[order.index(c)][...] for c in range(len(squares))]
    while len(values) > 1:
        values = [values[i] + values[i + 1] for i in range(0, len(values), 2)]
    norm = jnp.sqrt(jnp.sum(values[0], keepdims=True))
    return jnp.minimum(1.0, limit / (norm + 1e-06))


def rows_kernel(plan, limit, *refs):
    factor = clip_factor(limit, refs[: plan.chips])
    g_attn, g_exp, we, me, ve, *packs, mine = refs[plan.chips :]
    size, place = plan.size_a, lax.axis_index("expert")
    half = len(packs) // 2
    for i, states in enumerate(packs):
        q = 2 * (i % half) + i // half
        rows = pl.ds(pl.multiple_of((place ^ q) * size, 16), size)
        old = [states[pl.ds(i * size, size), :].astype(f32) for i in range(3)]
        weight, _, _ = adamw(g_attn[rows, :], *old, factor)
        mine[rows, :] = weight.astype(bf16)
    weight, _, _ = adamw(g_exp[...], we[...], me[...], ve[...], factor)
    mine[plan.all_a :, :] = weight.astype(bf16)


def own_kernel(plan, limit, *refs):
    factor = clip_factor(limit, refs[: plan.chips])
    g_attn, g_exp = refs[plan.chips : plan.chips + 2]
    state, new = refs[plan.chips + 2 : plan.chips + 8], refs[plan.chips + 8 :]
    rows = pl.ds(pl.multiple_of(lax.axis_index("expert") * plan.size_a, 16), plan.size_a)
    for b, grad in enumerate((g_attn[rows, :], g_exp[...])):
        values = adamw(grad, *[ref[...] for ref in state[3 * b : 3 * b + 3]], factor)
        for ref, value in zip(new[3 * b : 3 * b + 3], values):
            ref[...] = value


PARTS = 2


def order_kernel(plan, *refs):
    n_dp = plan.n_dp
    parts, (attn, exp, rows, rows_a, rows_e, attn_v, exp_v, sems) = refs[:n_dp], refs[n_dp:]
    me = lax.axis_index("dp")
    me_ex = lax.axis_index("expert")
    my_role = role_of(me // 2, me % 2, me_ex)
    for i, part in enumerate(parts):
        chip, role = (i % plan.chips) ^ (me // 2), (i // plan.chips) ^ my_role
        blocks = [(e, e * plan.size_a, plan.size_a) for e in range(plan.n_expert)]
        for expert, start, size in blocks + [(me_ex, plan.all_a, plan.size_e)]:
            owner = 2 * chip + role_of(chip, role, expert)
            to = pl.multiple_of(owner * plan.chunk + start, 16)
            rows[pl.ds(to, size), :] = part[pl.ds(start, size), :].astype(f32)
    count_e = exp.shape[1]

    def lanes(b):
        return pl.ds(b * LANES if isinstance(b, int) else pl.multiple_of(b * LANES, LANES), LANES)

    def turn(part):
        for e in range(plan.n_expert):
            first = e * plan.size_a + part * count
            value = jnp.stack([rows[pl.ds(j * plan.chunk + first, count), :] for j in range(n_dp)])
            value = value.transpose(1, 0, 2)
            for b in range(count):
                rows_a[pl.ds(e * n_dp, n_dp), lanes(b)] = value[b]
        first = plan.all_a + part * count * plan.rows_e
        value = jnp.stack([rows[pl.ds(j * plan.chunk + first, count * plan.rows_e), :] for j in range(n_dp)])
        value = value.transpose(1, 0, 2)
        for b in range(count):
            for r in range(plan.rows_e):
                start = (part * count + b) * count_e + r
                rows_e[pl.ds(start, n_dp, stride=plan.rows_e), :] = value[b * plan.rows_e + r]
        attn_v[:, pl.ds(part * count * LANES, count * LANES)] = rows_a[...].astype(bf16)

    def gather(b):
        places_a, places_e = plan.places(b)
        values = [rows[pl.ds(start, n_dp, stride=plan.chunk), :] for _, start in places_a]
        if plan.rows_a == 1:
            attn_v[:, lanes(b)] = jnp.concatenate(values, axis=0).astype(bf16)
        else:
            for (group, _), value in zip(places_a, values):
                start = (group // plan.rows_a) * n_dp * plan.rows_a + group % plan.rows_a
                rows_a[pl.ds(start, n_dp, stride=plan.rows_a), :] = value
            attn_v[:, lanes(b)] = rows_a[...].astype(bf16)
        for r, start in places_e:
            rows_e[pl.ds(b * count_e + r, n_dp, stride=plan.rows_e), :] = rows[
                pl.ds(start, n_dp, stride=plan.chunk), :
            ]

    def finish(b):
        exp_v[:, lanes(b)] = rows_e[pl.ds(b * count_e, count_e), :].astype(bf16)

    copies = []
    count = plan.blocks // PARTS
    for part in range(PARTS):
        if plan.turned:
            turn(part)
        else:
            each(count, lambda b: gather(part * count + b), n_dp <= 8)
        each(count, lambda b: finish(part * count + b), True)
        cols = pl.ds(part * count * LANES, count * LANES)
        copies.append(pltpu.make_async_copy(attn_v.at[:, cols], attn.at[:, cols], sems.at[2 * part]))
        copies.append(pltpu.make_async_copy(exp_v.at[:, cols], exp.at[0, :, cols], sems.at[2 * part + 1]))
        for copy in copies[-2:]:
            copy.start()
    for copy in copies:
        copy.wait()


def put_in_order(plan, parts):
    count_a = plan.n_expert * plan.n_dp * plan.rows_a
    count_e = plan.n_dp * plan.rows_e
    return call(
        lambda *refs: order_kernel(plan, *refs),
        parts,
        [((count_a, plan.width), bf16), ((1, count_e, plan.width), bf16)],
        [
            ((plan.n_dp * plan.chunk, LANES), f32),
            ((count_a, plan.width // PARTS if plan.turned else LANES), f32),
            ((plan.blocks * count_e, LANES), f32),
            ((count_a, plan.width), bf16),
            ((count_e, plan.width), bf16),
        ],
        out_space=pltpu.HBM,
        copies=True,
    )


def swap(value, chips=0, experts=0):
    n_expert, n_dp = lax.axis_size("expert"), lax.axis_size("dp")
    pairs = []
    for e in range(n_expert):
        for j in range(n_dp):
            role = role_of(j // 2, j % 2, e)
            chip, expert = (j // 2) ^ chips, e ^ experts
            pairs.append((e * n_dp + j, expert * n_dp + 2 * chip + role_of(chip, role, expert)))
    return lax.ppermute(value, ("expert", "dp"), pairs)


def swap_cores(value):
    return lax.ppermute(value, "dp", [(i, i ^ 1) for i in range(lax.axis_size("dp"))])


def to_blocks(value):
    rows, width = value.shape
    return value.reshape(rows, width // LANES, LANES).transpose(1, 0, 2).reshape(-1, LANES)


def from_blocks(value, rows):
    return value.reshape(-1, rows, LANES).transpose(1, 0, 2).reshape(rows, -1)


def body(act_attn, dy_attn, act_exp, dy_exp, w_attn, m_attn, v_attn, w_exp, m_exp, v_exp):
    width = w_attn.shape[1]
    n_expert = lax.axis_size("expert")
    n_dp = lax.axis_size("dp")
    rows_a, rows_e = w_attn.shape[0], w_exp.shape[1]
    plan = Plan(n_expert, n_dp, rows_a, rows_e, width)
    total_params = width * (act_attn.shape[1] + n_expert * act_exp.shape[2])
    limit = 0.5 * math.sqrt(total_params)
    chips, chunk = plan.chips, plan.chunk
    state_a = [to_blocks(value) for value in (w_attn, m_attn, v_attn)]
    state_e = [to_blocks(value[0]) for value in (w_exp, m_exp, v_exp)]

    held = [pltpu.with_memory_space_constraint(x, pltpu.HBM) for x in (act_attn.T, dy_attn, act_exp[0].T, dy_exp[0])]
    full, send, pack = make_terms(plan, *held, *[pltpu.with_memory_space_constraint(x, pltpu.HBM) for x in state_a])
    got = swap_cores(send)
    sums = [
        full[c * chunk : (c + 1) * chunk] + got[c * chunk : (c + 1) * chunk].astype(f32) for c in range(chips)
    ]
    got = [swap(sums[c].astype(bf16), chips=c) for c in reversed(range(1, chips))]
    shared = ((plan.all_a + 16, LANES), bf16)
    payload, g_exp = call(
        lambda *refs: share_kernel(plan, *refs), [sums[0]] + got, [shared, ((plan.size_e, LANES), f32)]
    )
    packs, distance = [pack], n_expert // 2
    while distance > 1:
        other, far = swap(payload, experts=distance), [swap(value, experts=distance) for value in packs]
        payload, held = call(
            lambda *refs: again_kernel(plan, *refs), [payload, other, far[0]], [shared, (pack.shape, bf16)]
        )
        packs += [held] + far[1:]
        distance //= 2
    other, far = swap(payload, experts=1), [swap(value, experts=1) for value in packs]
    states = [*packs, *far]
    g_attn, square = call(
        lambda *refs: last_kernel(plan, *refs), [payload, other], [((plan.all_a, LANES), f32), ((8, LANES), f32)]
    )
    square = square + swap_cores(square)
    squares = [square] + [swap(square, chips=c) for c in square_order(chips)[1:]]
    block_a, block_e = ((plan.size_a, LANES), f32), ((plan.size_e, LANES), f32)
    (mine,) = call(
        lambda *refs: rows_kernel(plan, limit, *refs),
        [*squares, g_attn, g_exp, *state_e, *states],
        [((chunk, LANES), bf16)],
    )
    wa, ma, va, we, me, ve = call(
        lambda *refs: own_kernel(plan, limit, *refs),
        [*squares, g_attn, g_exp, *state_a, *state_e],
        [block_a] * 3 + [block_e] * 3,
    )
    near = [mine] + [swap(mine, chips=c) for c in range(1, chips)]
    far = [swap_cores(piece) for piece in near]
    attn_full, expert_full = put_in_order(plan, near + far)
    new_a = [from_blocks(value, rows_a) for value in (wa, ma, va)]
    new_e = [from_blocks(value, rows_e)[None] for value in (we, me, ve)]
    return (*new_a, *new_e, attn_full, expert_full)


def solution(mesh):
    return jax.shard_map(
        body,
        mesh=mesh,
        in_specs=(
            P(("expert", "dp"), None),
            P(("expert", "dp"), None),
            P("expert", "dp", None),
            P("expert", "dp", None),
            P(("expert", "dp"), None),
            P(("expert", "dp"), None),
            P(("expert", "dp"), None),
            P("expert", "dp", None),
            P("expert", "dp", None),
            P("expert", "dp", None),
        ),
        out_specs=(
            P(("expert", "dp"), None),
            P(("expert", "dp"), None),
            P(("expert", "dp"), None),
            P("expert", "dp", None),
            P("expert", "dp", None),
            P("expert", "dp", None),
            P(),
            P("expert", None, None),
        ),
        check_vma=False,
    )
```

```python
import math

import jax
import jax.numpy as jnp
from jax import lax
from jax.experimental import pallas as pl
from jax.experimental.pallas import tpu as pltpu
from jax.sharding import PartitionSpec as P

beta_first = 0.9
beta_second = 0.95
bias_first = 1.0 - 0.9**10
bias_second = 1.0 - 0.95**10
learn_rate = 0.01
decay_rate = 0.1
adam_eps = 1e-08

LANES = 128
f32, bf16 = jnp.float32, jnp.bfloat16


def adamw(grad, weight, moment, second, factor):
    scaled = factor * grad
    moment_new = beta_first * moment + (1.0 - beta_first) * scaled
    second_new = beta_second * second + (1.0 - beta_second) * scaled * scaled
    update = moment_new / bias_first / (jnp.sqrt(second_new / bias_second) + adam_eps)
    weight_new = weight - learn_rate * (update + decay_rate * weight)
    return (weight_new, moment_new, second_new)


def role_of(chip, core, expert):
    return core ^ ((chip ^ expert ^ (expert // 2)) % 2)


class Plan:
    def __init__(self, n_expert, n_dp, rows_a, rows_e, width):
        self.n_expert, self.n_dp, self.rows_a, self.rows_e = n_expert, n_dp, rows_a, rows_e
        self.width = width
        self.chips = n_dp // 2
        self.blocks = width // LANES
        self.size_a = self.blocks * rows_a
        self.size_e = self.blocks * rows_e
        self.all_a = n_expert * self.size_a
        self.chunk = self.all_a + self.size_e
        self.turned = n_dp == 8 and rows_a == 1

    def places(self, block):
        attn = [
            (e * self.rows_a + r, e * self.size_a + block * self.rows_a + r)
            for e in range(self.n_expert)
            for r in range(self.rows_a)
        ]
        exp = [(r, self.all_a + block * self.rows_e + r) for r in range(self.rows_e)]
        return attn, exp


def dot(left, right):
    return lax.dot_general(left, right, (((1,), (0,)), ((), ())), preferred_element_type=f32)


def size_of(shape, dtype):
    return math.prod(shape) * jnp.dtype(dtype).itemsize


def call(kernel, args, outs, scratch=(), in_space=pltpu.VMEM, out_space=pltpu.VMEM, copies=False):
    held = sum(size_of(arg.shape, arg.dtype) for arg in args if in_space is pltpu.VMEM)
    held += sum(size_of(*out) for out in outs) + sum(size_of(*buffer) for buffer in scratch)
    semaphores = [pltpu.SemaphoreType.DMA((16,))] if copies else []
    return pl.pallas_call(
        kernel,
        in_specs=[pl.BlockSpec(memory_space=in_space)] * len(args),
        out_specs=[pl.BlockSpec(memory_space=out_space)] * len(outs),
        out_shape=[jax.ShapeDtypeStruct(shape, dtype) for shape, dtype in outs],
        scratch_shapes=[pltpu.VMEM(*buffer) for buffer in scratch] + semaphores,
        compiler_params=pltpu.CompilerParams(vmem_limit_bytes=held + 4 * 1024 * 1024),
    )(*args)


def two_pieces(value):
    high = value.astype(bf16).astype(f32)
    return high, (value - high).astype(bf16).astype(f32)


def by_eights(value):
    return jnp.sum(value.reshape(-1, 8, LANES), axis=0)


STEPS = (2, 1)


def each(count, step, unrolled):
    if unrolled:
        for i in range(count):
            step(i)
    else:
        pl.loop(0, count)(step)


def terms_kernel(plan, act_a, dy_a, act_e, dy_e, w, m, v, full, send, pack, act_a_v, dy_a_v, act_e_v, dy_e_v, state, sems):
    unit = plan.blocks // sum(STEPS)
    tiles = [(sum(STEPS[:t]) * unit, STEPS[t] * unit) for t in range(len(STEPS))]
    small = [
        pltpu.make_async_copy(act_a, act_a_v, sems.at[0]),
        pltpu.make_async_copy(act_e, act_e_v, sems.at[1]),
    ]
    big = []
    for t, (first, count) in enumerate(tiles):
        cols = pl.ds(first * LANES, count * LANES)
        big.append(pltpu.make_async_copy(dy_a.at[:, cols], dy_a_v.at[:, cols], sems.at[2 + 2 * t]))
        big.append(pltpu.make_async_copy(dy_e.at[:, cols], dy_e_v.at[:, cols], sems.at[3 + 2 * t]))
    extra = [pltpu.make_async_copy(ref, state.at[i], sems.at[2 + 2 * len(STEPS) + i]) for i, ref in enumerate((w, m, v))]
    for copy in small + big + extra:
        copy.start()

    me, me_ex = lax.axis_index("dp"), lax.axis_index("expert")
    my_role = role_of(me // 2, me % 2, me_ex)

    def pick(groups, per_owner, count, expert):
        shape = (groups * plan.n_dp, count)
        row = lax.broadcasted_iota(jnp.int32, shape, 0)
        col = lax.broadcasted_iota(jnp.int32, shape, 1)
        group, place = row // plan.n_dp, row % plan.n_dp
        chip, role = (place % plan.chips) ^ (me // 2), (place // plan.chips) ^ my_role
        if expert is None:
            expert, base = group // per_owner, (group // per_owner) * plan.n_dp
        else:
            base = 0
        owner = 2 * chip + role_of(chip, role, expert)
        want = (base + owner) * per_owner + group % per_owner
        return (want == col).astype(bf16)

    for copy in small:
        copy.wait()
    left_a = dot(pick(plan.n_expert * plan.rows_a, plan.rows_a, act_a.shape[0], None), act_a_v[...]).astype(bf16)
    left_e = dot(pick(plan.rows_e, plan.rows_e, act_e.shape[0], me_ex), act_e_v[...]).astype(bf16)
    n_dp = plan.n_dp

    def turn(start, pieces):
        value = jnp.stack(pieces).transpose(1, 0, 2)
        for c in range(plan.chips):
            rows = pl.ds(c * plan.chunk + start, len(pieces))
            full[rows, :] = value[c]
            send[rows, :] = value[plan.chips + c].astype(bf16)

    for t, (first, count) in enumerate(tiles):
        cols = pl.ds(first * LANES, count * LANES)
        big[2 * t].wait()
        terms_a = dot(left_a, dy_a_v[:, cols])
        big[2 * t + 1].wait()
        terms_e = dot(left_e, dy_e_v[:, cols])
        if plan.turned:
            blocks = [slice(b * LANES, (b + 1) * LANES) for b in range(count)]
            for e in range(plan.n_expert):
                turn(e * plan.size_a + first, [terms_a[e * n_dp : (e + 1) * n_dp, span] for span in blocks])
            pieces = [
                terms_e[r * n_dp : (r + 1) * n_dp, span] for span in blocks for r in range(plan.rows_e)
            ]
            turn(plan.all_a + first * plan.rows_e, pieces)
            continue
        for b in range(count):
            attn, exp = plan.places(first + b)
            span = slice(b * LANES, (b + 1) * LANES)
            for terms, places in ((terms_a, attn), (terms_e, exp)):
                for group, start in places:
                    full[pl.ds(start, n_dp, stride=plan.chunk), :] = terms[group * n_dp : (group + 1) * n_dp, span]
    for c in range(0 if plan.turned else plan.chips):
        send[pl.ds(c * plan.chunk, plan.chunk), :] = full[
            pl.ds((plan.chips + c) * plan.chunk, plan.chunk), :
        ].astype(bf16)
    for copy in extra:
        copy.wait()
    size = plan.size_a
    for i in range(3):
        pack[pl.ds(i * size, size), :] = state[i].astype(bf16)


def make_terms(plan, act_a, dy_a, act_e, dy_e, w, m, v):
    args = (act_a, dy_a, act_e, dy_e, w, m, v)
    half = plan.chips * plan.chunk
    return call(
        lambda *refs: terms_kernel(plan, *refs),
        args,
        [((half if plan.turned else 2 * half, LANES), f32), ((half, LANES), bf16), ((3 * plan.size_a, LANES), bf16)],
        [
            (act_a.shape, bf16),
            (dy_a.shape, bf16),
            (act_e.shape, bf16),
            (dy_e.shape, bf16),
            ((3,) + w.shape, f32),
        ],
        in_space=pltpu.HBM,
        copies=True,
    )


def share_kernel(plan, *refs):
    held, far, own, got, (payload, g_exp, both) = *refs[:3], refs[3:-3], refs[-3:]
    both[0], both[1] = held[...], far[...]
    total = own[...]
    for ref in got:
        total = total + ref[...].astype(f32)
    a = plan.all_a
    exp = total[a:]
    g_exp[...] = exp
    payload[:a, :] = total[:a].astype(bf16)
    payload[a:, :] = jnp.concatenate(two_pieces(by_eights(exp * exp)), axis=0).astype(bf16)


def pair_sum(plan, mine, other):
    a = plan.all_a
    attn = mine[:a, :].astype(f32) + other[:a, :].astype(f32)
    one, two = mine[a:, :].astype(f32), other[a:, :].astype(f32)
    return attn, (one[:8] + one[8:]) + (two[:8] + two[8:])


def again_kernel(plan, mine, other, payload):
    attn, square = pair_sum(plan, mine, other)
    a = plan.all_a
    payload[:a, :] = attn.astype(bf16)
    payload[a:, :] = jnp.concatenate(two_pieces(square), axis=0).astype(bf16)


def last_kernel(plan, mine, other, g_attn, square):
    attn, partial = pair_sum(plan, mine, other)
    g_attn[...] = attn
    square[...] = partial + by_eights(attn * attn)


def clip_factor(limit, squares):
    norm = jnp.sqrt(jnp.sum(jnp.sum(squares[...], axis=0), keepdims=True))
    return jnp.minimum(1.0, limit / (norm + 1e-06))


def rows_kernel(plan, limit, *refs):
    factor = clip_factor(limit, refs[0])
    g_attn, g_exp, we, me, ve, both, *far, mine = refs[1:]
    size, place = plan.size_a, lax.axis_index("expert")
    for q, states in enumerate([both.at[0], both.at[1], *far]):
        rows = pl.ds(pl.multiple_of((place ^ q) * size, 16), size)
        old = [states[pl.ds(i * size, size), :].astype(f32) for i in range(3)]
        weight, _, _ = adamw(g_attn[rows, :], *old, factor)
        mine[rows, :] = weight.astype(bf16)
    weight, _, _ = adamw(g_exp[...], we[...], me[...], ve[...], factor)
    mine[plan.all_a :, :] = weight.astype(bf16)


def own_kernel(plan, limit, *refs):
    factor = clip_factor(limit, refs[0])
    g_attn, g_exp = refs[1:3]
    state, new = refs[3:9], refs[9:]
    rows = pl.ds(pl.multiple_of(lax.axis_index("expert") * plan.size_a, 16), plan.size_a)
    for b, grad in enumerate((g_attn[rows, :], g_exp[...])):
        values = adamw(grad, *[ref[...] for ref in state[3 * b : 3 * b + 3]], factor)
        for ref, value in zip(new[3 * b : 3 * b + 3], values):
            ref[...] = value


PARTS = 2


def order_kernel(plan, *refs):
    n_dp = plan.n_dp
    parts, (attn, exp, rows, rows_a, rows_e, attn_v, exp_v, sems) = refs[:n_dp], refs[n_dp:]
    me = lax.axis_index("dp")
    me_ex = lax.axis_index("expert")
    my_role = role_of(me // 2, me % 2, me_ex)
    for i, part in enumerate(parts):
        chip, role = (i % plan.chips) ^ (me // 2), (i // plan.chips) ^ my_role
        blocks = [(e, e * plan.size_a, plan.size_a) for e in range(plan.n_expert)]
        for expert, start, size in blocks + [(me_ex, plan.all_a, plan.size_e)]:
            owner = 2 * chip + role_of(chip, role, expert)
            to = pl.multiple_of(owner * plan.chunk + start, 16)
            rows[pl.ds(to, size), :] = part[pl.ds(start, size), :].astype(f32)
    count_e = exp.shape[1]

    def lanes(b):
        return pl.ds(b * LANES if isinstance(b, int) else pl.multiple_of(b * LANES, LANES), LANES)

    def turn(part):
        for e in range(plan.n_expert):
            first = e * plan.size_a + part * count
            value = jnp.stack([rows[pl.ds(j * plan.chunk + first, count), :] for j in range(n_dp)])
            value = value.transpose(1, 0, 2)
            for b in range(count):
                rows_a[pl.ds(e * n_dp, n_dp), lanes(b)] = value[b]
        first = plan.all_a + part * count * plan.rows_e
        value = jnp.stack([rows[pl.ds(j * plan.chunk + first, count * plan.rows_e), :] for j in range(n_dp)])
        value = value.transpose(1, 0, 2)
        for b in range(count):
            for r in range(plan.rows_e):
                start = (part * count + b) * count_e + r
                rows_e[pl.ds(start, n_dp, stride=plan.rows_e), :] = value[b * plan.rows_e + r]
        attn_v[:, pl.ds(part * count * LANES, count * LANES)] = rows_a[...].astype(bf16)

    def gather(b):
        places_a, places_e = plan.places(b)
        values = [rows[pl.ds(start, n_dp, stride=plan.chunk), :] for _, start in places_a]
        if plan.rows_a == 1:
            attn_v[:, lanes(b)] = jnp.concatenate(values, axis=0).astype(bf16)
        else:
            for (group, _), value in zip(places_a, values):
                start = (group // plan.rows_a) * n_dp * plan.rows_a + group % plan.rows_a
                rows_a[pl.ds(start, n_dp, stride=plan.rows_a), :] = value
            attn_v[:, lanes(b)] = rows_a[...].astype(bf16)
        for r, start in places_e:
            rows_e[pl.ds(b * count_e + r, n_dp, stride=plan.rows_e), :] = rows[
                pl.ds(start, n_dp, stride=plan.chunk), :
            ]

    def finish(b):
        exp_v[:, lanes(b)] = rows_e[pl.ds(b * count_e, count_e), :].astype(bf16)

    copies = []
    count = plan.blocks // PARTS
    for part in range(PARTS):
        if plan.turned:
            turn(part)
        else:
            each(count, lambda b: gather(part * count + b), n_dp <= 8)
        each(count, lambda b: finish(part * count + b), True)
        cols = pl.ds(part * count * LANES, count * LANES)
        copies.append(pltpu.make_async_copy(attn_v.at[:, cols], attn.at[:, cols], sems.at[2 * part]))
        copies.append(pltpu.make_async_copy(exp_v.at[:, cols], exp.at[0, :, cols], sems.at[2 * part + 1]))
        for copy in copies[-2:]:
            copy.start()
    for copy in copies:
        copy.wait()


def put_in_order(plan, parts):
    count_a = plan.n_expert * plan.n_dp * plan.rows_a
    count_e = plan.n_dp * plan.rows_e
    return call(
        lambda *refs: order_kernel(plan, *refs),
        parts,
        [((count_a, plan.width), bf16), ((1, count_e, plan.width), bf16)],
        [
            ((plan.n_dp * plan.chunk, LANES), f32),
            ((count_a, plan.width // PARTS if plan.turned else LANES), f32),
            ((plan.blocks * count_e, LANES), f32),
            ((count_a, plan.width), bf16),
            ((count_e, plan.width), bf16),
        ],
        out_space=pltpu.HBM,
        copies=True,
    )


def swap(value, chips=0, experts=0):
    n_expert, n_dp = lax.axis_size("expert"), lax.axis_size("dp")
    pairs = []
    for e in range(n_expert):
        for j in range(n_dp):
            role = role_of(j // 2, j % 2, e)
            chip, expert = (j // 2) ^ chips, e ^ experts
            pairs.append((e * n_dp + j, expert * n_dp + 2 * chip + role_of(chip, role, expert)))
    return lax.ppermute(value, ("expert", "dp"), pairs)


def swap_cores(value):
    return lax.ppermute(value, "dp", [(i, i ^ 1) for i in range(lax.axis_size("dp"))])


def to_blocks(value):
    rows, width = value.shape
    return value.reshape(rows, width // LANES, LANES).transpose(1, 0, 2).reshape(-1, LANES)


def from_blocks(value, rows):
    return value.reshape(-1, rows, LANES).transpose(1, 0, 2).reshape(rows, -1)


def body(act_attn, dy_attn, act_exp, dy_exp, w_attn, m_attn, v_attn, w_exp, m_exp, v_exp):
    width = w_attn.shape[1]
    n_expert = lax.axis_size("expert")
    n_dp = lax.axis_size("dp")
    rows_a, rows_e = w_attn.shape[0], w_exp.shape[1]
    plan = Plan(n_expert, n_dp, rows_a, rows_e, width)
    total_params = width * (act_attn.shape[1] + n_expert * act_exp.shape[2])
    limit = 0.5 * math.sqrt(total_params)
    chips, chunk = plan.chips, plan.chunk
    state_a = [to_blocks(value) for value in (w_attn, m_attn, v_attn)]
    state_e = [to_blocks(value[0]) for value in (w_exp, m_exp, v_exp)]

    held = [pltpu.with_memory_space_constraint(x, pltpu.HBM) for x in (act_attn.T, dy_attn, act_exp[0].T, dy_exp[0])]
    full, send, pack = make_terms(plan, *held, *[pltpu.with_memory_space_constraint(x, pltpu.HBM) for x in state_a])
    got = swap_cores(send)
    sums = [
        full[c * chunk : (c + 1) * chunk] + got[c * chunk : (c + 1) * chunk].astype(f32) for c in range(chips)
    ]
    got = [swap(sums[c].astype(bf16), chips=c) for c in reversed(range(1, chips))]
    shared = ((plan.all_a + 16, LANES), bf16)
    packs = [pack, swap(pack, experts=1)]
    payload, g_exp, both = call(
        lambda *refs: share_kernel(plan, *refs),
        packs + [sums[0]] + got,
        [shared, ((plan.size_e, LANES), f32), ((2,) + pack.shape, bf16)],
    )
    distance = 1
    while 2 * distance < n_expert:
        other = swap(payload, experts=distance)
        (payload,) = call(lambda *refs: again_kernel(plan, *refs), [payload, other], [shared])
        distance *= 2
    other = swap(payload, experts=distance)
    far = [swap(pack, experts=q) for q in range(2, n_expert)]
    g_attn, square = call(
        lambda *refs: last_kernel(plan, *refs), [payload, other], [((plan.all_a, LANES), f32), ((8, LANES), f32)]
    )
    squares = lax.all_gather(square, "dp")
    block_a, block_e = ((plan.size_a, LANES), f32), ((plan.size_e, LANES), f32)
    (mine,) = call(
        lambda *refs: rows_kernel(plan, limit, *refs),
        [squares, g_attn, g_exp, *state_e, both, *far],
        [((chunk, LANES), bf16)],
    )
    wa, ma, va, we, me, ve = call(
        lambda *refs: own_kernel(plan, limit, *refs),
        [squares, g_attn, g_exp, *state_a, *state_e],
        [block_a] * 3 + [block_e] * 3,
    )
    near = [mine] + [swap(mine, chips=c) for c in range(1, chips)]
    far = [swap_cores(piece) for piece in near]
    attn_full, expert_full = put_in_order(plan, near + far)
    new_a = [from_blocks(value, rows_a) for value in (wa, ma, va)]
    new_e = [from_blocks(value, rows_e)[None] for value in (we, me, ve)]
    return (*new_a, *new_e, attn_full, expert_full)


def solution(mesh):
    return jax.shard_map(
        body,
        mesh=mesh,
        in_specs=(
            P(("expert", "dp"), None),
            P(("expert", "dp"), None),
            P("expert", "dp", None),
            P("expert", "dp", None),
            P(("expert", "dp"), None),
            P(("expert", "dp"), None),
            P(("expert", "dp"), None),
            P("expert", "dp", None),
            P("expert", "dp", None),
            P("expert", "dp", None),
        ),
        out_specs=(
            P(("expert", "dp"), None),
            P(("expert", "dp"), None),
            P(("expert", "dp"), None),
            P("expert", "dp", None),
            P("expert", "dp", None),
            P("expert", "dp", None),
            P(),
            P("expert", None, None),
        ),
        check_vma=False,
    )
```

```python
import math

import jax
import jax.numpy as jnp
from jax import lax
from jax.experimental import pallas as pl
from jax.experimental.pallas import tpu as pltpu
from jax.sharding import PartitionSpec as P

beta_first = 0.9
beta_second = 0.95
bias_first = 1.0 - 0.9**10
bias_second = 1.0 - 0.95**10
learn_rate = 0.01
decay_rate = 0.1
adam_eps = 1e-08

LANES = 128
f32, bf16 = jnp.float32, jnp.bfloat16


def adamw(grad, weight, moment, second, factor):
    scaled = factor * grad
    moment_new = beta_first * moment + (1.0 - beta_first) * scaled
    second_new = beta_second * second + (1.0 - beta_second) * scaled * scaled
    update = moment_new / bias_first / (jnp.sqrt(second_new / bias_second) + adam_eps)
    weight_new = weight - learn_rate * (update + decay_rate * weight)
    return (weight_new, moment_new, second_new)


def role_of(chip, core, expert):
    return core ^ ((chip ^ expert ^ (expert // 2)) % 2)


class Plan:
    def __init__(self, n_expert, n_dp, rows_a, rows_e, width):
        self.n_expert, self.n_dp, self.rows_a, self.rows_e = n_expert, n_dp, rows_a, rows_e
        self.width = width
        self.chips = n_dp // 2
        self.blocks = width // LANES
        self.size_a = self.blocks * rows_a
        self.size_e = self.blocks * rows_e
        self.all_a = n_expert * self.size_a
        self.chunk = self.all_a + self.size_e
        self.turned = n_dp == 8 and rows_a == 1

    def places(self, block):
        attn = [
            (e * self.rows_a + r, e * self.size_a + block * self.rows_a + r)
            for e in range(self.n_expert)
            for r in range(self.rows_a)
        ]
        exp = [(r, self.all_a + block * self.rows_e + r) for r in range(self.rows_e)]
        return attn, exp


def dot(left, right):
    return lax.dot_general(left, right, (((1,), (0,)), ((), ())), preferred_element_type=f32)


def size_of(shape, dtype):
    return math.prod(shape) * jnp.dtype(dtype).itemsize


def call(kernel, args, outs, scratch=(), in_space=pltpu.VMEM, out_space=pltpu.VMEM, copies=False):
    held = sum(size_of(arg.shape, arg.dtype) for arg in args if in_space is pltpu.VMEM)
    held += sum(size_of(*out) for out in outs) + sum(size_of(*buffer) for buffer in scratch)
    semaphores = [pltpu.SemaphoreType.DMA((16,))] if copies else []
    return pl.pallas_call(
        kernel,
        in_specs=[pl.BlockSpec(memory_space=in_space)] * len(args),
        out_specs=[pl.BlockSpec(memory_space=out_space)] * len(outs),
        out_shape=[jax.ShapeDtypeStruct(shape, dtype) for shape, dtype in outs],
        scratch_shapes=[pltpu.VMEM(*buffer) for buffer in scratch] + semaphores,
        compiler_params=pltpu.CompilerParams(vmem_limit_bytes=held + 4 * 1024 * 1024),
    )(*args)


def two_pieces(value):
    high = value.astype(bf16).astype(f32)
    return high, (value - high).astype(bf16).astype(f32)


def by_eights(value):
    return jnp.sum(value.reshape(-1, 8, LANES), axis=0)


STEPS = 2


def each(count, step, unrolled):
    if unrolled:
        for i in range(count):
            step(i)
    else:
        pl.loop(0, count)(step)


def terms_kernel(plan, act_a, dy_a, act_e, dy_e, w, m, v, full, send, pack, act_a_v, dy_a_v, act_e_v, dy_e_v, state, sems):
    tile = plan.width // STEPS
    small = [
        pltpu.make_async_copy(act_a, act_a_v, sems.at[0]),
        pltpu.make_async_copy(act_e, act_e_v, sems.at[1]),
    ]
    big = []
    for t in range(STEPS):
        cols = pl.ds(t * tile, tile)
        big.append(pltpu.make_async_copy(dy_a.at[:, cols], dy_a_v.at[:, cols], sems.at[2 + 2 * t]))
        big.append(pltpu.make_async_copy(dy_e.at[:, cols], dy_e_v.at[:, cols], sems.at[3 + 2 * t]))
    extra = [pltpu.make_async_copy(ref, state.at[i], sems.at[2 + 2 * STEPS + i]) for i, ref in enumerate((w, m, v))]
    for copy in small + big + extra:
        copy.start()

    me, me_ex = lax.axis_index("dp"), lax.axis_index("expert")
    my_role = role_of(me // 2, me % 2, me_ex)

    def pick(groups, per_owner, count, expert):
        shape = (groups * plan.n_dp, count)
        row = lax.broadcasted_iota(jnp.int32, shape, 0)
        col = lax.broadcasted_iota(jnp.int32, shape, 1)
        group, place = row // plan.n_dp, row % plan.n_dp
        chip, role = (place % plan.chips) ^ (me // 2), (place // plan.chips) ^ my_role
        if expert is None:
            expert, base = group // per_owner, (group // per_owner) * plan.n_dp
        else:
            base = 0
        owner = 2 * chip + role_of(chip, role, expert)
        want = (base + owner) * per_owner + group % per_owner
        return (want == col).astype(bf16)

    for copy in small:
        copy.wait()
    left_a = dot(pick(plan.n_expert * plan.rows_a, plan.rows_a, act_a.shape[0], None), act_a_v[...]).astype(bf16)
    left_e = dot(pick(plan.rows_e, plan.rows_e, act_e.shape[0], me_ex), act_e_v[...]).astype(bf16)
    n_dp = plan.n_dp

    def turn(start, pieces):
        value = jnp.stack(pieces).transpose(1, 0, 2)
        for c in range(plan.chips):
            rows = pl.ds(c * plan.chunk + start, len(pieces))
            full[rows, :] = value[c]
            send[rows, :] = value[plan.chips + c].astype(bf16)

    for t in range(STEPS):
        cols = pl.ds(t * tile, tile)
        big[2 * t].wait()
        terms_a = dot(left_a, dy_a_v[:, cols])
        big[2 * t + 1].wait()
        terms_e = dot(left_e, dy_e_v[:, cols])
        count = tile // LANES
        if plan.turned:
            blocks = [slice(b * LANES, (b + 1) * LANES) for b in range(count)]
            for e in range(plan.n_expert):
                turn(e * plan.size_a + t * count, [terms_a[e * n_dp : (e + 1) * n_dp, span] for span in blocks])
            pieces = [
                terms_e[r * n_dp : (r + 1) * n_dp, span] for span in blocks for r in range(plan.rows_e)
            ]
            turn(plan.all_a + t * count * plan.rows_e, pieces)
            continue
        for b in range(count):
            attn, exp = plan.places(t * count + b)
            span = slice(b * LANES, (b + 1) * LANES)
            for terms, places in ((terms_a, attn), (terms_e, exp)):
                for group, start in places:
                    full[pl.ds(start, n_dp, stride=plan.chunk), :] = terms[group * n_dp : (group + 1) * n_dp, span]
    for c in range(0 if plan.turned else plan.chips):
        send[pl.ds(c * plan.chunk, plan.chunk), :] = full[
            pl.ds((plan.chips + c) * plan.chunk, plan.chunk), :
        ].astype(bf16)
    for copy in extra:
        copy.wait()
    size = plan.size_a
    for i in range(3):
        pack[pl.ds(i * size, size), :] = state[i].astype(bf16)


def make_terms(plan, act_a, dy_a, act_e, dy_e, w, m, v):
    args = (act_a, dy_a, act_e, dy_e, w, m, v)
    half = plan.chips * plan.chunk
    return call(
        lambda *refs: terms_kernel(plan, *refs),
        args,
        [((half if plan.turned else 2 * half, LANES), f32), ((half, LANES), bf16), ((3 * plan.size_a, LANES), bf16)],
        [
            (act_a.shape, bf16),
            (dy_a.shape, bf16),
            (act_e.shape, bf16),
            (dy_e.shape, bf16),
            ((3,) + w.shape, f32),
        ],
        in_space=pltpu.HBM,
        copies=True,
    )


def share_kernel(plan, *refs):
    held, far, own, got, (payload, g_exp, both) = *refs[:3], refs[3:-3], refs[-3:]
    both[0], both[1] = held[...], far[...]
    total = own[...]
    for ref in got:
        total = total + ref[...].astype(f32)
    a = plan.all_a
    exp = total[a:]
    g_exp[...] = exp
    payload[:a, :] = total[:a].astype(bf16)
    payload[a:, :] = jnp.concatenate(two_pieces(by_eights(exp * exp)), axis=0).astype(bf16)


def pair_sum(plan, mine, other):
    a = plan.all_a
    attn = mine[:a, :].astype(f32) + other[:a, :].astype(f32)
    one, two = mine[a:, :].astype(f32), other[a:, :].astype(f32)
    return attn, (one[:8] + one[8:]) + (two[:8] + two[8:])


def again_kernel(plan, mine, other, payload):
    attn, square = pair_sum(plan, mine, other)
    a = plan.all_a
    payload[:a, :] = attn.astype(bf16)
    payload[a:, :] = jnp.concatenate(two_pieces(square), axis=0).astype(bf16)


def hold_kernel(*refs):
    count = len(refs) // 2
    for ref, out in zip(refs[:count], refs[count:]):
        out[...] = ref[...]


def last_kernel(plan, mine, other, g_attn, square):
    attn, partial = pair_sum(plan, mine, other)
    g_attn[...] = attn
    square[...] = partial + by_eights(attn * attn)


def square_order(chips):
    return [0, *reversed(range(1, chips - 1)), chips - 1]


def clip_factor(limit, squares):
    order = square_order(len(squares))
    values = [squares[order.index(c)][...] for c in range(len(squares))]
    while len(values) > 1:
        values = [values[i] + values[i + 1] for i in range(0, len(values), 2)]
    norm = jnp.sqrt(jnp.sum(values[0], keepdims=True))
    return jnp.minimum(1.0, limit / (norm + 1e-06))


def rows_kernel(plan, limit, *refs):
    factor = clip_factor(limit, refs[: plan.chips])
    g_attn, g_exp, we, me, ve, both, *far, mine = refs[plan.chips :]
    size, place = plan.size_a, lax.axis_index("expert")
    for q, states in enumerate([both.at[0], both.at[1], *far]):
        rows = pl.ds(pl.multiple_of((place ^ q) * size, 16), size)
        old = [states[pl.ds(i * size, size), :].astype(f32) for i in range(3)]
        weight, _, _ = adamw(g_attn[rows, :], *old, factor)
        mine[rows, :] = weight.astype(bf16)
    weight, _, _ = adamw(g_exp[...], we[...], me[...], ve[...], factor)
    mine[plan.all_a :, :] = weight.astype(bf16)


def own_kernel(plan, limit, *refs):
    factor = clip_factor(limit, refs[: plan.chips])
    g_attn, g_exp = refs[plan.chips : plan.chips + 2]
    state, new = refs[plan.chips + 2 : plan.chips + 8], refs[plan.chips + 8 :]
    rows = pl.ds(pl.multiple_of(lax.axis_index("expert") * plan.size_a, 16), plan.size_a)
    for b, grad in enumerate((g_attn[rows, :], g_exp[...])):
        values = adamw(grad, *[ref[...] for ref in state[3 * b : 3 * b + 3]], factor)
        for ref, value in zip(new[3 * b : 3 * b + 3], values):
            ref[...] = value


PARTS = 2


def order_kernel(plan, *refs):
    n_dp = plan.n_dp
    parts, (attn, exp, rows, rows_a, rows_e, attn_v, exp_v, sems) = refs[:n_dp], refs[n_dp:]
    me = lax.axis_index("dp")
    me_ex = lax.axis_index("expert")
    my_role = role_of(me // 2, me % 2, me_ex)
    for i, part in enumerate(parts):
        chip, role = (i % plan.chips) ^ (me // 2), (i // plan.chips) ^ my_role
        blocks = [(e, e * plan.size_a, plan.size_a) for e in range(plan.n_expert)]
        for expert, start, size in blocks + [(me_ex, plan.all_a, plan.size_e)]:
            owner = 2 * chip + role_of(chip, role, expert)
            to = pl.multiple_of(owner * plan.chunk + start, 16)
            rows[pl.ds(to, size), :] = part[pl.ds(start, size), :].astype(f32)
    count_e = exp.shape[1]

    def lanes(b):
        return pl.ds(b * LANES if isinstance(b, int) else pl.multiple_of(b * LANES, LANES), LANES)

    def turn(part):
        for e in range(plan.n_expert):
            first = e * plan.size_a + part * count
            value = jnp.stack([rows[pl.ds(j * plan.chunk + first, count), :] for j in range(n_dp)])
            value = value.transpose(1, 0, 2)
            for b in range(count):
                rows_a[pl.ds(e * n_dp, n_dp), lanes(b)] = value[b]
        first = plan.all_a + part * count * plan.rows_e
        value = jnp.stack([rows[pl.ds(j * plan.chunk + first, count * plan.rows_e), :] for j in range(n_dp)])
        value = value.transpose(1, 0, 2)
        for b in range(count):
            for r in range(plan.rows_e):
                start = (part * count + b) * count_e + r
                rows_e[pl.ds(start, n_dp, stride=plan.rows_e), :] = value[b * plan.rows_e + r]
        attn_v[:, pl.ds(part * count * LANES, count * LANES)] = rows_a[...].astype(bf16)

    def gather(b):
        places_a, places_e = plan.places(b)
        values = [rows[pl.ds(start, n_dp, stride=plan.chunk), :] for _, start in places_a]
        if plan.rows_a == 1:
            attn_v[:, lanes(b)] = jnp.concatenate(values, axis=0).astype(bf16)
        else:
            for (group, _), value in zip(places_a, values):
                start = (group // plan.rows_a) * n_dp * plan.rows_a + group % plan.rows_a
                rows_a[pl.ds(start, n_dp, stride=plan.rows_a), :] = value
            attn_v[:, lanes(b)] = rows_a[...].astype(bf16)
        for r, start in places_e:
            rows_e[pl.ds(b * count_e + r, n_dp, stride=plan.rows_e), :] = rows[
                pl.ds(start, n_dp, stride=plan.chunk), :
            ]

    def finish(b):
        exp_v[:, lanes(b)] = rows_e[pl.ds(b * count_e, count_e), :].astype(bf16)

    copies = []
    count = plan.blocks // PARTS
    for part in range(PARTS):
        if plan.turned:
            turn(part)
        else:
            each(count, lambda b: gather(part * count + b), n_dp <= 8)
        each(count, lambda b: finish(part * count + b), True)
        cols = pl.ds(part * count * LANES, count * LANES)
        copies.append(pltpu.make_async_copy(attn_v.at[:, cols], attn.at[:, cols], sems.at[2 * part]))
        copies.append(pltpu.make_async_copy(exp_v.at[:, cols], exp.at[0, :, cols], sems.at[2 * part + 1]))
        for copy in copies[-2:]:
            copy.start()
    for copy in copies:
        copy.wait()


def put_in_order(plan, parts):
    count_a = plan.n_expert * plan.n_dp * plan.rows_a
    count_e = plan.n_dp * plan.rows_e
    return call(
        lambda *refs: order_kernel(plan, *refs),
        parts,
        [((count_a, plan.width), bf16), ((1, count_e, plan.width), bf16)],
        [
            ((plan.n_dp * plan.chunk, LANES), f32),
            ((count_a, plan.width // PARTS if plan.turned else LANES), f32),
            ((plan.blocks * count_e, LANES), f32),
            ((count_a, plan.width), bf16),
            ((count_e, plan.width), bf16),
        ],
        out_space=pltpu.HBM,
        copies=True,
    )


def swap(value, chips=0, experts=0):
    n_expert, n_dp = lax.axis_size("expert"), lax.axis_size("dp")
    pairs = []
    for e in range(n_expert):
        for j in range(n_dp):
            role = role_of(j // 2, j % 2, e)
            chip, expert = (j // 2) ^ chips, e ^ experts
            pairs.append((e * n_dp + j, expert * n_dp + 2 * chip + role_of(chip, role, expert)))
    return lax.ppermute(value, ("expert", "dp"), pairs)


def swap_cores(value):
    return lax.ppermute(value, "dp", [(i, i ^ 1) for i in range(lax.axis_size("dp"))])


def to_blocks(value):
    rows, width = value.shape
    return value.reshape(rows, width // LANES, LANES).transpose(1, 0, 2).reshape(-1, LANES)


def from_blocks(value, rows):
    return value.reshape(-1, rows, LANES).transpose(1, 0, 2).reshape(rows, -1)


def body(act_attn, dy_attn, act_exp, dy_exp, w_attn, m_attn, v_attn, w_exp, m_exp, v_exp):
    width = w_attn.shape[1]
    n_expert = lax.axis_size("expert")
    n_dp = lax.axis_size("dp")
    rows_a, rows_e = w_attn.shape[0], w_exp.shape[1]
    plan = Plan(n_expert, n_dp, rows_a, rows_e, width)
    total_params = width * (act_attn.shape[1] + n_expert * act_exp.shape[2])
    limit = 0.5 * math.sqrt(total_params)
    chips, chunk = plan.chips, plan.chunk
    state_a = [to_blocks(value) for value in (w_attn, m_attn, v_attn)]
    state_e = [to_blocks(value[0]) for value in (w_exp, m_exp, v_exp)]

    held = [pltpu.with_memory_space_constraint(x, pltpu.HBM) for x in (act_attn.T, dy_attn, act_exp[0].T, dy_exp[0])]
    full, send, pack = make_terms(plan, *held, *[pltpu.with_memory_space_constraint(x, pltpu.HBM) for x in state_a])
    got = swap_cores(send)
    sums = [
        full[c * chunk : (c + 1) * chunk] + got[c * chunk : (c + 1) * chunk].astype(f32) for c in range(chips)
    ]
    got = [swap(sums[c].astype(bf16), chips=c) for c in reversed(range(1, chips))]
    shared = ((plan.all_a + 16, LANES), bf16)
    packs = [pack, swap(pack, experts=1)]
    payload, g_exp, both = call(
        lambda *refs: share_kernel(plan, *refs),
        packs + [sums[0]] + got,
        [shared, ((plan.size_e, LANES), f32), ((2,) + pack.shape, bf16)],
    )
    distance = 1
    while 2 * distance < n_expert:
        other = swap(payload, experts=distance)
        (payload,) = call(lambda *refs: again_kernel(plan, *refs), [payload, other], [shared])
        distance *= 2
    other = swap(payload, experts=distance)
    early = [q for q in range(2, n_expert) if q != distance]
    held = [pack] + [swap(pack, experts=q) for q in early]
    held = call(hold_kernel, held, [(pack.shape, bf16)] * len(held))
    far = dict(zip(early, held[1:]))
    far[distance] = swap(held[0], experts=distance)
    far = [far[q] for q in range(2, n_expert)]
    g_attn, square = call(
        lambda *refs: last_kernel(plan, *refs), [payload, other], [((plan.all_a, LANES), f32), ((8, LANES), f32)]
    )
    square = square + swap_cores(square)
    squares = [square] + [swap(square, chips=c) for c in square_order(chips)[1:]]
    block_a, block_e = ((plan.size_a, LANES), f32), ((plan.size_e, LANES), f32)
    (mine,) = call(
        lambda *refs: rows_kernel(plan, limit, *refs),
        [*squares, g_attn, g_exp, *state_e, both, *far],
        [((chunk, LANES), bf16)],
    )
    wa, ma, va, we, me, ve = call(
        lambda *refs: own_kernel(plan, limit, *refs),
        [*squares, g_attn, g_exp, *state_a, *state_e],
        [block_a] * 3 + [block_e] * 3,
    )
    near = [mine] + [swap(mine, chips=c) for c in range(1, chips)]
    far = [swap_cores(piece) for piece in near]
    attn_full, expert_full = put_in_order(plan, near + far)
    new_a = [from_blocks(value, rows_a) for value in (wa, ma, va)]
    new_e = [from_blocks(value, rows_e)[None] for value in (we, me, ve)]
    return (*new_a, *new_e, attn_full, expert_full)


def solution(mesh):
    return jax.shard_map(
        body,
        mesh=mesh,
        in_specs=(
            P(("expert", "dp"), None),
            P(("expert", "dp"), None),
            P("expert", "dp", None),
            P("expert", "dp", None),
            P(("expert", "dp"), None),
            P(("expert", "dp"), None),
            P(("expert", "dp"), None),
            P("expert", "dp", None),
            P("expert", "dp", None),
            P("expert", "dp", None),
        ),
        out_specs=(
            P(("expert", "dp"), None),
            P(("expert", "dp"), None),
            P(("expert", "dp"), None),
            P("expert", "dp", None),
            P("expert", "dp", None),
            P("expert", "dp", None),
            P(),
            P("expert", None, None),
        ),
        check_vma=False,
    )
```

```python
import math

import jax
import jax.numpy as jnp
from jax import lax
from jax.experimental import pallas as pl
from jax.experimental.pallas import tpu as pltpu
from jax.sharding import PartitionSpec as P

beta_first = 0.9
beta_second = 0.95
bias_first = 1.0 - 0.9**10
bias_second = 1.0 - 0.95**10
learn_rate = 0.01
decay_rate = 0.1
adam_eps = 1e-08

LANES = 128
f32, bf16 = jnp.float32, jnp.bfloat16


def adamw(grad, weight, moment, second, factor):
    scaled = factor * grad
    moment_new = beta_first * moment + (1.0 - beta_first) * scaled
    second_new = beta_second * second + (1.0 - beta_second) * scaled * scaled
    update = moment_new / bias_first / (jnp.sqrt(second_new / bias_second) + adam_eps)
    weight_new = weight - learn_rate * (update + decay_rate * weight)
    return (weight_new, moment_new, second_new)


def role_of(chip, core, expert):
    return core ^ ((chip ^ expert ^ (expert // 2)) % 2)


class Plan:
    def __init__(self, n_expert, n_dp, rows_a, rows_e, width):
        self.n_expert, self.n_dp, self.rows_a, self.rows_e = n_expert, n_dp, rows_a, rows_e
        self.width = width
        self.chips = n_dp // 2
        self.blocks = width // LANES
        self.size_a = self.blocks * rows_a
        self.size_e = self.blocks * rows_e
        self.all_a = n_expert * self.size_a
        self.chunk = self.all_a + self.size_e
        self.turned = n_dp == 8 and rows_a == 1

    def places(self, block):
        attn = [
            (e * self.rows_a + r, e * self.size_a + block * self.rows_a + r)
            for e in range(self.n_expert)
            for r in range(self.rows_a)
        ]
        exp = [(r, self.all_a + block * self.rows_e + r) for r in range(self.rows_e)]
        return attn, exp


def dot(left, right):
    return lax.dot_general(left, right, (((1,), (0,)), ((), ())), preferred_element_type=f32)


def size_of(shape, dtype):
    return math.prod(shape) * jnp.dtype(dtype).itemsize


def call(kernel, args, outs, scratch=(), in_space=pltpu.VMEM, out_space=pltpu.VMEM, copies=False):
    held = sum(size_of(arg.shape, arg.dtype) for arg in args if in_space is pltpu.VMEM)
    held += sum(size_of(*out) for out in outs) + sum(size_of(*buffer) for buffer in scratch)
    semaphores = [pltpu.SemaphoreType.DMA((16,))] if copies else []
    return pl.pallas_call(
        kernel,
        in_specs=[pl.BlockSpec(memory_space=in_space)] * len(args),
        out_specs=[pl.BlockSpec(memory_space=out_space)] * len(outs),
        out_shape=[jax.ShapeDtypeStruct(shape, dtype) for shape, dtype in outs],
        scratch_shapes=[pltpu.VMEM(*buffer) for buffer in scratch] + semaphores,
        compiler_params=pltpu.CompilerParams(vmem_limit_bytes=held + 4 * 1024 * 1024),
    )(*args)


def two_pieces(value):
    high = value.astype(bf16).astype(f32)
    return high, (value - high).astype(bf16).astype(f32)


def by_eights(value):
    return jnp.sum(value.reshape(-1, 8, LANES), axis=0)


STEPS = 2


def each(count, step, unrolled):
    if unrolled:
        for i in range(count):
            step(i)
    else:
        pl.loop(0, count)(step)


def terms_kernel(plan, act_a, dy_a, act_e, dy_e, w, m, v, full, send, pack, act_a_v, dy_a_v, act_e_v, dy_e_v, state, sems):
    tile = plan.width // STEPS
    small = [
        pltpu.make_async_copy(act_a, act_a_v, sems.at[0]),
        pltpu.make_async_copy(act_e, act_e_v, sems.at[1]),
    ]
    big = []
    for t in range(STEPS):
        cols = pl.ds(t * tile, tile)
        big.append(pltpu.make_async_copy(dy_a.at[:, cols], dy_a_v.at[:, cols], sems.at[2 + 2 * t]))
        big.append(pltpu.make_async_copy(dy_e.at[:, cols], dy_e_v.at[:, cols], sems.at[3 + 2 * t]))
    extra = [pltpu.make_async_copy(ref, state.at[i], sems.at[2 + 2 * STEPS + i]) for i, ref in enumerate((w, m, v))]
    for copy in small + big + extra:
        copy.start()

    me, me_ex = lax.axis_index("dp"), lax.axis_index("expert")
    my_role = role_of(me // 2, me % 2, me_ex)

    def pick(groups, per_owner, count, expert):
        shape = (groups * plan.n_dp, count)
        row = lax.broadcasted_iota(jnp.int32, shape, 0)
        col = lax.broadcasted_iota(jnp.int32, shape, 1)
        group, place = row // plan.n_dp, row % plan.n_dp
        chip, role = (place % plan.chips) ^ (me // 2), (place // plan.chips) ^ my_role
        if expert is None:
            expert, base = group // per_owner, (group // per_owner) * plan.n_dp
        else:
            base = 0
        owner = 2 * chip + role_of(chip, role, expert)
        want = (base + owner) * per_owner + group % per_owner
        return (want == col).astype(bf16)

    for copy in small:
        copy.wait()
    left_a = dot(pick(plan.n_expert * plan.rows_a, plan.rows_a, act_a.shape[0], None), act_a_v[...]).astype(bf16)
    left_e = dot(pick(plan.rows_e, plan.rows_e, act_e.shape[0], me_ex), act_e_v[...]).astype(bf16)
    n_dp = plan.n_dp

    def turn(start, pieces):
        value = jnp.stack(pieces).transpose(1, 0, 2)
        for c in range(plan.chips):
            rows = pl.ds(c * plan.chunk + start, len(pieces))
            full[rows, :] = value[c]
            send[rows, :] = value[plan.chips + c].astype(bf16)

    for t in range(STEPS):
        cols = pl.ds(t * tile, tile)
        big[2 * t].wait()
        terms_a = dot(left_a, dy_a_v[:, cols])
        big[2 * t + 1].wait()
        terms_e = dot(left_e, dy_e_v[:, cols])
        count = tile // LANES
        if plan.turned:
            blocks = [slice(b * LANES, (b + 1) * LANES) for b in range(count)]
            for e in range(plan.n_expert):
                turn(e * plan.size_a + t * count, [terms_a[e * n_dp : (e + 1) * n_dp, span] for span in blocks])
            pieces = [
                terms_e[r * n_dp : (r + 1) * n_dp, span] for span in blocks for r in range(plan.rows_e)
            ]
            turn(plan.all_a + t * count * plan.rows_e, pieces)
            continue
        for b in range(count):
            attn, exp = plan.places(t * count + b)
            span = slice(b * LANES, (b + 1) * LANES)
            for terms, places in ((terms_a, attn), (terms_e, exp)):
                for group, start in places:
                    full[pl.ds(start, n_dp, stride=plan.chunk), :] = terms[group * n_dp : (group + 1) * n_dp, span]
    for c in range(0 if plan.turned else plan.chips):
        send[pl.ds(c * plan.chunk, plan.chunk), :] = full[
            pl.ds((plan.chips + c) * plan.chunk, plan.chunk), :
        ].astype(bf16)
    for copy in extra:
        copy.wait()
    size = plan.size_a
    for i in range(3):
        pack[pl.ds(i * size, size), :] = state[i].astype(bf16)


def make_terms(plan, act_a, dy_a, act_e, dy_e, w, m, v):
    args = (act_a, dy_a, act_e, dy_e, w, m, v)
    half = plan.chips * plan.chunk
    return call(
        lambda *refs: terms_kernel(plan, *refs),
        args,
        [((half if plan.turned else 2 * half, LANES), f32), ((half, LANES), bf16), ((3 * plan.size_a, LANES), bf16)],
        [
            (act_a.shape, bf16),
            (dy_a.shape, bf16),
            (act_e.shape, bf16),
            (dy_e.shape, bf16),
            ((3,) + w.shape, f32),
        ],
        in_space=pltpu.HBM,
        copies=True,
    )


def share_kernel(plan, *refs):
    own, got, (payload, g_exp) = refs[0], refs[1:-2], refs[-2:]
    total = own[...]
    for ref in got:
        total = total + ref[...].astype(f32)
    a = plan.all_a
    exp = total[a:]
    g_exp[...] = exp
    payload[:a, :] = total[:a].astype(bf16)
    payload[a:, :] = jnp.concatenate(two_pieces(by_eights(exp * exp)), axis=0).astype(bf16)


def pair_sum(plan, mine, other):
    a = plan.all_a
    attn = mine[:a, :].astype(f32) + other[:a, :].astype(f32)
    one, two = mine[a:, :].astype(f32), other[a:, :].astype(f32)
    return attn, (one[:8] + one[8:]) + (two[:8] + two[8:])


def again_kernel(plan, mine, other, payload):
    attn, square = pair_sum(plan, mine, other)
    a = plan.all_a
    payload[:a, :] = attn.astype(bf16)
    payload[a:, :] = jnp.concatenate(two_pieces(square), axis=0).astype(bf16)


def hold_kernel(*refs):
    count = len(refs) // 2
    for ref, out in zip(refs[:count], refs[count:]):
        out[...] = ref[...]


def last_kernel(plan, mine, other, g_attn, square):
    attn, partial = pair_sum(plan, mine, other)
    g_attn[...] = attn
    square[...] = partial + by_eights(attn * attn)


def square_order(chips):
    return [0, *reversed(range(1, chips))]


def clip_factor(limit, squares):
    order = square_order(len(squares))
    values = [squares[order.index(c)][...] for c in range(len(squares))]
    while len(values) > 1:
        values = [values[i] + values[i + 1] for i in range(0, len(values), 2)]
    norm = jnp.sqrt(jnp.sum(values[0], keepdims=True))
    return jnp.minimum(1.0, limit / (norm + 1e-06))


def rows_kernel(plan, limit, *refs):
    factor = clip_factor(limit, refs[: plan.chips])
    g_attn, g_exp, we, me, ve, *packs, mine = refs[plan.chips :]
    size, place = plan.size_a, lax.axis_index("expert")
    for q, states in enumerate(packs):
        rows = pl.ds(pl.multiple_of((place ^ q) * size, 16), size)
        old = [states[pl.ds(i * size, size), :].astype(f32) for i in range(3)]
        weight, _, _ = adamw(g_attn[rows, :], *old, factor)
        mine[rows, :] = weight.astype(bf16)
    weight, _, _ = adamw(g_exp[...], we[...], me[...], ve[...], factor)
    mine[plan.all_a :, :] = weight.astype(bf16)


def own_kernel(plan, limit, *refs):
    factor = clip_factor(limit, refs[: plan.chips])
    g_attn, g_exp = refs[plan.chips : plan.chips + 2]
    state, new = refs[plan.chips + 2 : plan.chips + 8], refs[plan.chips + 8 :]
    rows = pl.ds(pl.multiple_of(lax.axis_index("expert") * plan.size_a, 16), plan.size_a)
    for b, grad in enumerate((g_attn[rows, :], g_exp[...])):
        values = adamw(grad, *[ref[...] for ref in state[3 * b : 3 * b + 3]], factor)
        for ref, value in zip(new[3 * b : 3 * b + 3], values):
            ref[...] = value


PARTS = 2


def order_kernel(plan, *refs):
    n_dp = plan.n_dp
    parts, (attn, exp, rows, rows_a, rows_e, attn_v, exp_v, sems) = refs[:n_dp], refs[n_dp:]
    me = lax.axis_index("dp")
    me_ex = lax.axis_index("expert")
    my_role = role_of(me // 2, me % 2, me_ex)
    for i, part in enumerate(parts):
        chip, role = (i % plan.chips) ^ (me // 2), (i // plan.chips) ^ my_role
        blocks = [(e, e * plan.size_a, plan.size_a) for e in range(plan.n_expert)]
        for expert, start, size in blocks + [(me_ex, plan.all_a, plan.size_e)]:
            owner = 2 * chip + role_of(chip, role, expert)
            to = pl.multiple_of(owner * plan.chunk + start, 16)
            rows[pl.ds(to, size), :] = part[pl.ds(start, size), :].astype(f32)
    count_e = exp.shape[1]

    def lanes(b):
        return pl.ds(b * LANES if isinstance(b, int) else pl.multiple_of(b * LANES, LANES), LANES)

    def turn(part):
        for e in range(plan.n_expert):
            first = e * plan.size_a + part * count
            value = jnp.stack([rows[pl.ds(j * plan.chunk + first, count), :] for j in range(n_dp)])
            value = value.transpose(1, 0, 2)
            for b in range(count):
                rows_a[pl.ds(e * n_dp, n_dp), lanes(b)] = value[b]
        first = plan.all_a + part * count * plan.rows_e
        value = jnp.stack([rows[pl.ds(j * plan.chunk + first, count * plan.rows_e), :] for j in range(n_dp)])
        value = value.transpose(1, 0, 2)
        for b in range(count):
            for r in range(plan.rows_e):
                start = (part * count + b) * count_e + r
                rows_e[pl.ds(start, n_dp, stride=plan.rows_e), :] = value[b * plan.rows_e + r]
        attn_v[:, pl.ds(part * count * LANES, count * LANES)] = rows_a[...].astype(bf16)

    def gather(b):
        places_a, places_e = plan.places(b)
        values = [rows[pl.ds(start, n_dp, stride=plan.chunk), :] for _, start in places_a]
        if plan.rows_a == 1:
            attn_v[:, lanes(b)] = jnp.concatenate(values, axis=0).astype(bf16)
        else:
            for (group, _), value in zip(places_a, values):
                start = (group // plan.rows_a) * n_dp * plan.rows_a + group % plan.rows_a
                rows_a[pl.ds(start, n_dp, stride=plan.rows_a), :] = value
            attn_v[:, lanes(b)] = rows_a[...].astype(bf16)
        for r, start in places_e:
            rows_e[pl.ds(b * count_e + r, n_dp, stride=plan.rows_e), :] = rows[
                pl.ds(start, n_dp, stride=plan.chunk), :
            ]

    def finish(b):
        exp_v[:, lanes(b)] = rows_e[pl.ds(b * count_e, count_e), :].astype(bf16)

    copies = []
    count = plan.blocks // PARTS
    for part in range(PARTS):
        if plan.turned:
            turn(part)
        else:
            each(count, lambda b: gather(part * count + b), n_dp <= 8)
        each(count, lambda b: finish(part * count + b), True)
        cols = pl.ds(part * count * LANES, count * LANES)
        copies.append(pltpu.make_async_copy(attn_v.at[:, cols], attn.at[:, cols], sems.at[2 * part]))
        copies.append(pltpu.make_async_copy(exp_v.at[:, cols], exp.at[0, :, cols], sems.at[2 * part + 1]))
        for copy in copies[-2:]:
            copy.start()
    for copy in copies:
        copy.wait()


def put_in_order(plan, parts):
    count_a = plan.n_expert * plan.n_dp * plan.rows_a
    count_e = plan.n_dp * plan.rows_e
    return call(
        lambda *refs: order_kernel(plan, *refs),
        parts,
        [((count_a, plan.width), bf16), ((1, count_e, plan.width), bf16)],
        [
            ((plan.n_dp * plan.chunk, LANES), f32),
            ((count_a, plan.width // PARTS if plan.turned else LANES), f32),
            ((plan.blocks * count_e, LANES), f32),
            ((count_a, plan.width), bf16),
            ((count_e, plan.width), bf16),
        ],
        out_space=pltpu.HBM,
        copies=True,
    )


def swap(value, chips=0, experts=0):
    n_expert, n_dp = lax.axis_size("expert"), lax.axis_size("dp")
    pairs = []
    for e in range(n_expert):
        for j in range(n_dp):
            role = role_of(j // 2, j % 2, e)
            chip, expert = (j // 2) ^ chips, e ^ experts
            pairs.append((e * n_dp + j, expert * n_dp + 2 * chip + role_of(chip, role, expert)))
    return lax.ppermute(value, ("expert", "dp"), pairs)


def swap_cores(value):
    return lax.ppermute(value, "dp", [(i, i ^ 1) for i in range(lax.axis_size("dp"))])


def to_blocks(value):
    rows, width = value.shape
    return value.reshape(rows, width // LANES, LANES).transpose(1, 0, 2).reshape(-1, LANES)


def from_blocks(value, rows):
    return value.reshape(-1, rows, LANES).transpose(1, 0, 2).reshape(rows, -1)


def body(act_attn, dy_attn, act_exp, dy_exp, w_attn, m_attn, v_attn, w_exp, m_exp, v_exp):
    width = w_attn.shape[1]
    n_expert = lax.axis_size("expert")
    n_dp = lax.axis_size("dp")
    rows_a, rows_e = w_attn.shape[0], w_exp.shape[1]
    plan = Plan(n_expert, n_dp, rows_a, rows_e, width)
    total_params = width * (act_attn.shape[1] + n_expert * act_exp.shape[2])
    limit = 0.5 * math.sqrt(total_params)
    chips, chunk = plan.chips, plan.chunk
    state_a = [to_blocks(value) for value in (w_attn, m_attn, v_attn)]
    state_e = [to_blocks(value[0]) for value in (w_exp, m_exp, v_exp)]

    held = [pltpu.with_memory_space_constraint(x, pltpu.HBM) for x in (act_attn.T, dy_attn, act_exp[0].T, dy_exp[0])]
    full, send, pack = make_terms(plan, *held, *[pltpu.with_memory_space_constraint(x, pltpu.HBM) for x in state_a])
    got = swap_cores(send)
    sums = [
        full[c * chunk : (c + 1) * chunk] + got[c * chunk : (c + 1) * chunk].astype(f32) for c in range(chips)
    ]
    got = [swap(sums[c].astype(bf16), chips=c) for c in reversed(range(1, chips))]
    shared = ((plan.all_a + 16, LANES), bf16)
    payload, g_exp = call(
        lambda *refs: share_kernel(plan, *refs), [sums[0]] + got, [shared, ((plan.size_e, LANES), f32)]
    )
    distance = 1
    while 2 * distance < n_expert:
        other = swap(payload, experts=distance)
        (payload,) = call(lambda *refs: again_kernel(plan, *refs), [payload, other], [shared])
        distance *= 2
    other = swap(payload, experts=distance)
    states = [pack] + [swap(pack, experts=q) for q in range(2, n_expert, 2)]
    states = call(hold_kernel, states, [(pack.shape, bf16)] * len(states))
    pairs = [(state, swap(state, experts=1)) for state in states]
    states = [state for pair in pairs for state in pair]
    g_attn, square = call(
        lambda *refs: last_kernel(plan, *refs), [payload, other], [((plan.all_a, LANES), f32), ((8, LANES), f32)]
    )
    square = square + swap_cores(square)
    squares = [square] + [swap(square, chips=c) for c in square_order(chips)[1:]]
    block_a, block_e = ((plan.size_a, LANES), f32), ((plan.size_e, LANES), f32)
    (mine,) = call(
        lambda *refs: rows_kernel(plan, limit, *refs),
        [*squares, g_attn, g_exp, *state_e, *states],
        [((chunk, LANES), bf16)],
    )
    wa, ma, va, we, me, ve = call(
        lambda *refs: own_kernel(plan, limit, *refs),
        [*squares, g_attn, g_exp, *state_a, *state_e],
        [block_a] * 3 + [block_e] * 3,
    )
    near = [mine] + [swap(mine, chips=c) for c in range(1, chips)]
    far = [swap_cores(piece) for piece in near]
    attn_full, expert_full = put_in_order(plan, near + far)
    new_a = [from_blocks(value, rows_a) for value in (wa, ma, va)]
    new_e = [from_blocks(value, rows_e)[None] for value in (we, me, ve)]
    return (*new_a, *new_e, attn_full, expert_full)


def solution(mesh):
    return jax.shard_map(
        body,
        mesh=mesh,
        in_specs=(
            P(("expert", "dp"), None),
            P(("expert", "dp"), None),
            P("expert", "dp", None),
            P("expert", "dp", None),
            P(("expert", "dp"), None),
            P(("expert", "dp"), None),
            P(("expert", "dp"), None),
            P("expert", "dp", None),
            P("expert", "dp", None),
            P("expert", "dp", None),
        ),
        out_specs=(
            P(("expert", "dp"), None),
            P(("expert", "dp"), None),
            P(("expert", "dp"), None),
            P("expert", "dp", None),
            P("expert", "dp", None),
            P("expert", "dp", None),
            P(),
            P("expert", None, None),
        ),
        check_vma=False,
    )
```

```python
import math

import jax
import jax.numpy as jnp
from jax import lax
from jax.experimental import pallas as pl
from jax.experimental.pallas import tpu as pltpu
from jax.sharding import PartitionSpec as P

beta_first = 0.9
beta_second = 0.95
bias_first = 1.0 - 0.9**10
bias_second = 1.0 - 0.95**10
learn_rate = 0.01
decay_rate = 0.1
adam_eps = 1e-08

LANES = 128
f32, bf16 = jnp.float32, jnp.bfloat16


def adamw(grad, weight, moment, second, factor):
    scaled = factor * grad
    moment_new = beta_first * moment + (1.0 - beta_first) * scaled
    second_new = beta_second * second + (1.0 - beta_second) * scaled * scaled
    update = moment_new / bias_first / (jnp.sqrt(second_new / bias_second) + adam_eps)
    weight_new = weight - learn_rate * (update + decay_rate * weight)
    return (weight_new, moment_new, second_new)


def role_of(chip, core, expert):
    return core ^ ((chip ^ expert ^ (expert // 2)) % 2)


class Plan:
    def __init__(self, n_expert, n_dp, rows_a, rows_e, width):
        self.n_expert, self.n_dp, self.rows_a, self.rows_e = n_expert, n_dp, rows_a, rows_e
        self.width = width
        self.chips = n_dp // 2
        self.blocks = width // LANES
        self.size_a = self.blocks * rows_a
        self.size_e = self.blocks * rows_e
        self.all_a = n_expert * self.size_a
        self.chunk = self.all_a + self.size_e
        self.turned = n_dp == 8 and rows_a == 1

    def places(self, block):
        attn = [
            (e * self.rows_a + r, e * self.size_a + block * self.rows_a + r)
            for e in range(self.n_expert)
            for r in range(self.rows_a)
        ]
        exp = [(r, self.all_a + block * self.rows_e + r) for r in range(self.rows_e)]
        return attn, exp


def dot(left, right):
    return lax.dot_general(left, right, (((1,), (0,)), ((), ())), preferred_element_type=f32)


def size_of(shape, dtype):
    return math.prod(shape) * jnp.dtype(dtype).itemsize


def call(kernel, args, outs, scratch=(), in_space=pltpu.VMEM, out_space=pltpu.VMEM, copies=False):
    held = sum(size_of(arg.shape, arg.dtype) for arg in args if in_space is pltpu.VMEM)
    held += sum(size_of(*out) for out in outs) + sum(size_of(*buffer) for buffer in scratch)
    semaphores = [pltpu.SemaphoreType.DMA((16,))] if copies else []
    return pl.pallas_call(
        kernel,
        in_specs=[pl.BlockSpec(memory_space=in_space)] * len(args),
        out_specs=[pl.BlockSpec(memory_space=out_space)] * len(outs),
        out_shape=[jax.ShapeDtypeStruct(shape, dtype) for shape, dtype in outs],
        scratch_shapes=[pltpu.VMEM(*buffer) for buffer in scratch] + semaphores,
        compiler_params=pltpu.CompilerParams(vmem_limit_bytes=held + 4 * 1024 * 1024),
    )(*args)


def two_pieces(value):
    high = value.astype(bf16).astype(f32)
    return high, (value - high).astype(bf16).astype(f32)


def by_eights(value):
    return jnp.sum(value.reshape(-1, 8, LANES), axis=0)


STEPS = 2


def each(count, step, unrolled):
    if unrolled:
        for i in range(count):
            step(i)
    else:
        pl.loop(0, count)(step)


def terms_kernel(plan, act_a, dy_a, act_e, dy_e, w, m, v, full, send, pack, act_a_v, dy_a_v, act_e_v, dy_e_v, state, sems):
    tile = plan.width // STEPS
    small = [
        pltpu.make_async_copy(act_a, act_a_v, sems.at[0]),
        pltpu.make_async_copy(act_e, act_e_v, sems.at[1]),
    ]
    big = []
    for t in range(STEPS):
        cols = pl.ds(t * tile, tile)
        big.append(pltpu.make_async_copy(dy_a.at[:, cols], dy_a_v.at[:, cols], sems.at[2 + 2 * t]))
        big.append(pltpu.make_async_copy(dy_e.at[:, cols], dy_e_v.at[:, cols], sems.at[3 + 2 * t]))
    extra = [pltpu.make_async_copy(ref, state.at[i], sems.at[2 + 2 * STEPS + i]) for i, ref in enumerate((w, m, v))]
    for copy in small + big + extra:
        copy.start()

    me, me_ex = lax.axis_index("dp"), lax.axis_index("expert")
    my_role = role_of(me // 2, me % 2, me_ex)

    def pick(groups, per_owner, count, expert):
        shape = (groups * plan.n_dp, count)
        row = lax.broadcasted_iota(jnp.int32, shape, 0)
        col = lax.broadcasted_iota(jnp.int32, shape, 1)
        group, place = row // plan.n_dp, row % plan.n_dp
        chip, role = (place % plan.chips) ^ (me // 2), (place // plan.chips) ^ my_role
        if expert is None:
            expert, base = group // per_owner, (group // per_owner) * plan.n_dp
        else:
            base = 0
        owner = 2 * chip + role_of(chip, role, expert)
        want = (base + owner) * per_owner + group % per_owner
        return (want == col).astype(bf16)

    for copy in small:
        copy.wait()
    left_a = dot(pick(plan.n_expert * plan.rows_a, plan.rows_a, act_a.shape[0], None), act_a_v[...]).astype(bf16)
    left_e = dot(pick(plan.rows_e, plan.rows_e, act_e.shape[0], me_ex), act_e_v[...]).astype(bf16)
    n_dp = plan.n_dp

    def turn(start, pieces):
        value = jnp.stack(pieces).transpose(1, 0, 2)
        for c in range(plan.chips):
            rows = pl.ds(c * plan.chunk + start, len(pieces))
            full[rows, :] = value[c]
            send[rows, :] = value[plan.chips + c].astype(bf16)

    for t in range(STEPS):
        cols = pl.ds(t * tile, tile)
        big[2 * t].wait()
        terms_a = dot(left_a, dy_a_v[:, cols])
        big[2 * t + 1].wait()
        terms_e = dot(left_e, dy_e_v[:, cols])
        count = tile // LANES
        if plan.turned:
            blocks = [slice(b * LANES, (b + 1) * LANES) for b in range(count)]
            for e in range(plan.n_expert):
                turn(e * plan.size_a + t * count, [terms_a[e * n_dp : (e + 1) * n_dp, span] for span in blocks])
            pieces = [
                terms_e[r * n_dp : (r + 1) * n_dp, span] for span in blocks for r in range(plan.rows_e)
            ]
            turn(plan.all_a + t * count * plan.rows_e, pieces)
            continue
        for b in range(count):
            attn, exp = plan.places(t * count + b)
            span = slice(b * LANES, (b + 1) * LANES)
            for terms, places in ((terms_a, attn), (terms_e, exp)):
                for group, start in places:
                    full[pl.ds(start, n_dp, stride=plan.chunk), :] = terms[group * n_dp : (group + 1) * n_dp, span]
    for c in range(0 if plan.turned else plan.chips):
        send[pl.ds(c * plan.chunk, plan.chunk), :] = full[
            pl.ds((plan.chips + c) * plan.chunk, plan.chunk), :
        ].astype(bf16)
    for copy in extra:
        copy.wait()
    size = plan.size_a
    for i in range(3):
        pack[pl.ds(i * size, size), :] = state[i].astype(bf16)


def make_terms(plan, act_a, dy_a, act_e, dy_e, w, m, v):
    args = (act_a, dy_a, act_e, dy_e, w, m, v)
    half = plan.chips * plan.chunk
    return call(
        lambda *refs: terms_kernel(plan, *refs),
        args,
        [((half if plan.turned else 2 * half, LANES), f32), ((half, LANES), bf16), ((3 * plan.size_a, LANES), bf16)],
        [
            (act_a.shape, bf16),
            (dy_a.shape, bf16),
            (act_e.shape, bf16),
            (dy_e.shape, bf16),
            ((3,) + w.shape, f32),
        ],
        in_space=pltpu.HBM,
        copies=True,
    )


def share_kernel(plan, *refs):
    held, far, own, got, (payload, g_exp, both) = *refs[:3], refs[3:-3], refs[-3:]
    both[0], both[1] = held[...], far[...]
    total = own[...]
    for ref in got:
        total = total + ref[...].astype(f32)
    a = plan.all_a
    exp = total[a:]
    g_exp[...] = exp
    payload[:a, :] = total[:a].astype(bf16)
    payload[a:, :] = jnp.concatenate(two_pieces(by_eights(exp * exp)), axis=0).astype(bf16)


def pair_sum(plan, mine, other):
    a = plan.all_a
    attn = mine[:a, :].astype(f32) + other[:a, :].astype(f32)
    one, two = mine[a:, :].astype(f32), other[a:, :].astype(f32)
    return attn, (one[:8] + one[8:]) + (two[:8] + two[8:])


def again_kernel(plan, mine, other, payload):
    attn, square = pair_sum(plan, mine, other)
    a = plan.all_a
    payload[:a, :] = attn.astype(bf16)
    payload[a:, :] = jnp.concatenate(two_pieces(square), axis=0).astype(bf16)


def hold_kernel(*refs):
    count = len(refs) // 2
    for ref, out in zip(refs[:count], refs[count:]):
        out[...] = ref[...]


def last_kernel(plan, mine, other, g_attn, square):
    attn, partial = pair_sum(plan, mine, other)
    g_attn[...] = attn
    square[...] = partial + by_eights(attn * attn)


def square_order(chips):
    return [0, *reversed(range(1, chips - 1)), chips - 1]


def clip_factor(limit, squares):
    order = square_order(len(squares))
    values = [squares[order.index(c)][...] for c in range(len(squares))]
    while len(values) > 1:
        values = [values[i] + values[i + 1] for i in range(0, len(values), 2)]
    norm = jnp.sqrt(jnp.sum(values[0], keepdims=True))
    return jnp.minimum(1.0, limit / (norm + 1e-06))


def rows_kernel(plan, limit, *refs):
    factor = clip_factor(limit, refs[: plan.chips])
    g_attn, g_exp, we, me, ve, both, *far, mine = refs[plan.chips :]
    size, place = plan.size_a, lax.axis_index("expert")
    for q, states in enumerate([both.at[0], both.at[1], *far]):
        rows = pl.ds(pl.multiple_of((place ^ q) * size, 16), size)
        old = [states[pl.ds(i * size, size), :].astype(f32) for i in range(3)]
        weight, _, _ = adamw(g_attn[rows, :], *old, factor)
        mine[rows, :] = weight.astype(bf16)
    weight, _, _ = adamw(g_exp[...], we[...], me[...], ve[...], factor)
    mine[plan.all_a :, :] = weight.astype(bf16)


def own_kernel(plan, limit, *refs):
    factor = clip_factor(limit, refs[: plan.chips])
    g_attn, g_exp = refs[plan.chips : plan.chips + 2]
    state, new = refs[plan.chips + 2 : plan.chips + 8], refs[plan.chips + 8 :]
    rows = pl.ds(pl.multiple_of(lax.axis_index("expert") * plan.size_a, 16), plan.size_a)
    for b, grad in enumerate((g_attn[rows, :], g_exp[...])):
        values = adamw(grad, *[ref[...] for ref in state[3 * b : 3 * b + 3]], factor)
        for ref, value in zip(new[3 * b : 3 * b + 3], values):
            ref[...] = value


PARTS = 2


def gather_order(chips):
    return [0, 1, chips - 1, *range(2, chips - 1)] if chips > 2 else list(range(chips))


def order_kernel(plan, *refs):
    n_dp = plan.n_dp
    parts, (attn, exp, rows, rows_a, rows_e, attn_v, exp_v, sems) = refs[:n_dp], refs[n_dp:]
    me = lax.axis_index("dp")
    me_ex = lax.axis_index("expert")
    my_role = role_of(me // 2, me % 2, me_ex)
    for i, part in enumerate(parts):
        chip, role = gather_order(plan.chips)[i % plan.chips] ^ (me // 2), (i // plan.chips) ^ my_role
        blocks = [(e, e * plan.size_a, plan.size_a) for e in range(plan.n_expert)]
        for expert, start, size in blocks + [(me_ex, plan.all_a, plan.size_e)]:
            owner = 2 * chip + role_of(chip, role, expert)
            to = pl.multiple_of(owner * plan.chunk + start, 16)
            rows[pl.ds(to, size), :] = part[pl.ds(start, size), :].astype(f32)
    count_e = exp.shape[1]

    def lanes(b):
        return pl.ds(b * LANES if isinstance(b, int) else pl.multiple_of(b * LANES, LANES), LANES)

    def turn(part):
        for e in range(plan.n_expert):
            first = e * plan.size_a + part * count
            value = jnp.stack([rows[pl.ds(j * plan.chunk + first, count), :] for j in range(n_dp)])
            value = value.transpose(1, 0, 2)
            for b in range(count):
                rows_a[pl.ds(e * n_dp, n_dp), lanes(b)] = value[b]
        first = plan.all_a + part * count * plan.rows_e
        value = jnp.stack([rows[pl.ds(j * plan.chunk + first, count * plan.rows_e), :] for j in range(n_dp)])
        value = value.transpose(1, 0, 2)
        for b in range(count):
            for r in range(plan.rows_e):
                start = (part * count + b) * count_e + r
                rows_e[pl.ds(start, n_dp, stride=plan.rows_e), :] = value[b * plan.rows_e + r]
        attn_v[:, pl.ds(part * count * LANES, count * LANES)] = rows_a[...].astype(bf16)

    def gather(b):
        places_a, places_e = plan.places(b)
        values = [rows[pl.ds(start, n_dp, stride=plan.chunk), :] for _, start in places_a]
        if plan.rows_a == 1:
            attn_v[:, lanes(b)] = jnp.concatenate(values, axis=0).astype(bf16)
        else:
            for (group, _), value in zip(places_a, values):
                start = (group // plan.rows_a) * n_dp * plan.rows_a + group % plan.rows_a
                rows_a[pl.ds(start, n_dp, stride=plan.rows_a), :] = value
            attn_v[:, lanes(b)] = rows_a[...].astype(bf16)
        for r, start in places_e:
            rows_e[pl.ds(b * count_e + r, n_dp, stride=plan.rows_e), :] = rows[
                pl.ds(start, n_dp, stride=plan.chunk), :
            ]

    def finish(b):
        exp_v[:, lanes(b)] = rows_e[pl.ds(b * count_e, count_e), :].astype(bf16)

    copies = []
    count = plan.blocks // PARTS
    for part in range(PARTS):
        if plan.turned:
            turn(part)
        else:
            each(count, lambda b: gather(part * count + b), n_dp <= 8)
        each(count, lambda b: finish(part * count + b), True)
        cols = pl.ds(part * count * LANES, count * LANES)
        copies.append(pltpu.make_async_copy(attn_v.at[:, cols], attn.at[:, cols], sems.at[2 * part]))
        copies.append(pltpu.make_async_copy(exp_v.at[:, cols], exp.at[0, :, cols], sems.at[2 * part + 1]))
        for copy in copies[-2:]:
            copy.start()
    for copy in copies:
        copy.wait()


def put_in_order(plan, parts):
    count_a = plan.n_expert * plan.n_dp * plan.rows_a
    count_e = plan.n_dp * plan.rows_e
    return call(
        lambda *refs: order_kernel(plan, *refs),
        parts,
        [((count_a, plan.width), bf16), ((1, count_e, plan.width), bf16)],
        [
            ((plan.n_dp * plan.chunk, LANES), f32),
            ((count_a, plan.width // PARTS if plan.turned else LANES), f32),
            ((plan.blocks * count_e, LANES), f32),
            ((count_a, plan.width), bf16),
            ((count_e, plan.width), bf16),
        ],
        out_space=pltpu.HBM,
        copies=True,
    )


def swap(value, chips=0, experts=0):
    n_expert, n_dp = lax.axis_size("expert"), lax.axis_size("dp")
    pairs = []
    for e in range(n_expert):
        for j in range(n_dp):
            role = role_of(j // 2, j % 2, e)
            chip, expert = (j // 2) ^ chips, e ^ experts
            pairs.append((e * n_dp + j, expert * n_dp + 2 * chip + role_of(chip, role, expert)))
    return lax.ppermute(value, ("expert", "dp"), pairs)


def swap_cores(value):
    return lax.ppermute(value, "dp", [(i, i ^ 1) for i in range(lax.axis_size("dp"))])


def to_blocks(value):
    rows, width = value.shape
    return value.reshape(rows, width // LANES, LANES).transpose(1, 0, 2).reshape(-1, LANES)


def from_blocks(value, rows):
    return value.reshape(-1, rows, LANES).transpose(1, 0, 2).reshape(rows, -1)


def body(act_attn, dy_attn, act_exp, dy_exp, w_attn, m_attn, v_attn, w_exp, m_exp, v_exp):
    width = w_attn.shape[1]
    n_expert = lax.axis_size("expert")
    n_dp = lax.axis_size("dp")
    rows_a, rows_e = w_attn.shape[0], w_exp.shape[1]
    plan = Plan(n_expert, n_dp, rows_a, rows_e, width)
    total_params = width * (act_attn.shape[1] + n_expert * act_exp.shape[2])
    limit = 0.5 * math.sqrt(total_params)
    chips, chunk = plan.chips, plan.chunk
    state_a = [to_blocks(value) for value in (w_attn, m_attn, v_attn)]
    state_e = [to_blocks(value[0]) for value in (w_exp, m_exp, v_exp)]

    held = [pltpu.with_memory_space_constraint(x, pltpu.HBM) for x in (act_attn.T, dy_attn, act_exp[0].T, dy_exp[0])]
    full, send, pack = make_terms(plan, *held, *[pltpu.with_memory_space_constraint(x, pltpu.HBM) for x in state_a])
    got = swap_cores(send)
    sums = [
        full[c * chunk : (c + 1) * chunk] + got[c * chunk : (c + 1) * chunk].astype(f32) for c in range(chips)
    ]
    got = [swap(sums[c].astype(bf16), chips=c) for c in reversed(range(1, chips))]
    shared = ((plan.all_a + 16, LANES), bf16)
    packs = [pack, swap(pack, experts=1)]
    payload, g_exp, both = call(
        lambda *refs: share_kernel(plan, *refs),
        packs + [sums[0]] + got,
        [shared, ((plan.size_e, LANES), f32), ((2,) + pack.shape, bf16)],
    )
    distance = 1
    while 2 * distance < n_expert:
        other = swap(payload, experts=distance)
        (payload,) = call(lambda *refs: again_kernel(plan, *refs), [payload, other], [shared])
        distance *= 2
    other = swap(payload, experts=distance)
    early = [q for q in range(2, n_expert) if q != distance]
    held = [pack] + [swap(pack, experts=q) for q in early]
    held = call(hold_kernel, held, [(pack.shape, bf16)] * len(held))
    far = dict(zip(early, held[1:]))
    far[distance] = swap(held[0], experts=distance)
    far = [far[q] for q in range(2, n_expert)]
    g_attn, square = call(
        lambda *refs: last_kernel(plan, *refs), [payload, other], [((plan.all_a, LANES), f32), ((8, LANES), f32)]
    )
    square = square + swap_cores(square)
    squares = [square] + [swap(square, chips=c) for c in square_order(chips)[1:]]
    block_a, block_e = ((plan.size_a, LANES), f32), ((plan.size_e, LANES), f32)
    (mine,) = call(
        lambda *refs: rows_kernel(plan, limit, *refs),
        [*squares, g_attn, g_exp, *state_e, both, *far],
        [((chunk, LANES), bf16)],
    )
    wa, ma, va, we, me, ve = call(
        lambda *refs: own_kernel(plan, limit, *refs),
        [*squares, g_attn, g_exp, *state_a, *state_e],
        [block_a] * 3 + [block_e] * 3,
    )
    near = [mine] + [swap(mine, chips=c) for c in gather_order(chips)[1:]]
    far = [swap_cores(piece) for piece in near]
    attn_full, expert_full = put_in_order(plan, near + far)
    new_a = [from_blocks(value, rows_a) for value in (wa, ma, va)]
    new_e = [from_blocks(value, rows_e)[None] for value in (we, me, ve)]
    return (*new_a, *new_e, attn_full, expert_full)


def solution(mesh):
    return jax.shard_map(
        body,
        mesh=mesh,
        in_specs=(
            P(("expert", "dp"), None),
            P(("expert", "dp"), None),
            P("expert", "dp", None),
            P("expert", "dp", None),
            P(("expert", "dp"), None),
            P(("expert", "dp"), None),
            P(("expert", "dp"), None),
            P("expert", "dp", None),
            P("expert", "dp", None),
            P("expert", "dp", None),
        ),
        out_specs=(
            P(("expert", "dp"), None),
            P(("expert", "dp"), None),
            P(("expert", "dp"), None),
            P("expert", "dp", None),
            P("expert", "dp", None),
            P("expert", "dp", None),
            P(),
            P("expert", None, None),
        ),
        check_vma=False,
    )
```

```python
import math

import jax
import jax.numpy as jnp
from jax import lax
from jax.experimental import pallas as pl
from jax.experimental.pallas import tpu as pltpu
from jax.sharding import PartitionSpec as P

beta_first = 0.9
beta_second = 0.95
bias_first = 1.0 - 0.9**10
bias_second = 1.0 - 0.95**10
learn_rate = 0.01
decay_rate = 0.1
adam_eps = 1e-08

LANES = 128
f32, bf16 = jnp.float32, jnp.bfloat16


def adamw(grad, weight, moment, second, factor):
    scaled = factor * grad
    moment_new = beta_first * moment + (1.0 - beta_first) * scaled
    second_new = beta_second * second + (1.0 - beta_second) * scaled * scaled
    update = moment_new / bias_first / (jnp.sqrt(second_new / bias_second) + adam_eps)
    weight_new = weight - learn_rate * (update + decay_rate * weight)
    return (weight_new, moment_new, second_new)


def role_of(chip, core, expert):
    return core ^ ((chip ^ expert ^ (expert // 2)) % 2)


class Plan:
    def __init__(self, n_expert, n_dp, rows_a, rows_e, width):
        self.n_expert, self.n_dp, self.rows_a, self.rows_e = n_expert, n_dp, rows_a, rows_e
        self.width = width
        self.chips = n_dp // 2
        self.blocks = width // LANES
        self.size_a = self.blocks * rows_a
        self.size_e = self.blocks * rows_e
        self.all_a = n_expert * self.size_a
        self.chunk = self.all_a + self.size_e
        self.turned = n_dp == 8 and rows_a == 1

    def places(self, block):
        attn = [
            (e * self.rows_a + r, e * self.size_a + block * self.rows_a + r)
            for e in range(self.n_expert)
            for r in range(self.rows_a)
        ]
        exp = [(r, self.all_a + block * self.rows_e + r) for r in range(self.rows_e)]
        return attn, exp


def dot(left, right):
    return lax.dot_general(left, right, (((1,), (0,)), ((), ())), preferred_element_type=f32)


def size_of(shape, dtype):
    return math.prod(shape) * jnp.dtype(dtype).itemsize


def call(kernel, args, outs, scratch=(), in_space=pltpu.VMEM, out_space=pltpu.VMEM, copies=False):
    held = sum(size_of(arg.shape, arg.dtype) for arg in args if in_space is pltpu.VMEM)
    held += sum(size_of(*out) for out in outs) + sum(size_of(*buffer) for buffer in scratch)
    semaphores = [pltpu.SemaphoreType.DMA((16,))] if copies else []
    return pl.pallas_call(
        kernel,
        in_specs=[pl.BlockSpec(memory_space=in_space)] * len(args),
        out_specs=[pl.BlockSpec(memory_space=out_space)] * len(outs),
        out_shape=[jax.ShapeDtypeStruct(shape, dtype) for shape, dtype in outs],
        scratch_shapes=[pltpu.VMEM(*buffer) for buffer in scratch] + semaphores,
        compiler_params=pltpu.CompilerParams(vmem_limit_bytes=held + 4 * 1024 * 1024),
    )(*args)


def two_pieces(value):
    high = value.astype(bf16).astype(f32)
    return high, (value - high).astype(bf16).astype(f32)


def by_eights(value):
    return jnp.sum(value.reshape(-1, 8, LANES), axis=0)


STEPS = 2


def each(count, step, unrolled):
    if unrolled:
        for i in range(count):
            step(i)
    else:
        pl.loop(0, count)(step)


def terms_kernel(plan, act_a, dy_a, act_e, dy_e, w, m, v, full, send, pack, act_a_v, dy_a_v, act_e_v, dy_e_v, state, sems):
    tile = plan.width // STEPS
    small = [
        pltpu.make_async_copy(act_a, act_a_v, sems.at[0]),
        pltpu.make_async_copy(act_e, act_e_v, sems.at[1]),
    ]
    big = []
    for t in range(STEPS):
        cols = pl.ds(t * tile, tile)
        big.append(pltpu.make_async_copy(dy_a.at[:, cols], dy_a_v.at[:, cols], sems.at[2 + 2 * t]))
        big.append(pltpu.make_async_copy(dy_e.at[:, cols], dy_e_v.at[:, cols], sems.at[3 + 2 * t]))
    extra = [pltpu.make_async_copy(ref, state.at[i], sems.at[2 + 2 * STEPS + i]) for i, ref in enumerate((w, m, v))]
    for copy in small + big + extra:
        copy.start()

    me, me_ex = lax.axis_index("dp"), lax.axis_index("expert")
    my_role = role_of(me // 2, me % 2, me_ex)

    def pick(groups, per_owner, count, expert):
        shape = (groups * plan.n_dp, count)
        row = lax.broadcasted_iota(jnp.int32, shape, 0)
        col = lax.broadcasted_iota(jnp.int32, shape, 1)
        group, place = row // plan.n_dp, row % plan.n_dp
        chip, role = (place % plan.chips) ^ (me // 2), (place // plan.chips) ^ my_role
        if expert is None:
            expert, base = group // per_owner, (group // per_owner) * plan.n_dp
        else:
            base = 0
        owner = 2 * chip + role_of(chip, role, expert)
        want = (base + owner) * per_owner + group % per_owner
        return (want == col).astype(bf16)

    for copy in small:
        copy.wait()
    left_a = dot(pick(plan.n_expert * plan.rows_a, plan.rows_a, act_a.shape[0], None), act_a_v[...]).astype(bf16)
    left_e = dot(pick(plan.rows_e, plan.rows_e, act_e.shape[0], me_ex), act_e_v[...]).astype(bf16)
    n_dp = plan.n_dp

    def turn(start, pieces):
        value = jnp.stack(pieces).transpose(1, 0, 2)
        for c in range(plan.chips):
            rows = pl.ds(c * plan.chunk + start, len(pieces))
            full[rows, :] = value[c]
            send[rows, :] = value[plan.chips + c].astype(bf16)

    for t in range(STEPS):
        cols = pl.ds(t * tile, tile)
        big[2 * t].wait()
        terms_a = dot(left_a, dy_a_v[:, cols])
        big[2 * t + 1].wait()
        terms_e = dot(left_e, dy_e_v[:, cols])
        count = tile // LANES
        if plan.turned:
            blocks = [slice(b * LANES, (b + 1) * LANES) for b in range(count)]
            for e in range(plan.n_expert):
                turn(e * plan.size_a + t * count, [terms_a[e * n_dp : (e + 1) * n_dp, span] for span in blocks])
            pieces = [
                terms_e[r * n_dp : (r + 1) * n_dp, span] for span in blocks for r in range(plan.rows_e)
            ]
            turn(plan.all_a + t * count * plan.rows_e, pieces)
            continue
        for b in range(count):
            attn, exp = plan.places(t * count + b)
            span = slice(b * LANES, (b + 1) * LANES)
            for terms, places in ((terms_a, attn), (terms_e, exp)):
                for group, start in places:
                    full[pl.ds(start, n_dp, stride=plan.chunk), :] = terms[group * n_dp : (group + 1) * n_dp, span]
    for c in range(0 if plan.turned else plan.chips):
        send[pl.ds(c * plan.chunk, plan.chunk), :] = full[
            pl.ds((plan.chips + c) * plan.chunk, plan.chunk), :
        ].astype(bf16)
    for copy in extra:
        copy.wait()
    size = plan.size_a
    for i in range(3):
        pack[pl.ds(i * size, size), :] = state[i].astype(bf16)


def make_terms(plan, act_a, dy_a, act_e, dy_e, w, m, v):
    args = (act_a, dy_a, act_e, dy_e, w, m, v)
    half = plan.chips * plan.chunk
    return call(
        lambda *refs: terms_kernel(plan, *refs),
        args,
        [((half if plan.turned else 2 * half, LANES), f32), ((half, LANES), bf16), ((3 * plan.size_a, LANES), bf16)],
        [
            (act_a.shape, bf16),
            (dy_a.shape, bf16),
            (act_e.shape, bf16),
            (dy_e.shape, bf16),
            ((3,) + w.shape, f32),
        ],
        in_space=pltpu.HBM,
        copies=True,
    )


def share_kernel(plan, *refs):
    held, far, own, got, (payload, g_exp, both) = *refs[:3], refs[3:-3], refs[-3:]
    both[0], both[1] = held[...], far[...]
    total = own[...]
    for ref in got:
        total = total + ref[...].astype(f32)
    a = plan.all_a
    exp = total[a:]
    g_exp[...] = exp
    payload[:a, :] = total[:a].astype(bf16)
    payload[a:, :] = jnp.concatenate(two_pieces(by_eights(exp * exp)), axis=0).astype(bf16)


def pair_sum(plan, mine, other):
    a = plan.all_a
    attn = mine[:a, :].astype(f32) + other[:a, :].astype(f32)
    one, two = mine[a:, :].astype(f32), other[a:, :].astype(f32)
    return attn, (one[:8] + one[8:]) + (two[:8] + two[8:])


def again_kernel(plan, mine, other, payload):
    attn, square = pair_sum(plan, mine, other)
    a = plan.all_a
    payload[:a, :] = attn.astype(bf16)
    payload[a:, :] = jnp.concatenate(two_pieces(square), axis=0).astype(bf16)


def hold_kernel(*refs):
    count = len(refs) // 2
    for ref, out in zip(refs[:count], refs[count:]):
        out[...] = ref[...]


def last_kernel(plan, mine, other, g_attn, square):
    attn, partial = pair_sum(plan, mine, other)
    g_attn[...] = attn
    square[...] = partial + by_eights(attn * attn)


def square_order(chips):
    return [0, *reversed(range(1, chips - 1)), chips - 1]


def clip_factor(limit, squares):
    order = square_order(len(squares))
    values = [squares[order.index(c)][...] for c in range(len(squares))]
    while len(values) > 1:
        values = [values[i] + values[i + 1] for i in range(0, len(values), 2)]
    norm = jnp.sqrt(jnp.sum(values[0], keepdims=True))
    return jnp.minimum(1.0, limit / (norm + 1e-06))


def rows_kernel(plan, limit, *refs):
    factor = clip_factor(limit, refs[: plan.chips])
    g_attn, g_exp, we, me, ve, both, *far, mine = refs[plan.chips :]
    size, place = plan.size_a, lax.axis_index("expert")
    for q, states in enumerate([both.at[0], both.at[1], *far]):
        rows = pl.ds(pl.multiple_of((place ^ q) * size, 16), size)
        old = [states[pl.ds(i * size, size), :].astype(f32) for i in range(3)]
        weight, _, _ = adamw(g_attn[rows, :], *old, factor)
        mine[rows, :] = weight.astype(bf16)
    weight, _, _ = adamw(g_exp[...], we[...], me[...], ve[...], factor)
    mine[plan.all_a :, :] = weight.astype(bf16)


def own_kernel(plan, limit, *refs):
    factor = clip_factor(limit, refs[: plan.chips])
    g_attn, g_exp = refs[plan.chips : plan.chips + 2]
    state, new = refs[plan.chips + 2 : plan.chips + 8], refs[plan.chips + 8 :]
    rows = pl.ds(pl.multiple_of(lax.axis_index("expert") * plan.size_a, 16), plan.size_a)
    for b, grad in enumerate((g_attn[rows, :], g_exp[...])):
        values = adamw(grad, *[ref[...] for ref in state[3 * b : 3 * b + 3]], factor)
        for ref, value in zip(new[3 * b : 3 * b + 3], values):
            ref[...] = value


PARTS = 2


def order_kernel(plan, *refs):
    n_dp = plan.n_dp
    parts, (attn, exp, rows, rows_a, rows_e, attn_v, exp_v, sems) = refs[:n_dp], refs[n_dp:]
    me = lax.axis_index("dp")
    me_ex = lax.axis_index("expert")
    my_role = role_of(me // 2, me % 2, me_ex)
    for i, part in enumerate(parts):
        chip, role = (i % plan.chips) ^ (me // 2), (i // plan.chips) ^ my_role
        blocks = [(e, e * plan.size_a, plan.size_a) for e in range(plan.n_expert)]
        for expert, start, size in blocks + [(me_ex, plan.all_a, plan.size_e)]:
            owner = 2 * chip + role_of(chip, role, expert)
            to = pl.multiple_of(owner * plan.chunk + start, 16)
            rows[pl.ds(to, size), :] = part[pl.ds(start, size), :].astype(f32)
    count_e = exp.shape[1]

    def lanes(b):
        return pl.ds(b * LANES if isinstance(b, int) else pl.multiple_of(b * LANES, LANES), LANES)

    def turn(part):
        for e in range(plan.n_expert):
            first = e * plan.size_a + part * count
            value = jnp.stack([rows[pl.ds(j * plan.chunk + first, count), :] for j in range(n_dp)])
            value = value.transpose(1, 0, 2)
            for b in range(count):
                rows_a[pl.ds(e * n_dp, n_dp), lanes(b)] = value[b]
        first = plan.all_a + part * count * plan.rows_e
        value = jnp.stack([rows[pl.ds(j * plan.chunk + first, count * plan.rows_e), :] for j in range(n_dp)])
        value = value.transpose(1, 0, 2)
        for b in range(count):
            for r in range(plan.rows_e):
                start = (part * count + b) * count_e + r
                rows_e[pl.ds(start, n_dp, stride=plan.rows_e), :] = value[b * plan.rows_e + r]
        attn_v[:, pl.ds(part * count * LANES, count * LANES)] = rows_a[...].astype(bf16)

    def gather(b):
        places_a, places_e = plan.places(b)
        values = [rows[pl.ds(start, n_dp, stride=plan.chunk), :] for _, start in places_a]
        if plan.rows_a == 1:
            attn_v[:, lanes(b)] = jnp.concatenate(values, axis=0).astype(bf16)
        else:
            for (group, _), value in zip(places_a, values):
                start = (group // plan.rows_a) * n_dp * plan.rows_a + group % plan.rows_a
                rows_a[pl.ds(start, n_dp, stride=plan.rows_a), :] = value
            attn_v[:, lanes(b)] = rows_a[...].astype(bf16)
        for r, start in places_e:
            rows_e[pl.ds(b * count_e + r, n_dp, stride=plan.rows_e), :] = rows[
                pl.ds(start, n_dp, stride=plan.chunk), :
            ]

    def finish(b):
        exp_v[:, lanes(b)] = rows_e[pl.ds(b * count_e, count_e), :].astype(bf16)

    copies = []
    count = plan.blocks // PARTS
    for part in range(PARTS):
        if plan.turned:
            turn(part)
        else:
            each(count, lambda b: gather(part * count + b), n_dp <= 8)
        each(count, lambda b: finish(part * count + b), True)
        cols = pl.ds(part * count * LANES, count * LANES)
        copies.append(pltpu.make_async_copy(attn_v.at[:, cols], attn.at[:, cols], sems.at[2 * part]))
        copies.append(pltpu.make_async_copy(exp_v.at[:, cols], exp.at[0, :, cols], sems.at[2 * part + 1]))
        for copy in copies[-2:]:
            copy.start()
    for copy in copies:
        copy.wait()


def put_in_order(plan, parts):
    count_a = plan.n_expert * plan.n_dp * plan.rows_a
    count_e = plan.n_dp * plan.rows_e
    return call(
        lambda *refs: order_kernel(plan, *refs),
        parts,
        [((count_a, plan.width), bf16), ((1, count_e, plan.width), bf16)],
        [
            ((plan.n_dp * plan.chunk, LANES), f32),
            ((count_a, plan.width // PARTS if plan.turned else LANES), f32),
            ((plan.blocks * count_e, LANES), f32),
            ((count_a, plan.width), bf16),
            ((count_e, plan.width), bf16),
        ],
        out_space=pltpu.HBM,
        copies=True,
    )


def swap(value, chips=0, experts=0):
    n_expert, n_dp = lax.axis_size("expert"), lax.axis_size("dp")
    pairs = []
    for e in range(n_expert):
        for j in range(n_dp):
            role = role_of(j // 2, j % 2, e)
            chip, expert = (j // 2) ^ chips, e ^ experts
            pairs.append((e * n_dp + j, expert * n_dp + 2 * chip + role_of(chip, role, expert)))
    return lax.ppermute(value, ("expert", "dp"), pairs)


def swap_cores(value):
    return lax.ppermute(value, "dp", [(i, i ^ 1) for i in range(lax.axis_size("dp"))])


def to_blocks(value):
    rows, width = value.shape
    return value.reshape(rows, width // LANES, LANES).transpose(1, 0, 2).reshape(-1, LANES)


def from_blocks(value, rows):
    return value.reshape(-1, rows, LANES).transpose(1, 0, 2).reshape(rows, -1)


def body(act_attn, dy_attn, act_exp, dy_exp, w_attn, m_attn, v_attn, w_exp, m_exp, v_exp):
    width = w_attn.shape[1]
    n_expert = lax.axis_size("expert")
    n_dp = lax.axis_size("dp")
    rows_a, rows_e = w_attn.shape[0], w_exp.shape[1]
    plan = Plan(n_expert, n_dp, rows_a, rows_e, width)
    total_params = width * (act_attn.shape[1] + n_expert * act_exp.shape[2])
    limit = 0.5 * math.sqrt(total_params)
    chips, chunk = plan.chips, plan.chunk
    state_a = [to_blocks(value) for value in (w_attn, m_attn, v_attn)]
    state_e = [to_blocks(value[0]) for value in (w_exp, m_exp, v_exp)]

    held = [pltpu.with_memory_space_constraint(x, pltpu.HBM) for x in (act_attn.T, dy_attn, act_exp[0].T, dy_exp[0])]
    full, send, pack = make_terms(plan, *held, *[pltpu.with_memory_space_constraint(x, pltpu.HBM) for x in state_a])
    got = swap_cores(send)
    sums = [
        full[c * chunk : (c + 1) * chunk] + got[c * chunk : (c + 1) * chunk].astype(f32) for c in range(chips)
    ]
    got = [swap(sums[c].astype(bf16), chips=c) for c in range(1, chips)]
    shared = ((plan.all_a + 16, LANES), bf16)
    packs = [pack, swap(pack, experts=1)]
    payload, g_exp, both = call(
        lambda *refs: share_kernel(plan, *refs),
        packs + [sums[0]] + got,
        [shared, ((plan.size_e, LANES), f32), ((2,) + pack.shape, bf16)],
    )
    distance = 1
    while 2 * distance < n_expert:
        other = swap(payload, experts=distance)
        (payload,) = call(lambda *refs: again_kernel(plan, *refs), [payload, other], [shared])
        distance *= 2
    other = swap(payload, experts=distance)
    early = [q for q in range(2, n_expert) if q != distance]
    held = [pack] + [swap(pack, experts=q) for q in early]
    held = call(hold_kernel, held, [(pack.shape, bf16)] * len(held))
    far = dict(zip(early, held[1:]))
    far[distance] = swap(held[0], experts=distance)
    far = [far[q] for q in range(2, n_expert)]
    g_attn, square = call(
        lambda *refs: last_kernel(plan, *refs), [payload, other], [((plan.all_a, LANES), f32), ((8, LANES), f32)]
    )
    square = square + swap_cores(square)
    squares = [square] + [swap(square, chips=c) for c in square_order(chips)[1:]]
    block_a, block_e = ((plan.size_a, LANES), f32), ((plan.size_e, LANES), f32)
    (mine,) = call(
        lambda *refs: rows_kernel(plan, limit, *refs),
        [*squares, g_attn, g_exp, *state_e, both, *far],
        [((chunk, LANES), bf16)],
    )
    wa, ma, va, we, me, ve = call(
        lambda *refs: own_kernel(plan, limit, *refs),
        [*squares, g_attn, g_exp, *state_a, *state_e],
        [block_a] * 3 + [block_e] * 3,
    )
    near = [mine] + [swap(mine, chips=c) for c in range(1, chips)]
    far = [swap_cores(piece) for piece in near]
    attn_full, expert_full = put_in_order(plan, near + far)
    new_a = [from_blocks(value, rows_a) for value in (wa, ma, va)]
    new_e = [from_blocks(value, rows_e)[None] for value in (we, me, ve)]
    return (*new_a, *new_e, attn_full, expert_full)


def solution(mesh):
    return jax.shard_map(
        body,
        mesh=mesh,
        in_specs=(
            P(("expert", "dp"), None),
            P(("expert", "dp"), None),
            P("expert", "dp", None),
            P("expert", "dp", None),
            P(("expert", "dp"), None),
            P(("expert", "dp"), None),
            P(("expert", "dp"), None),
            P("expert", "dp", None),
            P("expert", "dp", None),
            P("expert", "dp", None),
        ),
        out_specs=(
            P(("expert", "dp"), None),
            P(("expert", "dp"), None),
            P(("expert", "dp"), None),
            P("expert", "dp", None),
            P("expert", "dp", None),
            P("expert", "dp", None),
            P(),
            P("expert", None, None),
        ),
        check_vma=False,
    )
```
